32 devices in a mesh: head: 4 (over z), ctx: 8 (over y, x, core).
Axes of the slice: x: 2, y: 2, z: 4, core: 2. Of those that a mesh axis runs over, the one named last changes fastest.
Arguments:
- inputs: bfloat16 [2048, 4096], P('ctx'), may hold values from -8 to 8
- out_grad: bfloat16 [2048, 4096], P('ctx', 'head'), may hold values from -6 to 6
- w_query: bfloat16 [4096, 4096], P(None, 'head'), may hold values from -4 to 4
- w_key: bfloat16 [4096, 1024], P(None, 'head'), may hold values from -4 to 4
- value_projection: bfloat16 [4096, 1024], P(None, 'head'), may hold values from -0.09375 to 0.09375
- w_out: bfloat16 [4096, 4096], P('head'), may hold values from -0.09375 to 0.09375
- doc_lengths: int32 [8], replicated, may hold values from 1 to 1024, 2048 in all
- span_order: int32 [16], replicated, may hold values from 0 to 15, as said below
Outputs:
- input_grad: bfloat16 [2048, 4096], P('ctx', 'head')
The draws below stay inside these ranges and needn't reach their ends.
Inputs may be any that keep to these rules, and one draw needn't show every extreme that they name: `span_order`: A permutation of 0 to 15; entries 2 d and 2 d + 1 are c and 15 - c for some c, in either order.
All inputs are finite; a program needn't handle non-finite values.
Results may differ from the reference program's by a relative error of at most 0.012.
The reference program's roundings to bfloat16 on the way count: a program that leaves them out, or rounds other values in their place, can miss the bound.
Values may be sent and summed in bfloat16 or wider, within the bound.
No kernel may reach another device: no remote copies, remote signals or barrier semaphores. Data moves between devices by JAX's collectives and lax.ppermute only.
A program may use at most 64 MiB of HBM per device.

```python
import math
import jax
import jax.numpy as jnp
import numpy as np
from jax import lax

MODEL_WIDTH = 4096
ASKER_NUM = 32
SHARED_KV_NUM = 8
CHANNEL_DIM = 128
TOK_DEV = 256
NDOC = 8
TOKEN_SPAN = 2048
SPANS = 16


def draw_inputs(key, part):
    base = jnp.clip(jax.random.normal(jax.random.fold_in(key, 1), (TOKEN_SPAN, MODEL_WIDTH), jnp.float32), -6.0, 6.0)
    return base.astype(jnp.bfloat16)


def matched_weight(key, salt, columns):
    base = jax.random.normal(jax.random.fold_in(key, salt), (MODEL_WIDTH, columns), jnp.float32)
    base = jnp.clip(base, -5.0, 5.0) / math.sqrt(MODEL_WIDTH)
    return base


def draw_w_query(key, part):
    return matched_weight(key, 21, ASKER_NUM * CHANNEL_DIM).astype(jnp.bfloat16)


def draw_w_key(key, part):
    return matched_weight(key, 22, SHARED_KV_NUM * CHANNEL_DIM).astype(jnp.bfloat16)


def draw_span_order(key, part):
    pairs = SPANS // 2
    lower = jax.random.permutation(jax.random.fold_in(key, 31), pairs).astype(jnp.int32)
    flips = jax.random.randint(jax.random.fold_in(key, 32), (pairs,), 0, 2)
    first = jnp.where(flips == 1, SPANS - 1 - lower, lower)
    second = SPANS - 1 - first
    return jnp.stack([first, second], axis=1).reshape(SPANS).astype(jnp.int32)


def block_levels(rng, shape, cuts, low, high):
    gain, own = 1.0, jax.random.fold_in(rng, 6)
    for position, parts in cuts:
        draws = jnp.exp(jax.random.uniform(jax.random.fold_in(own, position), (parts,), jnp.float32, low / len(cuts), high / len(cuts)))
        gain = gain * jnp.repeat(draws, shape[position] // parts).reshape([-1 if axis == position else 1 for axis in range(len(shape))])
    return gain


def length_profile(amount, total, bound, slope):
    loads = [(1 << 20) // math.isqrt(grade ** slope) + 1 for grade in range(2, amount + 1)]
    surplus, counts = total - bound - (amount - 1), [1] * (amount - 1)
    while surplus > 0:
        free = [i for i in range(amount - 1) if counts[i] < bound]
        pool, budget = sum([loads[i] for i in free]), surplus
        for i in free:
            extra = min(bound - counts[i], max(1, budget * loads[i] // pool), surplus)
            counts[i] = counts[i] + extra
            surplus = surplus - extra
    return np.array([bound] + counts)


def ragged(stream_key, number_of, total, bound, skew):
    if number_of == 2:
        one = jax.random.randint(stream_key, (), max(1, total - bound), min(bound, total - 1) + 1)
        return jnp.stack([one, total - one])
    sizes = jnp.asarray(length_profile(number_of, total, bound, skew), jnp.int32)
    pairs = (number_of - 1) // 2
    donor, sink = sizes[1:1 + 2 * pairs:2], sizes[2:2 + 2 * pairs:2]
    room = jnp.minimum(donor - 1, bound - sink)
    moved = jax.random.randint(jax.random.fold_in(stream_key, 1), (pairs,), 0, 1 << 20) % (room + 1)
    sizes = sizes.at[1:1 + 2 * pairs:2].set(donor - moved).at[2:2 + 2 * pairs:2].set(sink + moved)
    return sizes[jax.random.permutation(jax.random.fold_in(stream_key, 2), number_of)]


def noise(own_key, extent, scale, reach, split=(), held_as=jnp.bfloat16):
    values = jax.random.normal(own_key, extent, jnp.float32) * scale
    if len(split) > 0:
        values = block_levels(own_key, extent, split, -0.22, 0.18) * values
    return jnp.clip(values, min=-reach, max=reach).astype(held_as)


def setup_inputs(seed: int = 0) -> dict:
    splits = jax.random.split(jax.random.key(seed), 9)
    return {
        "inputs": draw_inputs(jax.random.fold_in(splits[8], 71), 0),
        "out_grad": noise(splits[1], (TOKEN_SPAN, MODEL_WIDTH), 1.0, 6.0, ((0, 8), (1, 4))),
        "w_query": draw_w_query(jax.random.fold_in(splits[8], 71), 0),
        "w_key": draw_w_key(jax.random.fold_in(splits[8], 71), 0),
        "value_projection": noise(splits[4], (MODEL_WIDTH, SHARED_KV_NUM * CHANNEL_DIM), MODEL_WIDTH ** -0.5, 0.09375, ((1, 4),)),
        "w_out": noise(splits[5], (ASKER_NUM * CHANNEL_DIM, MODEL_WIDTH), (ASKER_NUM * CHANNEL_DIM) ** -0.5, 0.09375, ((0, 4),)),
        "doc_lengths": ragged(splits[6], NDOC, TOKEN_SPAN, TOKEN_SPAN // 2, 2).astype(jnp.int32),
        "span_order": draw_span_order(jax.random.fold_in(splits[8], 71), 0),
    }


masked_score = -1e+30

def reference(inputs, out_grad, w_query, w_key, value_projection, w_out, doc_lengths, span_order):
    half = TOK_DEV // 2
    rows = jnp.arange(TOKEN_SPAN, dtype=jnp.int32)
    positions = span_order[rows // half] * half + rows % half
    ends = jnp.cumsum(doc_lengths)
    documents = lax.optimization_barrier(jnp.sum((positions[:, None] >= ends[None, :]).astype(jnp.int32), axis=1))
    allowed = (positions[None, :] <= positions[:, None]) & (documents[None, :] == documents[:, None])
    query = jnp.dot(inputs, w_query, preferred_element_type=jnp.float32).astype(jnp.bfloat16)
    keys = jnp.dot(inputs, w_key, preferred_element_type=jnp.float32).astype(jnp.bfloat16)
    values = jnp.dot(inputs, value_projection, preferred_element_type=jnp.float32).astype(jnp.bfloat16)
    context_grad = jnp.dot(out_grad, w_out.T, preferred_element_type=jnp.float32).astype(jnp.bfloat16)
    sharing_bundles = ASKER_NUM // SHARED_KV_NUM
    scale = 1.0 / math.sqrt(CHANNEL_DIM)

    def single_attender(head):
        query_head = lax.dynamic_slice_in_dim(query, head * CHANNEL_DIM, CHANNEL_DIM, 1)
        grad_head = lax.dynamic_slice_in_dim(context_grad, head * CHANNEL_DIM, CHANNEL_DIM, 1)
        key_head = lax.dynamic_slice_in_dim(keys, head // sharing_bundles * CHANNEL_DIM, CHANNEL_DIM, 1)
        value_head = lax.dynamic_slice_in_dim(values, head // sharing_bundles * CHANNEL_DIM, CHANNEL_DIM, 1)
        logits = jnp.dot(query_head, key_head.T, preferred_element_type=jnp.float32) * scale
        logits = jnp.where(allowed, logits, masked_score)
        maxima = lax.optimization_barrier(jnp.max(logits, axis=1, keepdims=True))
        weights = jnp.exp(logits - maxima)
        probability = weights / lax.optimization_barrier(jnp.sum(weights, axis=1, keepdims=True))
        slopes = jnp.dot(grad_head, value_head.T, preferred_element_type=jnp.float32)
        delta = lax.optimization_barrier(jnp.sum(probability * slopes, axis=1, keepdims=True))
        score_grad = (probability * (slopes - delta)).astype(jnp.bfloat16)
        rounded = probability.astype(jnp.bfloat16)
        value_term = jnp.dot(rounded.T, grad_head, preferred_element_type=jnp.float32)
        query_term = jnp.dot(score_grad, key_head, preferred_element_type=jnp.float32) * scale
        key_term = jnp.dot(score_grad.T, query_head, preferred_element_type=jnp.float32) * scale
        return (query_term, key_term, value_term)
    asker_pieces, lookup_pieces, content_pieces = lax.map(single_attender, jnp.arange(ASKER_NUM, dtype=jnp.int32))
    query_grad = jnp.transpose(asker_pieces, (1, 0, 2)).reshape(TOKEN_SPAN, ASKER_NUM * CHANNEL_DIM).astype(jnp.bfloat16)
    lookup_aggregate = lax.optimization_barrier(jnp.sum(lookup_pieces.reshape(SHARED_KV_NUM, sharing_bundles, TOKEN_SPAN, CHANNEL_DIM), axis=1))
    content_aggregate = lax.optimization_barrier(jnp.sum(content_pieces.reshape(SHARED_KV_NUM, sharing_bundles, TOKEN_SPAN, CHANNEL_DIM), axis=1))
    key_gradient = jnp.transpose(lookup_aggregate, (1, 0, 2)).reshape(TOKEN_SPAN, SHARED_KV_NUM * CHANNEL_DIM).astype(jnp.bfloat16)
    value_gradient = jnp.transpose(content_aggregate, (1, 0, 2)).reshape(TOKEN_SPAN, SHARED_KV_NUM * CHANNEL_DIM).astype(jnp.bfloat16)
    total = jnp.dot(query_grad, w_query.T, preferred_element_type=jnp.float32)
    total = total + jnp.dot(key_gradient, w_key.T, preferred_element_type=jnp.float32)
    total = total + jnp.dot(value_gradient, value_projection.T, preferred_element_type=jnp.float32)
    return total.astype(jnp.bfloat16)
```

```python
import functools
import math

import jax
import jax.numpy as jnp
from jax import lax
from jax.experimental import pallas as pl
from jax.experimental.pallas import tpu as pltpu
from jax.sharding import PartitionSpec as P

ASKER_NUM = 32
SHARED_KV_NUM = 8
CHANNEL_DIM = 128

masked_score = -1e30
MIB = 1 << 20
VMEM = pltpu.VMEM


def mm(a, b):
    return lax.dot_general(a, b, (((1,), (0,)), ((), ())), preferred_element_type=jnp.float32)


def mm_nt(a, b):
    return lax.dot_general(a, b, (((1,), (1,)), ((), ())), preferred_element_type=jnp.float32)


def mm_tn(a, b):
    return lax.dot_general(a, b, (((0,), (0,)), ((), ())), preferred_element_type=jnp.float32)


def params(limit):
    return pltpu.CompilerParams(vmem_limit_bytes=limit * MIB)


def cost(flops, moved):
    return pl.CostEstimate(flops=flops, bytes_accessed=moved, transcendentals=0)


def kv_body(x_ref, wk_ref, wv_ref, out_ref, acc):
    width = wk_ref.shape[1]
    step = pl.program_id(0)

    @pl.when(step == 0)
    def _():
        acc[...] = jnp.zeros_like(acc)

    x = x_ref[...]
    acc[:, :width] += mm(x, wk_ref[...])
    acc[:, width:] += mm(x, wv_ref[...])

    @pl.when(step == pl.num_programs(0) - 1)
    def _():
        out_ref[...] = acc[...].astype(out_ref.dtype)


def project_kv(x, wk, wv):
    tokens, depth = x.shape
    width = wk.shape[1]
    part = min(depth, 1024)
    return pl.pallas_call(
        kv_body,
        grid=(depth // part,),
        in_specs=[
            pl.BlockSpec((tokens, part), lambda i: (0, i)),
            pl.BlockSpec((part, width), lambda i: (i, 0)),
            pl.BlockSpec((part, width), lambda i: (i, 0)),
        ],
        out_specs=pl.BlockSpec((tokens, 2 * width), lambda i: (0, 0)),
        out_shape=jax.ShapeDtypeStruct((tokens, 2 * width), jnp.bfloat16),
        scratch_shapes=[VMEM((tokens, 2 * width), jnp.float32)],
        compiler_params=params(24),
        cost_estimate=cost(4 * tokens * depth * width, 2 * depth * (tokens + 2 * width)),
        name="project_kv",
    )(x, wk, wv)


def project_body(x_ref, w_ref, out_ref):
    out_ref[...] = mm(x_ref[...], w_ref[...]).astype(out_ref.dtype)


def project(x, w):
    tokens, depth = x.shape
    width = w.shape[1]
    part = min(width, 256)
    return pl.pallas_call(
        project_body,
        grid=(width // part,),
        in_specs=[
            pl.BlockSpec((tokens, depth), lambda i: (0, 0)),
            pl.BlockSpec((depth, part), lambda i: (0, i)),
        ],
        out_specs=pl.BlockSpec((tokens, part), lambda i: (0, i)),
        out_shape=jax.ShapeDtypeStruct((tokens, width), jnp.bfloat16),
        compiler_params=params(24),
        cost_estimate=cost(2 * tokens * depth * width, 2 * depth * (tokens + width)),
        name="project",
    )(x, w)


def back_body(x_ref, w_ref, out_ref):
    out_ref[...] = mm_nt(x_ref[...], w_ref[...]).astype(out_ref.dtype)


def back_project(x, w):
    tokens, depth = x.shape
    width = w.shape[0]
    part = min(width, 256)
    return pl.pallas_call(
        back_body,
        grid=(width // part,),
        in_specs=[
            pl.BlockSpec((tokens, depth), lambda i: (0, 0)),
            pl.BlockSpec((part, depth), lambda i: (i, 0)),
        ],
        out_specs=pl.BlockSpec((tokens, part), lambda i: (0, i)),
        out_shape=jax.ShapeDtypeStruct((tokens, width), jnp.bfloat16),
        compiler_params=params(24),
        cost_estimate=cost(2 * tokens * depth * width, 2 * depth * (tokens + width)),
        name="back_project",
    )(x, w)


def input_body(count, dq_ref, *refs):
    terms = refs[:count]
    wq_ref, wk_ref, wv_ref, out_ref, grads = refs[count:]
    width = wk_ref.shape[1]

    @pl.when(pl.program_id(0) == 0)
    def _():
        total = terms[0][...].astype(jnp.float32)
        for term in terms[1:]:
            total = total + term[...].astype(jnp.float32)
        grads[...] = total.astype(grads.dtype)

    total = mm_nt(dq_ref[...], wq_ref[...])
    total = total + mm_nt(grads[:, :width], wk_ref[...])
    total = total + mm_nt(grads[:, width:], wv_ref[...])
    out_ref[...] = total.astype(out_ref.dtype)


def input_terms(dq, terms, wq, wk, wv):
    tokens, depth = dq.shape
    rows, width = wk.shape
    part = min(rows, 512)
    whole = lambda a: pl.BlockSpec(a.shape, lambda i: (0, 0))
    return pl.pallas_call(
        functools.partial(input_body, len(terms)),
        grid=(rows // part,),
        in_specs=[whole(dq)]
        + [whole(t) for t in terms]
        + [
            pl.BlockSpec((part, depth), lambda i: (i, 0)),
            pl.BlockSpec((part, width), lambda i: (i, 0)),
            pl.BlockSpec((part, width), lambda i: (i, 0)),
        ],
        out_specs=pl.BlockSpec((tokens, part), lambda i: (0, i)),
        out_shape=jax.ShapeDtypeStruct((tokens, rows), jnp.bfloat16),
        scratch_shapes=[VMEM((tokens, 2 * width), jnp.bfloat16)],
        compiler_params=params(24),
        cost_estimate=cost(
            2 * tokens * rows * (depth + 2 * width), 2 * rows * (tokens + depth + 2 * width)
        ),
        name="input_terms",
    )(dq, *terms, wq, wk, wv)


def find_places(order, places, me, spans):
    for i in range(spans):
        places[order[i]] = ((i // 2) ^ me) * 2 + (i % 2)


def own_span(order, lengths, docs, me, j, half):
    span = order[2 * me + j]
    position = span * half + lax.broadcasted_iota(jnp.int32, (1, half), 1)
    first, end = 0, 0
    start = jnp.zeros((1, half), jnp.int32)
    for k in range(docs):
        end = end + lengths[k]
        start = jnp.where(position >= end, end, start)
        first = jnp.where(span * half >= end, end, first)
    return span, position, start, first // half


def stack_heads(ref, rows, group, share, dim):
    base = group * share
    return jnp.concatenate(
        [ref[rows, (base + h) * dim : (base + h + 1) * dim] for h in range(share)], axis=0
    )


def load_blocks(refs, held):
    rows = refs[0].shape[0]
    for k, ref in enumerate(refs):
        held[k * rows : (k + 1) * rows, :] = ref[...]


def allowed_of(p, position, start, half, share):
    key = p * half + lax.broadcasted_iota(jnp.int32, (half, 1), 0)
    allowed = (key <= position) & (key >= start)
    return jnp.concatenate([allowed] * share, axis=1)


def stats_body(sizes, order, lengths, q_ref, *refs):
    peers, half, groups, share, dim, docs = sizes
    blocks = refs[:peers]
    level_ref, mixed_ref, held, places = refs[peers:]
    me = lax.axis_index("ctx")
    width = groups * dim
    factor = math.log2(math.e) / math.sqrt(dim)
    find_places(order, places, me, 2 * peers)
    load_blocks(blocks, held)
    columns = share * half
    for j in range(2):
        span, position, start, lowest = own_span(order, lengths, docs, me, j, half)
        rows = slice(j * half, (j + 1) * half)
        queries = [stack_heads(q_ref, rows, g, share, dim) for g in range(groups)]

        def visit(p, carry):
            place = pl.multiple_of(places[p] * half, half)
            allowed = allowed_of(p, position, start, half, share)
            fresh = []
            for g in range(groups):
                top, total, mixed = carry[g]
                keys = held[pl.ds(place, half), g * dim : (g + 1) * dim]
                values = held[pl.ds(place, half), width + g * dim : width + (g + 1) * dim]
                logits = mm_nt(keys, queries[g]) * factor
                logits = jnp.where(allowed, logits, masked_score)
                higher = jnp.maximum(top, jnp.max(logits, axis=0, keepdims=True))
                weights = jnp.where(allowed, jnp.exp2(logits - higher), 0.0)
                fade = jnp.exp2(top - higher)
                total = total * fade + jnp.sum(weights, axis=0, keepdims=True)
                mixed = mixed * fade + mm_tn(values, weights.astype(jnp.bfloat16))
                fresh.append((higher, total, mixed))
            return tuple(fresh)

        empty = (
            jnp.full((1, columns), masked_score, jnp.float32),
            jnp.zeros((1, columns), jnp.float32),
            jnp.zeros((dim, columns), jnp.float32),
        )
        done = lax.fori_loop(lowest, span + 1, visit, (empty,) * groups)
        for g in range(groups):
            top, total, mixed = done[g]
            level_ref[j * groups + g] = top + jnp.log2(total)
            mixed_ref[j * groups + g] = mixed / total


def stats(q, blocks, span_order, doc_lengths, sizes):
    peers, half, groups, share, dim, docs = sizes
    columns = share * half
    return pl.pallas_call(
        functools.partial(stats_body, sizes),
        in_specs=[pl.BlockSpec(memory_space=pltpu.SMEM)] * 2
        + [pl.BlockSpec(memory_space=VMEM)] * (1 + peers),
        out_specs=[pl.BlockSpec(memory_space=VMEM)] * 2,
        out_shape=[
            jax.ShapeDtypeStruct((2 * groups, 1, columns), jnp.float32),
            jax.ShapeDtypeStruct((2 * groups, dim, columns), jnp.float32),
        ],
        scratch_shapes=[
            VMEM((2 * peers * half, 2 * groups * dim), jnp.bfloat16),
            pltpu.SMEM((2 * peers,), jnp.int32),
        ],
        compiler_params=params(40),
        cost_estimate=cost(9 * peers * half * half * columns * groups * dim // dim, 6 * MIB),
        name="stats",
    )(span_order, doc_lengths, q, *blocks)


def grads_body(sizes, order, lengths, q_ref, g_ref, level_ref, mixed_ref, *refs):
    peers, half, groups, share, dim, docs = sizes
    blocks = refs[:peers]
    dq_ref, even_ref, odd_ref, held, sums, places = refs[peers:]
    me = lax.axis_index("ctx")
    width = groups * dim
    scale = 1.0 / math.sqrt(dim)
    factor = math.log2(math.e) * scale
    find_places(order, places, me, 2 * peers)
    load_blocks(blocks, held)
    sums[...] = jnp.zeros_like(sums)
    columns = share * half
    for j in range(2):
        span, position, start, lowest = own_span(order, lengths, docs, me, j, half)
        rows = slice(j * half, (j + 1) * half)
        queries = [stack_heads(q_ref, rows, g, share, dim) for g in range(groups)]
        outs = [stack_heads(g_ref, rows, g, share, dim) for g in range(groups)]
        levels = [level_ref[j * groups + g] for g in range(groups)]
        deltas = []
        for g in range(groups):
            turned = jnp.concatenate(
                [
                    outs[g][h * half : (h + 1) * half].astype(jnp.float32).T
                    for h in range(share)
                ],
                axis=1,
            )
            deltas.append(jnp.sum(turned * mixed_ref[j * groups + g], axis=0, keepdims=True))

        def visit(p, carry):
            place = pl.multiple_of(places[p] * half, half)
            allowed = allowed_of(p, position, start, half, share)
            fresh = []
            for g in range(groups):
                keys = held[pl.ds(place, half), g * dim : (g + 1) * dim]
                values = held[pl.ds(place, half), width + g * dim : width + (g + 1) * dim]
                logits = mm_nt(keys, queries[g]) * factor
                chance = jnp.where(allowed, jnp.exp2(logits - levels[g]), 0.0)
                slopes = mm_nt(values, outs[g])
                score = (chance * (slopes - deltas[g])).astype(jnp.bfloat16)
                sums[pl.ds(place, half), g * dim : (g + 1) * dim] += mm(score, queries[g])
                sums[pl.ds(place, half), width + g * dim : width + (g + 1) * dim] += mm(
                    chance.astype(jnp.bfloat16), outs[g]
                )
                fresh.append(carry[g] + mm_tn(keys, score))
            return tuple(fresh)

        empty = jnp.zeros((dim, columns), jnp.float32)
        done = lax.fori_loop(lowest, span + 1, visit, (empty,) * groups)
        for g in range(groups):
            for h in range(share):
                head = g * share + h
                dq_ref[rows, head * dim : (head + 1) * dim] = (
                    (done[g][:, h * half : (h + 1) * half].T * scale).astype(dq_ref.dtype)
                )
    tokens = 2 * half
    for k in range(peers):
        out, at = (even_ref, odd_ref)[k % 2], k // 2
        part = sums[k * tokens : (k + 1) * tokens, :]
        out[at, :, :width] = (part[:, :width] * scale).astype(out.dtype)
        out[at, :, width:] = part[:, width:].astype(out.dtype)


def grads(q, g, level, mixed, blocks, span_order, doc_lengths, sizes):
    peers, half, groups, share, dim, docs = sizes
    tokens, width = 2 * half, groups * dim
    columns = share * half
    terms = jax.ShapeDtypeStruct((peers // 2, tokens, 2 * width), jnp.bfloat16)
    return pl.pallas_call(
        functools.partial(grads_body, sizes),
        in_specs=[pl.BlockSpec(memory_space=pltpu.SMEM)] * 2
        + [pl.BlockSpec(memory_space=VMEM)] * (4 + peers),
        out_specs=[pl.BlockSpec(memory_space=VMEM)] * 3,
        out_shape=[jax.ShapeDtypeStruct(q.shape, jnp.bfloat16), terms, terms],
        scratch_shapes=[
            VMEM((peers * tokens, 2 * width), jnp.bfloat16),
            VMEM((peers * tokens, 2 * width), jnp.float32),
            pltpu.SMEM((2 * peers,), jnp.int32),
        ],
        compiler_params=params(48),
        cost_estimate=cost(18 * peers * half * half * columns * groups, 12 * MIB),
        name="grads",
    )(span_order, doc_lengths, q, g, level, mixed, *blocks)


def swap(x, k, size):
    return lax.ppermute(x, "ctx", [(i, i ^ k) for i in range(size)])


def gather_ctx(x):
    size = lax.axis_size("ctx")
    even = [x] + [swap(x, k, size) for k in range(2, size, 2)]
    odd = [swap(block, 1, size) for block in even]
    return [block for pair in zip(even, odd) for block in pair]


def pair_body(even_ref, odd_ref, *outs):
    for k, out in enumerate(outs):
        out[...] = (
            even_ref[k].astype(jnp.float32) + odd_ref[k].astype(jnp.float32)
        ).astype(out.dtype)


def scatter_ctx(even, odd):
    size = lax.axis_size("ctx")
    count, rows, width = even.shape
    got = swap(odd, 1, size)
    pairs = pl.pallas_call(
        pair_body,
        in_specs=[pl.BlockSpec(memory_space=VMEM)] * 2,
        out_specs=[pl.BlockSpec(memory_space=VMEM)] * count,
        out_shape=[jax.ShapeDtypeStruct((rows, width), jnp.bfloat16)] * count,
        compiler_params=params(24),
        cost_estimate=cost(even.size, 6 * even.size),
        name="pair_sums",
    )(even, got)
    return [pairs[0]] + [swap(pairs[k], 2 * k, size) for k in range(1, count)]


def shards(inputs, out_grad, w_query, w_key, value_projection, w_out, doc_lengths, span_order):
    tokens = inputs.shape[0]
    share = ASKER_NUM // SHARED_KV_NUM
    sizes = (
        lax.axis_size("ctx"),
        tokens // 2,
        w_key.shape[1] // CHANNEL_DIM,
        share,
        CHANNEL_DIM,
        doc_lengths.shape[0],
    )
    gathered = lax.all_gather(out_grad, "head", axis=1, tiled=True)
    own = project_kv(inputs, w_key, value_projection)
    blocks = gather_ctx(own)
    query = project(inputs, w_query)
    level, mixed = stats(query, blocks, span_order, doc_lengths, sizes)
    context_grad = back_project(gathered, w_out)
    query_grad, even, odd = grads(
        query, context_grad, level, mixed, blocks, span_order, doc_lengths, sizes
    )
    terms = scatter_ctx(even, odd)
    partial_value = input_terms(query_grad, terms, w_query, w_key, value_projection)
    return lax.psum_scatter(partial_value, "head", scatter_dimension=1, tiled=True)


def solution(mesh):
    in_specs = (
        P("ctx", None),
        P("ctx", "head"),
        P(None, "head"),
        P(None, "head"),
        P(None, "head"),
        P("head", None),
        P(),
        P(),
    )
    out_specs = P("ctx", "head")
    return jax.shard_map(shards, mesh=mesh, in_specs=in_specs, out_specs=out_specs, check_vma=False)
```

```python
import functools
import math

import jax
import jax.numpy as jnp
from jax import lax
from jax.experimental import pallas as pl
from jax.experimental.pallas import tpu as pltpu
from jax.sharding import PartitionSpec as P

ASKER_NUM = 32
SHARED_KV_NUM = 8
CHANNEL_DIM = 128

masked_score = -1e30
MIB = 1 << 20
VMEM = pltpu.VMEM


def mm(a, b):
    return lax.dot_general(a, b, (((1,), (0,)), ((), ())), preferred_element_type=jnp.float32)


def mm_nt(a, b):
    return lax.dot_general(a, b, (((1,), (1,)), ((), ())), preferred_element_type=jnp.float32)


def mm_tn(a, b):
    return lax.dot_general(a, b, (((0,), (0,)), ((), ())), preferred_element_type=jnp.float32)


def params():
    return pltpu.CompilerParams(vmem_limit_bytes=56 * MIB)


def cost(flops, moved):
    return pl.CostEstimate(flops=flops, bytes_accessed=moved, transcendentals=0)


def head_index():
    return lax.axis_index("head").astype(jnp.int32).reshape(1)


def upper_half(order):
    first = order[2 * lax.axis_index("ctx")]
    return jnp.where(2 * first >= order.shape[0], 0, 1)


def kv_body(x_ref, wk_ref, wv_ref, out_ref, acc):
    width = wk_ref.shape[1]
    step = pl.program_id(0)

    @pl.when(step == 0)
    def _():
        acc[...] = jnp.zeros_like(acc)

    x = x_ref[...]
    acc[:, :width] += mm(x, wk_ref[...])
    acc[:, width:] += mm(x, wv_ref[...])

    @pl.when(step == pl.num_programs(0) - 1)
    def _():
        out_ref[...] = acc[...].astype(out_ref.dtype)


def project_kv(x, wk, wv):
    tokens, depth = x.shape
    width = wk.shape[1]
    part = min(depth, 1024)
    return pl.pallas_call(
        kv_body,
        grid=(depth // part,),
        in_specs=[
            pl.BlockSpec((tokens, part), lambda i: (0, i)),
            pl.BlockSpec((part, width), lambda i: (i, 0)),
            pl.BlockSpec((part, width), lambda i: (i, 0)),
        ],
        out_specs=pl.BlockSpec((tokens, 2 * width), lambda i: (0, 0)),
        out_shape=jax.ShapeDtypeStruct((tokens, 2 * width), jnp.bfloat16),
        scratch_shapes=[VMEM((tokens, 2 * width), jnp.float32)],
        compiler_params=params(),
        cost_estimate=cost(4 * tokens * depth * width, 2 * depth * (tokens + 2 * width)),
        name="project_kv",
    )(x, wk, wv)


def project_body(x_ref, w_ref, out_ref):
    out_ref[...] = mm(x_ref[...], w_ref[...]).astype(out_ref.dtype)


def project(x, w):
    tokens, depth = x.shape
    width = w.shape[1]
    part = min(width, 256)
    return pl.pallas_call(
        project_body,
        grid=(width // part,),
        in_specs=[
            pl.BlockSpec((tokens, depth), lambda i: (0, 0)),
            pl.BlockSpec((depth, part), lambda i: (0, i)),
        ],
        out_specs=pl.BlockSpec((tokens, part), lambda i: (0, i)),
        out_shape=jax.ShapeDtypeStruct((tokens, width), jnp.bfloat16),
        compiler_params=params(),
        cost_estimate=cost(2 * tokens * depth * width, 2 * depth * (tokens + width)),
        name="project",
    )(x, w)


def split_body(order, x_ref, upper_ref, lower_ref):
    half = upper_ref.shape[0]
    at = upper_half(order) * half
    upper_ref[...] = x_ref[pl.ds(pl.multiple_of(at, half), half), :]
    lower_ref[...] = x_ref[pl.ds(pl.multiple_of(half - at, half), half), :]


def split_rows(x, span_order):
    tokens, width = x.shape
    return pl.pallas_call(
        split_body,
        in_specs=[pl.BlockSpec(memory_space=pltpu.SMEM), pl.BlockSpec(memory_space=VMEM)],
        out_specs=[pl.BlockSpec(memory_space=VMEM)] * 2,
        out_shape=[jax.ShapeDtypeStruct((tokens // 2, width), x.dtype)] * 2,
        compiler_params=params(),
        cost_estimate=cost(0, 4 * x.size),
        name="split_rows",
    )(span_order, x)


def back_body(*refs):
    w_ref, out_ref = refs[-2:]
    me = lax.axis_index("head")
    total = None
    for k, x_ref in enumerate(refs[:-2]):
        depth = x_ref.shape[1]
        at = pl.multiple_of((me ^ k) * depth, depth)
        term = mm_nt(x_ref[...], w_ref[:, pl.ds(at, depth)])
        total = term if total is None else total + term
    out_ref[...] = total.astype(out_ref.dtype)


def back_project(blocks, w):
    rows, depth = blocks[0].shape
    width = w.shape[0]
    part = min(width, 256)
    return pl.pallas_call(
        back_body,
        grid=(width // part,),
        in_specs=[pl.BlockSpec((rows, depth), lambda i: (0, 0))] * len(blocks)
        + [pl.BlockSpec((part, w.shape[1]), lambda i: (i, 0))],
        out_specs=pl.BlockSpec((rows, part), lambda i: (0, i)),
        out_shape=jax.ShapeDtypeStruct((rows, width), jnp.bfloat16),
        compiler_params=params(),
        cost_estimate=cost(2 * rows * w.size, 2 * w.size),
        name="back_project",
    )(*blocks, w)


def query_terms_body(me, dq_ref, w_ref, out_ref):
    out_ref[0] = mm_nt(dq_ref[...], w_ref[...])


def query_terms(dq, w, size):
    rows, depth = dq.shape
    share = w.shape[0] // size
    part = min(share, 512)
    count = share // part
    return pl.pallas_call(
        query_terms_body,
        grid_spec=pltpu.PrefetchScalarGridSpec(
            num_scalar_prefetch=1,
            grid=(size, count),
            in_specs=[
                pl.BlockSpec((rows, depth), lambda k, i, me: (0, 0)),
                pl.BlockSpec((part, depth), lambda k, i, me: ((me[0] ^ k) * count + i, 0)),
            ],
            out_specs=pl.BlockSpec((1, rows, part), lambda k, i, me: (k, 0, i)),
        ),
        out_shape=jax.ShapeDtypeStruct((size, rows, share), jnp.float32),
        compiler_params=params(),
        cost_estimate=cost(2 * rows * w.size, 2 * w.size + 4 * rows * w.shape[0]),
        name="query_terms",
    )(head_index(), dq, w)


def all_terms_body(count, me, first_ref, *refs):
    terms = refs[:count]
    wk_ref, wv_ref, out_ref, grads = refs[count:]
    width = wk_ref.shape[1]

    @pl.when((pl.program_id(0) == 0) & (pl.program_id(1) == 0))
    def _():
        total = terms[0][...].astype(jnp.float32)
        for term in terms[1:]:
            total = total + term[...].astype(jnp.float32)
        grads[...] = total.astype(grads.dtype)

    total = first_ref[0] + mm_nt(grads[:, :width], wk_ref[...])
    total = total + mm_nt(grads[:, width:], wv_ref[...])
    out_ref[0] = total.astype(out_ref.dtype)


def all_terms(first, terms, wk, wv):
    size, rows, share = first.shape
    width = wk.shape[1]
    part = min(share, 1024)
    count = share // part
    return pl.pallas_call(
        functools.partial(all_terms_body, len(terms)),
        grid_spec=pltpu.PrefetchScalarGridSpec(
            num_scalar_prefetch=1,
            grid=(size, count),
            in_specs=[pl.BlockSpec((1, rows, part), lambda k, i, me: (k, 0, i))]
            + [pl.BlockSpec((rows, 2 * width), lambda k, i, me: (0, 0))] * len(terms)
            + [pl.BlockSpec((part, width), lambda k, i, me: ((me[0] ^ k) * count + i, 0))] * 2,
            out_specs=pl.BlockSpec((1, rows, part), lambda k, i, me: (k, 0, i)),
            scratch_shapes=[VMEM((rows, 2 * width), jnp.bfloat16)],
        ),
        out_shape=jax.ShapeDtypeStruct((size, rows, share), jnp.bfloat16),
        compiler_params=params(),
        cost_estimate=cost(4 * rows * wk.size, 4 * wk.size + 6 * first.size),
        name="all_terms",
    )(head_index(), first, *terms, wk, wv)


def join_body(count, order, *refs):
    out_ref = refs[-1]
    half = refs[0].shape[0]
    at = upper_half(order) * half
    for j, place in enumerate((at, half - at)):
        total = refs[j * count][...].astype(jnp.float32)
        for ref in refs[j * count + 1 : (j + 1) * count]:
            total = total + ref[...].astype(jnp.float32)
        out_ref[pl.ds(pl.multiple_of(place, half), half), :] = total.astype(out_ref.dtype)


def join_rows(upper, lower, span_order):
    rows, width = upper[0].shape
    return pl.pallas_call(
        functools.partial(join_body, len(upper)),
        in_specs=[pl.BlockSpec(memory_space=pltpu.SMEM)]
        + [pl.BlockSpec(memory_space=VMEM)] * (2 * len(upper)),
        out_specs=pl.BlockSpec(memory_space=VMEM),
        out_shape=jax.ShapeDtypeStruct((2 * rows, width), jnp.bfloat16),
        compiler_params=params(),
        cost_estimate=cost(8 * rows * width, 20 * rows * width),
        name="join_rows",
    )(span_order, *upper, *lower)


def find_places(order, places, me, spans):
    for i in range(spans):
        places[order[i]] = ((i // 2) ^ me) * 2 + (i % 2)


def own_span(order, lengths, docs, me, j, half):
    span = order[2 * me + j]
    position = span * half + lax.broadcasted_iota(jnp.int32, (1, half), 1)
    first, end = 0, 0
    start = jnp.zeros((1, half), jnp.int32)
    for k in range(docs):
        end = end + lengths[k]
        start = jnp.where(position >= end, end, start)
        first = jnp.where(span * half >= end, end, first)
    return span, position, start, first // half


def stack_heads(ref, rows, group, share, dim):
    base = group * share
    return jnp.concatenate(
        [ref[rows, (base + h) * dim : (base + h + 1) * dim] for h in range(share)], axis=0
    )


def load_blocks(refs, held):
    rows = refs[0].shape[0]
    for k, ref in enumerate(refs):
        held[k * rows : (k + 1) * rows, :] = ref[...]


def allowed_of(p, position, start, half, share):
    key = p * half + lax.broadcasted_iota(jnp.int32, (half, 1), 0)
    allowed = (key <= position) & (key >= start)
    return jnp.concatenate([allowed] * share, axis=1)


def stats_body(sizes, order, lengths, q_ref, *refs):
    peers, half, groups, share, dim, docs = sizes
    blocks = refs[:peers]
    level_ref, mixed_ref, held, places = refs[peers:]
    me = lax.axis_index("ctx")
    width = groups * dim
    factor = math.log2(math.e) / math.sqrt(dim)
    find_places(order, places, me, 2 * peers)
    load_blocks(blocks, held)
    columns = share * half
    for j in range(2):
        span, position, start, lowest = own_span(order, lengths, docs, me, j, half)
        rows = slice(j * half, (j + 1) * half)
        queries = [stack_heads(q_ref, rows, g, share, dim) for g in range(groups)]

        def visit(p, carry):
            place = pl.multiple_of(places[p] * half, half)
            allowed = allowed_of(p, position, start, half, share)
            fresh = []
            for g in range(groups):
                top, total, mixed = carry[g]
                keys = held[pl.ds(place, half), g * dim : (g + 1) * dim]
                values = held[pl.ds(place, half), width + g * dim : width + (g + 1) * dim]
                logits = mm_nt(keys, queries[g]) * factor
                logits = jnp.where(allowed, logits, masked_score)
                higher = jnp.maximum(top, jnp.max(logits, axis=0, keepdims=True))
                weights = jnp.where(allowed, jnp.exp2(logits - higher), 0.0)
                fade = jnp.exp2(top - higher)
                total = total * fade + jnp.sum(weights, axis=0, keepdims=True)
                mixed = mixed * fade + mm_tn(values, weights.astype(jnp.bfloat16))
                fresh.append((higher, total, mixed))
            return tuple(fresh)

        empty = (
            jnp.full((1, columns), masked_score, jnp.float32),
            jnp.zeros((1, columns), jnp.float32),
            jnp.zeros((dim, columns), jnp.float32),
        )
        done = lax.fori_loop(lowest, span + 1, visit, (empty,) * groups)
        for g in range(groups):
            top, total, mixed = done[g]
            level_ref[j * groups + g] = top + jnp.log2(total)
            mixed_ref[j * groups + g] = mixed / total


def stats(q, blocks, span_order, doc_lengths, sizes):
    peers, half, groups, share, dim, docs = sizes
    columns = share * half
    return pl.pallas_call(
        functools.partial(stats_body, sizes),
        in_specs=[pl.BlockSpec(memory_space=pltpu.SMEM)] * 2
        + [pl.BlockSpec(memory_space=VMEM)] * (1 + peers),
        out_specs=[pl.BlockSpec(memory_space=VMEM)] * 2,
        out_shape=[
            jax.ShapeDtypeStruct((2 * groups, 1, columns), jnp.float32),
            jax.ShapeDtypeStruct((2 * groups, dim, columns), jnp.float32),
        ],
        scratch_shapes=[
            VMEM((2 * peers * half, 2 * groups * dim), jnp.bfloat16),
            pltpu.SMEM((2 * peers,), jnp.int32),
        ],
        compiler_params=params(),
        cost_estimate=cost(9 * peers * half * half * columns * groups * dim // dim, 6 * MIB),
        name="stats",
    )(span_order, doc_lengths, q, *blocks)


def grads_body(sizes, upper, order, lengths, q_ref, g_ref, level_ref, mixed_ref, *refs):
    peers, half, groups, share, dim, docs = sizes
    spans = 2 * peers
    if upper:
        blocks = refs[:peers]
        dq_ref, even_ref, odd_ref, rest_ref, held, sums, places = refs[peers:]
    else:
        rest_ref, blocks = refs[0], refs[1 : 1 + peers]
        dq_ref, even_ref, odd_ref, held, sums, places = refs[1 + peers :]
    me = lax.axis_index("ctx")
    width = groups * dim
    scale = 1.0 / math.sqrt(dim)
    factor = math.log2(math.e) * scale
    find_places(order, places, me, spans)
    load_blocks(blocks, held)
    columns = share * half
    at = upper_half(order)
    j = at if upper else 1 - at
    span, position, start, lowest = own_span(order, lengths, docs, me, j, half)
    if upper:
        sums[...] = jnp.zeros_like(sums)
    else:
        sums[...] = rest_ref[...]
    rows = pl.ds(pl.multiple_of(j * half, half), half)
    queries = [stack_heads(q_ref, rows, g, share, dim) for g in range(groups)]
    outs = [stack_heads(g_ref, slice(0, half), g, share, dim) for g in range(groups)]
    levels = [level_ref[j * groups + g] for g in range(groups)]
    deltas = []
    for g in range(groups):
        turned = jnp.concatenate(
            [outs[g][h * half : (h + 1) * half].astype(jnp.float32).T for h in range(share)],
            axis=1,
        )
        deltas.append(jnp.sum(turned * mixed_ref[j * groups + g], axis=0, keepdims=True))

    def visit(p, carry):
        place = pl.multiple_of(places[p] * half, half)
        target = pl.ds(pl.multiple_of(p * half, half), half)
        allowed = allowed_of(p, position, start, half, share)
        fresh = []
        for g in range(groups):
            keys = held[pl.ds(place, half), g * dim : (g + 1) * dim]
            values = held[pl.ds(place, half), width + g * dim : width + (g + 1) * dim]
            logits = mm_nt(keys, queries[g]) * factor
            chance = jnp.where(allowed, jnp.exp2(logits - levels[g]), 0.0)
            slopes = mm_nt(values, outs[g])
            score = (chance * (slopes - deltas[g])).astype(jnp.bfloat16)
            sums[target, g * dim : (g + 1) * dim] += mm(score, queries[g])
            sums[target, width + g * dim : width + (g + 1) * dim] += mm(
                chance.astype(jnp.bfloat16), outs[g]
            )
            fresh.append(carry[g] + mm_tn(keys, score))
        return tuple(fresh)

    empty = jnp.zeros((dim, columns), jnp.float32)
    done = lax.fori_loop(lowest, span + 1, visit, (empty,) * groups)
    for g in range(groups):
        for h in range(share):
            head = g * share + h
            dq_ref[:, head * dim : (head + 1) * dim] = (
                (done[g][:, h * half : (h + 1) * half].T * scale).astype(dq_ref.dtype)
            )
    for k in range(peers):
        out, slot = (even_ref, odd_ref)[k % 2], k // 2
        first = order[2 * (me ^ k)]
        other = spans - 1 - first
        pick = jnp.maximum(first, other) if upper else jnp.minimum(first, other)
        part = pl.ds(pl.multiple_of(pick * half, half), half)
        out[slot, :, :width] = (sums[part, :width] * scale).astype(out.dtype)
        out[slot, :, width:] = sums[part, width:].astype(out.dtype)
    if upper:
        rest_ref[...] = sums[: peers * half, :]


def grads(upper, q, g, level, mixed, rest, blocks, span_order, doc_lengths, sizes):
    peers, half, groups, share, dim, docs = sizes
    tokens, width = 2 * half, groups * dim
    columns = share * half
    terms = jax.ShapeDtypeStruct((peers // 2, half, 2 * width), jnp.bfloat16)
    rests = jax.ShapeDtypeStruct((peers * half, 2 * width), jnp.float32)
    outs = [jax.ShapeDtypeStruct(g.shape, jnp.bfloat16), terms, terms] + [rests] * upper
    return pl.pallas_call(
        functools.partial(grads_body, sizes, upper),
        in_specs=[pl.BlockSpec(memory_space=pltpu.SMEM)] * 2
        + [pl.BlockSpec(memory_space=VMEM)] * (4 + len(rest) + peers),
        out_specs=[pl.BlockSpec(memory_space=VMEM)] * len(outs),
        out_shape=outs,
        scratch_shapes=[
            VMEM((peers * tokens, 2 * width), jnp.bfloat16),
            VMEM(((2 if upper else 1) * peers * half, 2 * width), jnp.float32),
            pltpu.SMEM((2 * peers,), jnp.int32),
        ],
        compiler_params=params(),
        cost_estimate=cost((12 if upper else 6) * peers * half * half * columns * groups, 8 * MIB),
        name="upper_grads" if upper else "lower_grads",
    )(span_order, doc_lengths, q, g, level, mixed, *rest, *blocks)


def swap(x, k, axis):
    return lax.ppermute(x, axis, [(i, i ^ k) for i in range(lax.axis_size(axis))])


def gather_ctx(x):
    even = [x] + [swap(x, k, "ctx") for k in range(2, lax.axis_size("ctx"), 2)]
    odd = [swap(block, 1, "ctx") for block in even]
    return [block for pair in zip(even, odd) for block in pair]


def gather_head(x):
    return [x] + [swap(x, k, "head") for k in range(1, lax.axis_size("head"))]


def scatter_head(x):
    return [x[0]] + [swap(x[k], k, "head") for k in range(1, lax.axis_size("head"))]


def pair_body(even_ref, odd_ref, *outs):
    for k, out in enumerate(outs):
        out[...] = (
            even_ref[k].astype(jnp.float32) + odd_ref[k].astype(jnp.float32)
        ).astype(out.dtype)


def scatter_ctx(even, odd):
    count, rows, width = even.shape
    got = swap(odd, 1, "ctx")
    pairs = pl.pallas_call(
        pair_body,
        in_specs=[pl.BlockSpec(memory_space=VMEM)] * 2,
        out_specs=[pl.BlockSpec(memory_space=VMEM)] * count,
        out_shape=[jax.ShapeDtypeStruct((rows, width), jnp.bfloat16)] * count,
        compiler_params=params(),
        cost_estimate=cost(even.size, 6 * even.size),
        name="pair_sums",
    )(even, got)
    return [pairs[0]] + [swap(pairs[k], 2 * k, "ctx") for k in range(1, count)]


def shards(inputs, out_grad, w_query, w_key, value_projection, w_out, doc_lengths, span_order):
    tokens = inputs.shape[0]
    share = ASKER_NUM // SHARED_KV_NUM
    sizes = (
        lax.axis_size("ctx"),
        tokens // 2,
        w_key.shape[1] // CHANNEL_DIM,
        share,
        CHANNEL_DIM,
        doc_lengths.shape[0],
    )
    heads = lax.axis_size("head")
    upper_out, lower_out = split_rows(out_grad, span_order)
    upper_out = gather_head(upper_out)
    own = project_kv(inputs, w_key, value_projection)
    blocks = gather_ctx(own)
    query = project(inputs, w_query)
    level, mixed = stats(query, blocks, span_order, doc_lengths, sizes)
    upper_out, lower_out = lax.optimization_barrier((upper_out, lower_out))
    context_grad = back_project(upper_out, w_out)
    lower_out = gather_head(lower_out)
    query_grad, even, odd, rest = grads(
        True, query, context_grad, level, mixed, (), blocks, span_order, doc_lengths, sizes
    )
    first = query_terms(query_grad, w_query, heads)
    terms = scatter_ctx(even, odd)
    upper = scatter_head(all_terms(first, terms, w_key, value_projection))
    context_grad = back_project(lower_out, w_out)
    query_grad, even, odd = grads(
        False, query, context_grad, level, mixed, (rest,), blocks, span_order, doc_lengths, sizes
    )
    first = query_terms(query_grad, w_query, heads)
    terms = scatter_ctx(even, odd)
    lower = scatter_head(all_terms(first, terms, w_key, value_projection))
    return join_rows(upper, lower, span_order)


def solution(mesh):
    in_specs = (
        P("ctx", None),
        P("ctx", "head"),
        P(None, "head"),
        P(None, "head"),
        P(None, "head"),
        P("head", None),
        P(),
        P(),
    )
    out_specs = P("ctx", "head")
    return jax.shard_map(shards, mesh=mesh, in_specs=in_specs, out_specs=out_specs, check_vma=False)
```

```python
import functools
import math

import jax
import jax.numpy as jnp
from jax import lax
from jax.experimental import pallas as pl
from jax.experimental.pallas import tpu as pltpu
from jax.sharding import PartitionSpec as P

ASKER_NUM = 32
SHARED_KV_NUM = 8
CHANNEL_DIM = 128

masked_score = -1e30
MIB = 1 << 20
VMEM = pltpu.VMEM


def mm(a, b):
    return lax.dot_general(a, b, (((1,), (0,)), ((), ())), preferred_element_type=jnp.float32)


def mm_nt(a, b):
    return lax.dot_general(a, b, (((1,), (1,)), ((), ())), preferred_element_type=jnp.float32)


def mm_tn(a, b):
    return lax.dot_general(a, b, (((0,), (0,)), ((), ())), preferred_element_type=jnp.float32)


def params():
    return pltpu.CompilerParams(vmem_limit_bytes=20 * MIB)


def cost(flops, moved):
    return pl.CostEstimate(flops=flops, bytes_accessed=moved, transcendentals=0)


def head_index():
    return lax.axis_index("head").astype(jnp.int32).reshape(1)


def upper_half(order):
    first = order[2 * lax.axis_index("ctx")]
    return jnp.where(2 * first >= order.shape[0], 0, 1)


def kv_body(x_ref, wk_ref, wv_ref, out_ref, acc):
    width = wk_ref.shape[1]
    step = pl.program_id(0)

    @pl.when(step == 0)
    def _():
        acc[...] = jnp.zeros_like(acc)

    x = x_ref[...]
    acc[:, :width] += mm(x, wk_ref[...])
    acc[:, width:] += mm(x, wv_ref[...])

    @pl.when(step == pl.num_programs(0) - 1)
    def _():
        out_ref[...] = acc[...].astype(out_ref.dtype)


def project_kv(x, wk, wv):
    tokens, depth = x.shape
    width = wk.shape[1]
    part = min(depth, 1024)
    return pl.pallas_call(
        kv_body,
        grid=(depth // part,),
        in_specs=[
            pl.BlockSpec((tokens, part), lambda i: (0, i)),
            pl.BlockSpec((part, width), lambda i: (i, 0)),
            pl.BlockSpec((part, width), lambda i: (i, 0)),
        ],
        out_specs=pl.BlockSpec((tokens, 2 * width), lambda i: (0, 0)),
        out_shape=jax.ShapeDtypeStruct((tokens, 2 * width), jnp.bfloat16),
        scratch_shapes=[VMEM((tokens, 2 * width), jnp.float32)],
        compiler_params=params(),
        cost_estimate=cost(4 * tokens * depth * width, 2 * depth * (tokens + 2 * width)),
        name="project_kv",
    )(x, wk, wv)


def project_body(x_ref, w_ref, out_ref):
    out_ref[...] = mm(x_ref[...], w_ref[...]).astype(out_ref.dtype)


def project(x, w):
    tokens, depth = x.shape
    width = w.shape[1]
    part = min(width, 256)
    return pl.pallas_call(
        project_body,
        grid=(width // part,),
        in_specs=[
            pl.BlockSpec((tokens, depth), lambda i: (0, 0)),
            pl.BlockSpec((depth, part), lambda i: (0, i)),
        ],
        out_specs=pl.BlockSpec((tokens, part), lambda i: (0, i)),
        out_shape=jax.ShapeDtypeStruct((tokens, width), jnp.bfloat16),
        compiler_params=params(),
        cost_estimate=cost(2 * tokens * depth * width, 2 * depth * (tokens + width)),
        name="project",
    )(x, w)


def split_body(order, x_ref, upper_ref, lower_ref):
    half = upper_ref.shape[0]
    at = upper_half(order) * half
    upper_ref[...] = x_ref[pl.ds(pl.multiple_of(at, half), half), :]
    lower_ref[...] = x_ref[pl.ds(pl.multiple_of(half - at, half), half), :]


def split_rows(x, span_order):
    tokens, width = x.shape
    return pl.pallas_call(
        split_body,
        in_specs=[pl.BlockSpec(memory_space=pltpu.SMEM), pl.BlockSpec(memory_space=VMEM)],
        out_specs=[pl.BlockSpec(memory_space=VMEM)] * 2,
        out_shape=[jax.ShapeDtypeStruct((tokens // 2, width), x.dtype)] * 2,
        compiler_params=params(),
        cost_estimate=cost(0, 4 * x.size),
        name="split_rows",
    )(span_order, x)


def back_body(*refs):
    w_ref, out_ref = refs[-2:]
    me = lax.axis_index("head")
    total = None
    for k, x_ref in enumerate(refs[:-2]):
        depth = x_ref.shape[1]
        at = pl.multiple_of((me ^ k) * depth, depth)
        term = mm_nt(x_ref[...], w_ref[:, pl.ds(at, depth)])
        total = term if total is None else total + term
    out_ref[...] = total.astype(out_ref.dtype)


def back_project(blocks, w):
    rows, depth = blocks[0].shape
    width = w.shape[0]
    part = min(width, 256)
    return pl.pallas_call(
        back_body,
        grid=(width // part,),
        in_specs=[pl.BlockSpec((rows, depth), lambda i: (0, 0))] * len(blocks)
        + [pl.BlockSpec((part, w.shape[1]), lambda i: (i, 0))],
        out_specs=pl.BlockSpec((rows, part), lambda i: (0, i)),
        out_shape=jax.ShapeDtypeStruct((rows, width), jnp.bfloat16),
        compiler_params=params(),
        cost_estimate=cost(2 * rows * w.size, 2 * w.size),
        name="back_project",
    )(*blocks, w)


def query_terms_body(me, dq_ref, w_ref, out_ref):
    out_ref[...] = mm_nt(dq_ref[...], w_ref[...])


def query_terms(dq, w, size, k):
    rows, depth = dq.shape
    share = w.shape[0] // size
    part = min(share, 256)
    count = share // part
    return pl.pallas_call(
        query_terms_body,
        grid_spec=pltpu.PrefetchScalarGridSpec(
            num_scalar_prefetch=1,
            grid=(count,),
            in_specs=[
                pl.BlockSpec((rows, depth), lambda i, me: (0, 0)),
                pl.BlockSpec((part, depth), lambda i, me: ((me[0] ^ k) * count + i, 0)),
            ],
            out_specs=pl.BlockSpec((rows, part), lambda i, me: (0, i)),
        ),
        out_shape=jax.ShapeDtypeStruct((rows, share), jnp.float32),
        compiler_params=params(),
        cost_estimate=cost(2 * rows * share * depth, 2 * share * depth + 4 * rows * share),
        name="query_terms",
    )(head_index(), dq, w)


def all_terms_body(count, me, first_ref, *refs):
    terms = refs[:count]
    wk_ref, wv_ref, out_ref, grads = refs[count:]
    width = wk_ref.shape[1]

    @pl.when(pl.program_id(0) == 0)
    def _():
        total = terms[0][...].astype(jnp.float32)
        for term in terms[1:]:
            total = total + term[...].astype(jnp.float32)
        grads[...] = total.astype(grads.dtype)

    total = first_ref[...] + mm_nt(grads[:, :width], wk_ref[...])
    total = total + mm_nt(grads[:, width:], wv_ref[...])
    out_ref[...] = total.astype(out_ref.dtype)


def all_terms(first, terms, wk, wv, k):
    rows, share = first.shape
    width = wk.shape[1]
    part = min(share, 512)
    count = share // part
    return pl.pallas_call(
        functools.partial(all_terms_body, len(terms)),
        grid_spec=pltpu.PrefetchScalarGridSpec(
            num_scalar_prefetch=1,
            grid=(count,),
            in_specs=[pl.BlockSpec((rows, part), lambda i, me: (0, i))]
            + [pl.BlockSpec((rows, 2 * width), lambda i, me: (0, 0))] * len(terms)
            + [pl.BlockSpec((part, width), lambda i, me: ((me[0] ^ k) * count + i, 0))] * 2,
            out_specs=pl.BlockSpec((rows, part), lambda i, me: (0, i)),
            scratch_shapes=[VMEM((rows, 2 * width), jnp.bfloat16)],
        ),
        out_shape=jax.ShapeDtypeStruct((rows, share), jnp.bfloat16),
        compiler_params=params(),
        cost_estimate=cost(4 * rows * share * width, 4 * share * width + 6 * rows * share),
        name="all_terms",
    )(head_index(), first, *terms, wk, wv)


def join_body(count, order, *refs):
    out_ref = refs[-1]
    half = refs[0].shape[0]
    at = upper_half(order) * half
    for j, place in enumerate((at, half - at)):
        total = refs[j * count][...].astype(jnp.float32)
        for ref in refs[j * count + 1 : (j + 1) * count]:
            total = total + ref[...].astype(jnp.float32)
        out_ref[pl.ds(pl.multiple_of(place, half), half), :] = total.astype(out_ref.dtype)


def join_rows(upper, lower, span_order):
    rows, width = upper[0].shape
    return pl.pallas_call(
        functools.partial(join_body, len(upper)),
        in_specs=[pl.BlockSpec(memory_space=pltpu.SMEM)]
        + [pl.BlockSpec(memory_space=VMEM)] * (2 * len(upper)),
        out_specs=pl.BlockSpec(memory_space=VMEM),
        out_shape=jax.ShapeDtypeStruct((2 * rows, width), jnp.bfloat16),
        compiler_params=params(),
        cost_estimate=cost(8 * rows * width, 20 * rows * width),
        name="join_rows",
    )(span_order, *upper, *lower)


def find_places(order, places, me, spans):
    for i in range(spans):
        places[order[i]] = ((i // 2) ^ me) * 2 + (i % 2)


def own_span(order, lengths, docs, me, j, half):
    span = order[2 * me + j]
    position = span * half + lax.broadcasted_iota(jnp.int32, (1, half), 1)
    first, end = 0, 0
    start = jnp.zeros((1, half), jnp.int32)
    for k in range(docs):
        end = end + lengths[k]
        start = jnp.where(position >= end, end, start)
        first = jnp.where(span * half >= end, end, first)
    return span, position, start, first // half


def stack_heads(ref, rows, group, share, dim):
    base = group * share
    return jnp.concatenate(
        [ref[rows, (base + h) * dim : (base + h + 1) * dim] for h in range(share)], axis=0
    )


def load_blocks(refs, held):
    rows = refs[0].shape[0]
    for k, ref in enumerate(refs):
        held[k * rows : (k + 1) * rows, :] = ref[...]


def allowed_of(p, position, start, half, share):
    key = p * half + lax.broadcasted_iota(jnp.int32, (half, 1), 0)
    allowed = (key <= position) & (key >= start)
    return jnp.concatenate([allowed] * share, axis=1)


def stats_body(sizes, order, lengths, q_ref, *refs):
    peers, half, groups, share, dim, docs = sizes
    blocks = refs[:peers]
    level_ref, mixed_ref, held, places = refs[peers:]
    me = lax.axis_index("ctx")
    width = groups * dim
    factor = math.log2(math.e) / math.sqrt(dim)
    find_places(order, places, me, 2 * peers)
    load_blocks(blocks, held)
    columns = share * half
    for j in range(2):
        span, position, start, lowest = own_span(order, lengths, docs, me, j, half)
        rows = slice(j * half, (j + 1) * half)
        queries = [stack_heads(q_ref, rows, g, share, dim) for g in range(groups)]

        def visit(p, carry):
            place = pl.multiple_of(places[p] * half, half)
            allowed = allowed_of(p, position, start, half, share)
            fresh = []
            for g in range(groups):
                top, total, mixed = carry[g]
                keys = held[pl.ds(place, half), g * dim : (g + 1) * dim]
                values = held[pl.ds(place, half), width + g * dim : width + (g + 1) * dim]
                logits = mm_nt(keys, queries[g]) * factor
                logits = jnp.where(allowed, logits, masked_score)
                higher = jnp.maximum(top, jnp.max(logits, axis=0, keepdims=True))
                weights = jnp.where(allowed, jnp.exp2(logits - higher), 0.0)
                fade = jnp.exp2(top - higher)
                total = total * fade + jnp.sum(weights, axis=0, keepdims=True)
                mixed = mixed * fade + mm_tn(values, weights.astype(jnp.bfloat16))
                fresh.append((higher, total, mixed))
            return tuple(fresh)

        empty = (
            jnp.full((1, columns), masked_score, jnp.float32),
            jnp.zeros((1, columns), jnp.float32),
            jnp.zeros((dim, columns), jnp.float32),
        )
        done = lax.fori_loop(lowest, span + 1, visit, (empty,) * groups)
        for g in range(groups):
            top, total, mixed = done[g]
            level_ref[j * groups + g] = top + jnp.log2(total)
            mixed_ref[j * groups + g] = mixed / total


def stats(q, blocks, span_order, doc_lengths, sizes):
    peers, half, groups, share, dim, docs = sizes
    columns = share * half
    return pl.pallas_call(
        functools.partial(stats_body, sizes),
        in_specs=[pl.BlockSpec(memory_space=pltpu.SMEM)] * 2
        + [pl.BlockSpec(memory_space=VMEM)] * (1 + peers),
        out_specs=[pl.BlockSpec(memory_space=VMEM)] * 2,
        out_shape=[
            jax.ShapeDtypeStruct((2 * groups, 1, columns), jnp.float32),
            jax.ShapeDtypeStruct((2 * groups, dim, columns), jnp.float32),
        ],
        scratch_shapes=[
            VMEM((2 * peers * half, 2 * groups * dim), jnp.bfloat16),
            pltpu.SMEM((2 * peers,), jnp.int32),
        ],
        compiler_params=params(),
        cost_estimate=cost(9 * peers * half * half * columns * groups * dim // dim, 6 * MIB),
        name="stats",
    )(span_order, doc_lengths, q, *blocks)


def grads_body(sizes, upper, order, lengths, q_ref, g_ref, level_ref, mixed_ref, *refs):
    peers, half, groups, share, dim, docs = sizes
    spans = 2 * peers
    if upper:
        blocks = refs[:peers]
        dq_ref, even_ref, odd_ref, rest_ref, held, sums, places = refs[peers:]
    else:
        rest_ref, blocks = refs[0], refs[1 : 1 + peers]
        dq_ref, even_ref, odd_ref, held, sums, places = refs[1 + peers :]
    me = lax.axis_index("ctx")
    width = groups * dim
    scale = 1.0 / math.sqrt(dim)
    factor = math.log2(math.e) * scale
    find_places(order, places, me, spans)
    load_blocks(blocks, held)
    columns = share * half
    at = upper_half(order)
    j = at if upper else 1 - at
    span, position, start, lowest = own_span(order, lengths, docs, me, j, half)
    if upper:
        sums[...] = jnp.zeros_like(sums)
    else:
        sums[...] = rest_ref[...]
    rows = pl.ds(pl.multiple_of(j * half, half), half)
    queries = [stack_heads(q_ref, rows, g, share, dim) for g in range(groups)]
    outs = [stack_heads(g_ref, slice(0, half), g, share, dim) for g in range(groups)]
    levels = [level_ref[j * groups + g] for g in range(groups)]
    deltas = []
    for g in range(groups):
        turned = jnp.concatenate(
            [outs[g][h * half : (h + 1) * half].astype(jnp.float32).T for h in range(share)],
            axis=1,
        )
        deltas.append(jnp.sum(turned * mixed_ref[j * groups + g], axis=0, keepdims=True))

    def visit(p, carry):
        place = pl.multiple_of(places[p] * half, half)
        target = pl.ds(pl.multiple_of(p * half, half), half)
        allowed = allowed_of(p, position, start, half, share)
        fresh = []
        for g in range(groups):
            keys = held[pl.ds(place, half), g * dim : (g + 1) * dim]
            values = held[pl.ds(place, half), width + g * dim : width + (g + 1) * dim]
            logits = mm_nt(keys, queries[g]) * factor
            chance = jnp.where(allowed, jnp.exp2(logits - levels[g]), 0.0)
            slopes = mm_nt(values, outs[g])
            score = (chance * (slopes - deltas[g])).astype(jnp.bfloat16)
            sums[target, g * dim : (g + 1) * dim] += mm(score, queries[g])
            sums[target, width + g * dim : width + (g + 1) * dim] += mm(
                chance.astype(jnp.bfloat16), outs[g]
            )
            fresh.append(carry[g] + mm_tn(keys, score))
        return tuple(fresh)

    empty = jnp.zeros((dim, columns), jnp.float32)
    done = lax.fori_loop(lowest, span + 1, visit, (empty,) * groups)
    for g in range(groups):
        for h in range(share):
            head = g * share + h
            dq_ref[:, head * dim : (head + 1) * dim] = (
                (done[g][:, h * half : (h + 1) * half].T * scale).astype(dq_ref.dtype)
            )
    for k in range(peers):
        out, slot = (even_ref, odd_ref)[k % 2], k // 2
        first = order[2 * (me ^ k)]
        other = spans - 1 - first
        pick = jnp.maximum(first, other) if upper else jnp.minimum(first, other)
        part = pl.ds(pl.multiple_of(pick * half, half), half)
        out[slot, :, :width] = (sums[part, :width] * scale).astype(out.dtype)
        out[slot, :, width:] = sums[part, width:].astype(out.dtype)
    if upper:
        rest_ref[...] = sums[: peers * half, :]


def grads(upper, q, g, level, mixed, rest, blocks, span_order, doc_lengths, sizes):
    peers, half, groups, share, dim, docs = sizes
    tokens, width = 2 * half, groups * dim
    columns = share * half
    terms = jax.ShapeDtypeStruct((peers // 2, half, 2 * width), jnp.bfloat16)
    rests = jax.ShapeDtypeStruct((peers * half, 2 * width), jnp.float32)
    outs = [jax.ShapeDtypeStruct(g.shape, jnp.bfloat16), terms, terms] + [rests] * upper
    return pl.pallas_call(
        functools.partial(grads_body, sizes, upper),
        in_specs=[pl.BlockSpec(memory_space=pltpu.SMEM)] * 2
        + [pl.BlockSpec(memory_space=VMEM)] * (4 + len(rest) + peers),
        out_specs=[pl.BlockSpec(memory_space=VMEM)] * len(outs),
        out_shape=outs,
        scratch_shapes=[
            VMEM((peers * tokens, 2 * width), jnp.bfloat16),
            VMEM(((2 if upper else 1) * peers * half, 2 * width), jnp.float32),
            pltpu.SMEM((2 * peers,), jnp.int32),
        ],
        compiler_params=params(),
        cost_estimate=cost((12 if upper else 6) * peers * half * half * columns * groups, 8 * MIB),
        name="upper_grads" if upper else "lower_grads",
    )(span_order, doc_lengths, q, g, level, mixed, *rest, *blocks)


def swap(x, k, axis):
    return lax.ppermute(x, axis, [(i, i ^ k) for i in range(lax.axis_size(axis))])


def gather_ctx(x):
    even = [x] + [swap(x, k, "ctx") for k in range(2, lax.axis_size("ctx"), 2)]
    odd = [swap(block, 1, "ctx") for block in even]
    return [block for pair in zip(even, odd) for block in pair]


def gather_head(x):
    return [x] + [swap(x, k, "head") for k in range(1, lax.axis_size("head"))]


def pair_body(even_ref, odd_ref, *outs):
    for k, out in enumerate(outs):
        out[...] = (
            even_ref[k].astype(jnp.float32) + odd_ref[k].astype(jnp.float32)
        ).astype(out.dtype)


def scatter_ctx(even, odd):
    count, rows, width = even.shape
    got = swap(odd, 1, "ctx")
    pairs = pl.pallas_call(
        pair_body,
        in_specs=[pl.BlockSpec(memory_space=VMEM)] * 2,
        out_specs=[pl.BlockSpec(memory_space=VMEM)] * count,
        out_shape=[jax.ShapeDtypeStruct((rows, width), jnp.bfloat16)] * count,
        compiler_params=params(),
        cost_estimate=cost(even.size, 6 * even.size),
        name="pair_sums",
    )(even, got)
    return [pairs[0]] + [swap(pairs[k], 2 * k, "ctx") for k in range(1, count)]


def shards(inputs, out_grad, w_query, w_key, value_projection, w_out, doc_lengths, span_order):
    tokens = inputs.shape[0]
    share = ASKER_NUM // SHARED_KV_NUM
    sizes = (
        lax.axis_size("ctx"),
        tokens // 2,
        w_key.shape[1] // CHANNEL_DIM,
        share,
        CHANNEL_DIM,
        doc_lengths.shape[0],
    )
    heads = lax.axis_size("head")

    def scatter_head(query_grad, even, odd):
        first = [query_terms(query_grad, w_query, heads, k) for k in range(heads)]
        terms = scatter_ctx(even, odd)
        got = []
        for k in list(range(1, heads)) + [0]:
            part = all_terms(first[k], terms, w_key, value_projection, k)
            got.append(swap(part, k, "head") if k else part)
        return got, part

    upper_out, lower_out = split_rows(out_grad, span_order)
    upper_out = gather_head(upper_out)
    own = project_kv(inputs, w_key, value_projection)
    blocks = gather_ctx(own)
    query = project(inputs, w_query)
    level, mixed = stats(query, blocks, span_order, doc_lengths, sizes)
    upper_out, lower_out = lax.optimization_barrier((upper_out, lower_out))
    context_grad = back_project(upper_out, w_out)
    lower_out = gather_head(lower_out)
    query_grad, even, odd, rest = grads(
        True, query, context_grad, level, mixed, (), blocks, span_order, doc_lengths, sizes
    )
    upper, last = scatter_head(query_grad, even, odd)
    lower_out, last = lax.optimization_barrier((lower_out, last))
    upper[-1] = last
    context_grad = back_project(lower_out, w_out)
    query_grad, even, odd = grads(
        False, query, context_grad, level, mixed, (rest,), blocks, span_order, doc_lengths, sizes
    )
    lower, last = scatter_head(query_grad, even, odd)
    return join_rows(upper, lower, span_order)


def solution(mesh):
    in_specs = (
        P("ctx", None),
        P("ctx", "head"),
        P(None, "head"),
        P(None, "head"),
        P(None, "head"),
        P("head", None),
        P(),
        P(),
    )
    out_specs = P("ctx", "head")
    return jax.shard_map(shards, mesh=mesh, in_specs=in_specs, out_specs=out_specs, check_vma=False)
```

```python
import functools
import math

import jax
import jax.numpy as jnp
from jax import lax
from jax.experimental import pallas as pl
from jax.experimental.pallas import tpu as pltpu
from jax.sharding import PartitionSpec as P

ASKER_NUM = 32
SHARED_KV_NUM = 8
CHANNEL_DIM = 128

masked_score = -1e30
MIB = 1 << 20
VMEM = pltpu.VMEM
HBM = pltpu.HBM


def mm(a, b):
    return lax.dot_general(a, b, (((1,), (0,)), ((), ())), preferred_element_type=jnp.float32)


def mm_nt(a, b):
    return lax.dot_general(a, b, (((1,), (1,)), ((), ())), preferred_element_type=jnp.float32)


def mm_tn(a, b):
    return lax.dot_general(a, b, (((0,), (0,)), ((), ())), preferred_element_type=jnp.float32)


def params():
    return pltpu.CompilerParams(vmem_limit_bytes=24 * MIB)


def cost():
    return pl.CostEstimate(flops=1, bytes_accessed=1, transcendentals=0)


def upper_half(order):
    first = order[2 * lax.axis_index("ctx")]
    return jnp.where(2 * first >= order.shape[0], 0, 1)


def in_hbm(x):
    return pltpu.with_memory_space_constraint(x, HBM)


def fetch(src, dst, sem):
    copy = pltpu.make_async_copy(src, dst, sem)
    copy.start()
    return copy


def kv_body(parts, x_ref, wk_ref, wv_ref, out_ref, x, wk, wv, acc, sems):
    width = wk.shape[1]
    depth = wk.shape[0] // parts
    copies = []
    for i in range(parts):
        rows = slice(i * depth, (i + 1) * depth)
        copies.append(
            [
                fetch(x_ref.at[:, rows], x.at[:, rows], sems.at[i, 0]),
                fetch(wk_ref.at[rows], wk.at[rows], sems.at[i, 1]),
                fetch(wv_ref.at[rows], wv.at[rows], sems.at[i, 2]),
            ]
        )
    for i in range(parts):
        rows = slice(i * depth, (i + 1) * depth)
        for copy in copies[i]:
            copy.wait()
        left = x[:, rows]
        terms = mm(left, wk[rows, :]), mm(left, wv[rows, :])
        for j, term in enumerate(terms):
            columns = slice(j * width, (j + 1) * width)
            total = term if i == 0 else acc[:, columns] + term
            if i < parts - 1:
                acc[:, columns] = total
            else:
                out_ref[:, columns] = total.astype(out_ref.dtype)


def project_kv(x, wk, wv):
    tokens, depth = x.shape
    width = wk.shape[1]
    parts = 4
    return pl.pallas_call(
        functools.partial(kv_body, parts),
        in_specs=[pl.BlockSpec(memory_space=HBM)] * 3,
        out_specs=pl.BlockSpec(memory_space=VMEM),
        out_shape=jax.ShapeDtypeStruct((tokens, 2 * width), jnp.bfloat16),
        scratch_shapes=[
            VMEM(x.shape, x.dtype),
            VMEM(wk.shape, wk.dtype),
            VMEM(wv.shape, wv.dtype),
            VMEM((tokens, 2 * width), jnp.float32),
            pltpu.SemaphoreType.DMA((parts, 3)),
        ],
        compiler_params=params(),
        cost_estimate=cost(),
        name="project_kv",
    )(in_hbm(x), in_hbm(wk), in_hbm(wv))


def project_body(parts, x_ref, w_ref, out_ref, x, w, acc, sems):
    depth = w.shape[0] // parts
    copies = []
    for i in range(parts):
        rows = slice(i * depth, (i + 1) * depth)
        copies.append(
            [
                fetch(x_ref.at[:, rows], x.at[:, rows], sems.at[i, 0]),
                fetch(w_ref.at[rows], w.at[rows], sems.at[i, 1]),
            ]
        )
    for i in range(parts):
        rows = slice(i * depth, (i + 1) * depth)
        for copy in copies[i]:
            copy.wait()
        total = mm(x[:, rows], w[rows, :])
        if i:
            total = acc[...] + total
        if i < parts - 1:
            acc[...] = total
        else:
            out_ref[...] = total.astype(out_ref.dtype)


def project(x, w):
    tokens, depth = x.shape
    width = w.shape[1]
    parts = 4
    return pl.pallas_call(
        functools.partial(project_body, parts),
        in_specs=[pl.BlockSpec(memory_space=HBM)] * 2,
        out_specs=pl.BlockSpec(memory_space=VMEM),
        out_shape=jax.ShapeDtypeStruct((tokens, width), jnp.bfloat16),
        scratch_shapes=[
            VMEM(x.shape, x.dtype),
            VMEM(w.shape, w.dtype),
            VMEM((tokens, width), jnp.float32),
            pltpu.SemaphoreType.DMA((parts, 2)),
        ],
        compiler_params=params(),
        cost_estimate=cost(),
        name="project",
    )(in_hbm(x), in_hbm(w))


def back_body(places, given, rows, *refs):
    refs = list(refs)
    sems, w = refs.pop(), refs.pop()
    out_ref, w_ref = refs.pop(), refs.pop()
    me = lax.axis_index("head")
    depth = w.shape[2]
    copies = [
        fetch(w_ref.at[:, pl.ds(pl.multiple_of((me ^ k) * depth, depth), depth)], w.at[i], sems.at[i])
        for i, k in enumerate(places)
    ]
    total = refs.pop(0)[...] if given else None
    for i, copy in enumerate(copies):
        x = refs.pop(0)[...]
        if x.shape[0] < rows:
            x = jnp.concatenate([x, refs.pop(0)[...]], axis=0)
        copy.wait()
        term = mm_nt(x, w[i])
        total = term if total is None else total + term
    out_ref[...] = total.astype(out_ref.dtype)


def back_project(blocks, places, w, total, dtype):
    rows, depth = blocks[0][0].shape[0] * len(blocks[0]), blocks[0][0].shape[1]
    given = [] if total is None else [total]
    flat = [x for block in blocks for x in block]
    return pl.pallas_call(
        functools.partial(back_body, places, len(given), rows),
        in_specs=[pl.BlockSpec(memory_space=VMEM)] * (len(given) + len(flat))
        + [pl.BlockSpec(memory_space=HBM)],
        out_specs=pl.BlockSpec(memory_space=VMEM),
        out_shape=jax.ShapeDtypeStruct((rows, w.shape[0]), dtype),
        scratch_shapes=[
            VMEM((len(places), w.shape[0], depth), w.dtype),
            pltpu.SemaphoreType.DMA((len(places),)),
        ],
        compiler_params=params(),
        cost_estimate=cost(),
        name="context_grad",
    )(*given, *flat, in_hbm(w))


def query_terms_body(upper_ref, lower_ref, w_ref, upper_out, lower_out, w, sems):
    me = lax.axis_index("head")
    size, share = w.shape[:2]
    copies = [
        fetch(w_ref.at[pl.ds(pl.multiple_of((me ^ k) * share, share), share)], w.at[k], sems.at[k])
        for k in range(size)
    ]
    half = upper_ref.shape[0]
    x = jnp.concatenate([upper_ref[...], lower_ref[...]], axis=0)
    for k, copy in enumerate(copies):
        copy.wait()
        total = mm_nt(x, w[k])
        upper_out[k] = total[:half]
        lower_out[k] = total[half:]


def query_terms(upper, lower, w, size):
    rows, depth = upper.shape
    share = w.shape[0] // size
    return pl.pallas_call(
        query_terms_body,
        in_specs=[pl.BlockSpec(memory_space=VMEM)] * 2 + [pl.BlockSpec(memory_space=HBM)],
        out_specs=[pl.BlockSpec(memory_space=VMEM)] * 2,
        out_shape=[jax.ShapeDtypeStruct((size, rows, share), jnp.float32)] * 2,
        scratch_shapes=[
            VMEM((size, share, depth), w.dtype),
            pltpu.SemaphoreType.DMA((size,)),
        ],
        compiler_params=params(),
        cost_estimate=cost(),
        name="query_terms",
    )(upper, lower, in_hbm(w))


def all_terms_body(count, first_ref, *refs):
    terms, (wk_ref, wv_ref), refs = refs[:count], refs[count : count + 2], refs[count + 2 :]
    outs, (wk, wv, sems) = refs[:-3], refs[-3:]
    me = lax.axis_index("head")
    size, share, width = wk.shape
    copies = {}
    for k in range(size - 1, -1, -1):
        rows = pl.ds(pl.multiple_of((me ^ k) * share, share), share)
        copies[k] = [
            fetch(wk_ref.at[rows], wk.at[k], sems.at[k, 0]),
            fetch(wv_ref.at[rows], wv.at[k], sems.at[k, 1]),
        ]
    grads = terms[0][...].astype(jnp.float32)
    for term in terms[1:]:
        grads = grads + term[...].astype(jnp.float32)
    grads = grads.astype(jnp.bfloat16)
    for k, pair in copies.items():
        for copy in pair:
            copy.wait()
        total = first_ref[k] + mm_nt(grads[:, :width], wk[k])
        total = total + mm_nt(grads[:, width:], wv[k])
        outs[k][...] = total.astype(outs[k].dtype)


def all_terms(first, terms, wk, wv):
    size, rows, share = first.shape
    width = wk.shape[1]
    return pl.pallas_call(
        functools.partial(all_terms_body, len(terms)),
        in_specs=[pl.BlockSpec(memory_space=VMEM)] * (1 + len(terms))
        + [pl.BlockSpec(memory_space=HBM)] * 2,
        out_specs=[pl.BlockSpec(memory_space=VMEM)] * size,
        out_shape=[jax.ShapeDtypeStruct((rows, share), jnp.bfloat16)] * size,
        scratch_shapes=[
            VMEM((size, share, width), wk.dtype),
            VMEM((size, share, width), wv.dtype),
            pltpu.SemaphoreType.DMA((size, 2)),
        ],
        compiler_params=params(),
        cost_estimate=cost(),
        name="all_terms",
    )(first, *terms, in_hbm(wk), in_hbm(wv))


def add_body(a_ref, b_ref, out_ref):
    total = a_ref[...].astype(jnp.float32) + b_ref[...].astype(jnp.float32)
    out_ref[...] = total.astype(out_ref.dtype)


def add(a, b):
    return pl.pallas_call(
        add_body,
        in_specs=[pl.BlockSpec(memory_space=VMEM)] * 2,
        out_specs=pl.BlockSpec(memory_space=VMEM),
        out_shape=jax.ShapeDtypeStruct(a.shape, a.dtype),
        compiler_params=params(),
        cost_estimate=cost(),
        name="add",
    )(a, b)


def join_body(count, order, *refs):
    out_ref = refs[-1]
    half = refs[0].shape[0]
    at = upper_half(order) * half
    for j, place in enumerate((at, half - at)):
        total = refs[j * count][...].astype(jnp.float32)
        for ref in refs[j * count + 1 : (j + 1) * count]:
            total = total + ref[...].astype(jnp.float32)
        out_ref[pl.ds(pl.multiple_of(place, half), half), :] = total.astype(out_ref.dtype)


def join_rows(upper, lower, span_order):
    rows, width = upper[0].shape
    return pl.pallas_call(
        functools.partial(join_body, len(upper)),
        in_specs=[pl.BlockSpec(memory_space=pltpu.SMEM)]
        + [pl.BlockSpec(memory_space=VMEM)] * (2 * len(upper)),
        out_specs=pl.BlockSpec(memory_space=VMEM),
        out_shape=jax.ShapeDtypeStruct((2 * rows, width), jnp.bfloat16),
        compiler_params=params(),
        cost_estimate=cost(),
        name="join_rows",
    )(span_order, *upper, *lower)


def find_places(order, places, me, spans):
    for i in range(spans):
        places[order[i]] = ((i // 2) ^ me) * 2 + (i % 2)


def own_span(order, lengths, docs, me, j, half):
    span = order[2 * me + j]
    position = span * half + lax.broadcasted_iota(jnp.int32, (1, half), 1)
    first, end = 0, 0
    start = jnp.zeros((1, half), jnp.int32)
    for k in range(docs):
        end = end + lengths[k]
        start = jnp.where(position >= end, end, start)
        first = jnp.where(span * half >= end, end, first)
    return span, position, start, first // half


def stack_heads(ref, rows, group, share, dim):
    base = group * share
    return jnp.concatenate(
        [ref[rows, (base + h) * dim : (base + h + 1) * dim] for h in range(share)], axis=0
    )


def load_blocks(refs, held):
    rows = refs[0].shape[0]
    for k, ref in enumerate(refs):
        held[k * rows : (k + 1) * rows, :] = ref[...]


def allowed_of(p, position, start, half, share):
    key = p * half + lax.broadcasted_iota(jnp.int32, (half, 1), 0)
    allowed = (key <= position) & (key >= start)
    return jnp.concatenate([allowed] * share, axis=1)


def stats_body(sizes, upper, order, lengths, q_ref, *refs):
    peers, half, groups, share, dim, docs = sizes
    blocks = refs[:peers]
    level_ref, mixed_ref, held, places = refs[peers:]
    me = lax.axis_index("ctx")
    width = groups * dim
    factor = math.log2(math.e) / math.sqrt(dim)
    find_places(order, places, me, 2 * peers)
    load_blocks(blocks, held)
    columns = share * half
    at = upper_half(order)
    j = at if upper else 1 - at
    span, position, start, lowest = own_span(order, lengths, docs, me, j, half)
    rows = pl.ds(pl.multiple_of(j * half, half), half)
    queries = [stack_heads(q_ref, rows, g, share, dim) for g in range(groups)]

    def visit(p, carry):
        place = pl.multiple_of(places[p] * half, half)
        allowed = allowed_of(p, position, start, half, share)
        fresh = []
        for g in range(groups):
            top, total, mixed = carry[g]
            keys = held[pl.ds(place, half), g * dim : (g + 1) * dim]
            values = held[pl.ds(place, half), width + g * dim : width + (g + 1) * dim]
            logits = mm_nt(keys, queries[g]) * factor
            logits = jnp.where(allowed, logits, masked_score)
            higher = jnp.maximum(top, jnp.max(logits, axis=0, keepdims=True))
            weights = jnp.where(allowed, jnp.exp2(logits - higher), 0.0)
            fade = jnp.exp2(top - higher)
            total = total * fade + jnp.sum(weights, axis=0, keepdims=True)
            mixed = mixed * fade + mm_tn(values, weights.astype(jnp.bfloat16))
            fresh.append((higher, total, mixed))
        return tuple(fresh)

    empty = (
        jnp.full((1, columns), masked_score, jnp.float32),
        jnp.zeros((1, columns), jnp.float32),
        jnp.zeros((dim, columns), jnp.float32),
    )
    done = lax.fori_loop(lowest, span + 1, visit, (empty,) * groups)
    for g in range(groups):
        top, total, mixed = done[g]
        level_ref[g] = top + jnp.log2(total)
        mixed_ref[g] = mixed / total


def stats(upper, q, *args):
    *blocks, span_order, doc_lengths, sizes = args
    peers, half, groups, share, dim, docs = sizes
    columns = share * half
    return pl.pallas_call(
        functools.partial(stats_body, sizes, upper),
        in_specs=[pl.BlockSpec(memory_space=pltpu.SMEM)] * 2
        + [pl.BlockSpec(memory_space=VMEM)] * (1 + peers),
        out_specs=[pl.BlockSpec(memory_space=VMEM)] * 2,
        out_shape=[
            jax.ShapeDtypeStruct((groups, 1, columns), jnp.float32),
            jax.ShapeDtypeStruct((groups, dim, columns), jnp.float32),
        ],
        scratch_shapes=[
            VMEM((2 * peers * half, 2 * groups * dim), jnp.bfloat16),
            pltpu.SMEM((2 * peers,), jnp.int32),
        ],
        compiler_params=params(),
        cost_estimate=cost(),
        name="upper_stats" if upper else "lower_stats",
    )(span_order, doc_lengths, q, *blocks)


def grads_body(sizes, upper, order, lengths, q_ref, g_ref, level_ref, mixed_ref, *refs):
    peers, half, groups, share, dim, docs = sizes
    spans = 2 * peers
    if upper:
        blocks = refs[:peers]
        dq_ref, even_ref, odd_ref, rest_ref, held, sums, places = refs[peers:]
    else:
        rest_ref, blocks = refs[0], refs[1 : 1 + peers]
        dq_ref, even_ref, odd_ref, held, sums, places = refs[1 + peers :]
    me = lax.axis_index("ctx")
    width = groups * dim
    scale = 1.0 / math.sqrt(dim)
    factor = math.log2(math.e) * scale
    find_places(order, places, me, spans)
    load_blocks(blocks, held)
    columns = share * half
    at = upper_half(order)
    j = at if upper else 1 - at
    span, position, start, lowest = own_span(order, lengths, docs, me, j, half)
    if upper:
        sums[...] = jnp.zeros_like(sums)
    else:
        sums[...] = rest_ref[...]
    rows = pl.ds(pl.multiple_of(j * half, half), half)
    queries = [stack_heads(q_ref, rows, g, share, dim) for g in range(groups)]
    outs = [stack_heads(g_ref, rows, g, share, dim) for g in range(groups)]
    levels = [level_ref[g] for g in range(groups)]
    deltas = []
    for g in range(groups):
        turned = jnp.concatenate(
            [outs[g][h * half : (h + 1) * half].astype(jnp.float32).T for h in range(share)],
            axis=1,
        )
        deltas.append(jnp.sum(turned * mixed_ref[g], axis=0, keepdims=True))

    def visit(p, carry):
        place = pl.multiple_of(places[p] * half, half)
        target = pl.ds(pl.multiple_of(p * half, half), half)
        allowed = allowed_of(p, position, start, half, share)
        fresh = []
        for g in range(groups):
            keys = held[pl.ds(place, half), g * dim : (g + 1) * dim]
            values = held[pl.ds(place, half), width + g * dim : width + (g + 1) * dim]
            logits = mm_nt(keys, queries[g]) * factor
            chance = jnp.where(allowed, jnp.exp2(logits - levels[g]), 0.0)
            slopes = mm_nt(values, outs[g])
            score = (chance * (slopes - deltas[g])).astype(jnp.bfloat16)
            sums[target, g * dim : (g + 1) * dim] += mm(score, queries[g])
            sums[target, width + g * dim : width + (g + 1) * dim] += mm(
                chance.astype(jnp.bfloat16), outs[g]
            )
            fresh.append(carry[g] + mm_tn(keys, score))
        return tuple(fresh)

    empty = jnp.zeros((dim, columns), jnp.float32)
    done = lax.fori_loop(lowest, span + 1, visit, (empty,) * groups)
    for g in range(groups):
        for h in range(share):
            head = g * share + h
            dq_ref[:, head * dim : (head + 1) * dim] = (
                (done[g][:, h * half : (h + 1) * half].T * scale).astype(dq_ref.dtype)
            )
    for k in range(peers):
        out, slot = (even_ref, odd_ref)[k % 2], k // 2
        first = order[2 * (me ^ k)]
        other = spans - 1 - first
        pick = jnp.maximum(first, other) if upper else jnp.minimum(first, other)
        part = pl.ds(pl.multiple_of(pick * half, half), half)
        out[slot, :, :width] = (sums[part, :width] * scale).astype(out.dtype)
        out[slot, :, width:] = sums[part, width:].astype(out.dtype)
    if upper:
        rest_ref[...] = sums[: peers * half, :]


def grads(upper, q, g, level, mixed, *args):
    *blocks, span_order, doc_lengths, sizes = args
    peers, half, groups, share, dim, docs = sizes
    tokens, width = 2 * half, groups * dim
    columns = share * half
    terms = jax.ShapeDtypeStruct((peers // 2, half, 2 * width), jnp.bfloat16)
    rests = jax.ShapeDtypeStruct((peers * half, 2 * width), jnp.float32)
    outs = [jax.ShapeDtypeStruct((half, g.shape[1]), jnp.bfloat16), terms, terms] + [rests] * upper
    return pl.pallas_call(
        functools.partial(grads_body, sizes, upper),
        in_specs=[pl.BlockSpec(memory_space=pltpu.SMEM)] * 2
        + [pl.BlockSpec(memory_space=VMEM)] * (4 + len(blocks)),
        out_specs=[pl.BlockSpec(memory_space=VMEM)] * len(outs),
        out_shape=outs,
        scratch_shapes=[
            VMEM((peers * tokens, 2 * width), jnp.bfloat16),
            VMEM(((2 if upper else 1) * peers * half, 2 * width), jnp.float32),
            pltpu.SMEM((2 * peers,), jnp.int32),
        ],
        compiler_params=params(),
        cost_estimate=cost(),
        name="upper_grads" if upper else "lower_grads",
    )(span_order, doc_lengths, q, g, level, mixed, *blocks)


def swap(x, k, axis):
    return lax.ppermute(x, axis, [(i, i ^ k) for i in range(lax.axis_size(axis))])


def gather(x, axis):
    got, bit = {0: x}, lax.axis_size(axis) // 2
    while bit:
        got |= {k ^ bit: swap(block, bit, axis) for k, block in got.items()}
        bit //= 2
    return [got[k] for k in range(len(got))]


def pair_body(even_ref, odd_ref, *outs):
    for k, out in enumerate(outs):
        out[...] = (
            even_ref[k].astype(jnp.float32) + odd_ref[k].astype(jnp.float32)
        ).astype(out.dtype)


def pair_sums(even, got):
    count, rows, width = even.shape
    return pl.pallas_call(
        pair_body,
        in_specs=[pl.BlockSpec(memory_space=VMEM)] * 2,
        out_specs=[pl.BlockSpec(memory_space=VMEM)] * count,
        out_shape=[jax.ShapeDtypeStruct((rows, width), jnp.bfloat16)] * count,
        compiler_params=params(),
        cost_estimate=cost(),
        name="pair_sums",
    )(even, got)


def scatter_ctx(pairs):
    return [part if k == 0 else swap(part, 2 * k, "ctx") for k, part in enumerate(pairs)]


def shards(inputs, out_grad, w_query, w_key, value_projection, w_out, doc_lengths, span_order):
    tokens = inputs.shape[0]
    share = ASKER_NUM // SHARED_KV_NUM
    half = tokens // 2
    sizes = (
        lax.axis_size("ctx"),
        tokens // 2,
        w_key.shape[1] // CHANNEL_DIM,
        share,
        CHANNEL_DIM,
        doc_lengths.shape[0],
    )
    heads = lax.axis_size("head")
    last = [span_order]

    def turn(call, *args):
        held, *args = lax.optimization_barrier((last[0], *args))
        out = call(*args)
        last[0] = out if hasattr(out, "shape") else out[0]
        return out

    def attend(upper, call, *args):
        return turn(lambda *a: call(upper, *a, span_order, doc_lengths, sizes), *args)

    def context(blocks, places, total, dtype):
        shape = jax.tree.structure((blocks, total))

        def call(*flat):
            parts, given = jax.tree.unflatten(shape, flat)
            return back_project(parts, places, w_out, given, dtype)

        return turn(call, *jax.tree.leaves((blocks, total)))

    def send_first(parts):
        return {k ^ 1: swap(parts[k], 1, "head") for k in range(heads - 1, 0, -2)}

    def send_rest(parts, got):
        ends, bit = [parts[0], got[0]], 2
        parts = {k: turn(add, parts[k], got[k]) for k in range(2, heads, 2)}
        while bit < heads:
            moved = {k ^ bit: swap(parts[k], bit, "head") for k in parts if k & bit}
            ends.append(moved.pop(0))
            parts = {k: turn(add, parts[k], moved[k]) for k in moved}
            bit *= 2
        return ends

    far = [{0: out_grad[:half]}, {0: out_grad[half:]}]
    bit = heads // 2
    while bit > 1:
        far = [got | {k ^ bit: swap(x, bit, "head") for k, x in got.items()} for got in far]
        bit //= 2
    near = swap(out_grad, 1, "head")
    own = turn(project_kv, inputs, w_key, value_projection)
    blocks = gather(own, "ctx")
    query = turn(project, inputs, w_query)
    passed = [{k ^ 1: swap(x, 1, "head") for k, x in got.items() if k} for got in far]
    firsts = {0: (out_grad,), 1: (near,)}
    firsts |= {k: (far[0][k], far[1][k]) for k in range(2, heads, 2)}
    lasts = {k: (passed[0][k], passed[1][k]) for k in range(3, heads, 2)}
    upper_stats = attend(True, stats, query, *blocks)
    total = context(list(firsts.values()), list(firsts), None, jnp.float32)
    context_grad = context(list(lasts.values()), list(lasts), total, jnp.bfloat16)
    upper_dq, even, odd, rest = attend(True, grads, query, context_grad, *upper_stats, *blocks)
    upper_odd = swap(odd, 1, "ctx")
    lower_stats = attend(False, stats, query, *blocks)
    upper = scatter_ctx(turn(pair_sums, even, upper_odd))
    lower_dq, even, odd = attend(
        False, grads, query, context_grad, *lower_stats, rest, *blocks
    )
    lower_odd = swap(odd, 1, "ctx")
    first = turn(lambda a, b: query_terms(a, b, w_query, heads), upper_dq, lower_dq)
    pairs = turn(pair_sums, even, lower_odd)
    upper = turn(lambda a, *b: all_terms(a, b, w_key, value_projection), first[0], *upper)
    upper_got = send_first(upper)
    lower = scatter_ctx(pairs)
    lower = turn(lambda a, *b: all_terms(a, b, w_key, value_projection), first[1], *lower)
    upper = send_rest(upper, upper_got)
    lower = send_rest(lower, send_first(lower))
    return join_rows(upper, lower, span_order)


def solution(mesh):
    in_specs = (
        P("ctx", None),
        P("ctx", "head"),
        P(None, "head"),
        P(None, "head"),
        P(None, "head"),
        P("head", None),
        P(),
        P(),
    )
    out_specs = P("ctx", "head")
    return jax.shard_map(shards, mesh=mesh, in_specs=in_specs, out_specs=out_specs, check_vma=False)
```

```python
import functools
import math

import jax
import jax.numpy as jnp
from jax import lax
from jax.experimental import pallas as pl
from jax.experimental.pallas import tpu as pltpu
from jax.sharding import PartitionSpec as P

ASKER_NUM = 32
SHARED_KV_NUM = 8
CHANNEL_DIM = 128

masked_score = -1e30
MIB = 1 << 20
COST = 0
AT_ONCE = 4
VMEM = pltpu.VMEM
HBM = pltpu.HBM


def mm(a, b):
    return lax.dot_general(a, b, (((1,), (0,)), ((), ())), preferred_element_type=jnp.float32)


def mm_nt(a, b):
    return lax.dot_general(a, b, (((1,), (1,)), ((), ())), preferred_element_type=jnp.float32)


def mm_tn(a, b):
    return lax.dot_general(a, b, (((0,), (0,)), ((), ())), preferred_element_type=jnp.float32)


def params():
    return pltpu.CompilerParams(vmem_limit_bytes=24 * MIB)


def cost(micros):
    return pl.CostEstimate(flops=int(micros * COST), bytes_accessed=1, transcendentals=0)


def upper_half(order):
    first = order[2 * lax.axis_index("ctx")]
    return jnp.where(2 * first >= order.shape[0], 0, 1)


def in_hbm(x):
    return pltpu.with_memory_space_constraint(x, HBM)


def fetch(src, dst, sem):
    copy = pltpu.make_async_copy(src, dst, sem)
    copy.start()
    return copy


def kv_body(parts, x_ref, wk_ref, wv_ref, out_ref, x, wk, wv, acc, sems):
    width = wk.shape[1]
    depth = wk.shape[0] // parts
    copies = []
    for i in range(parts):
        rows = slice(i * depth, (i + 1) * depth)
        copies.append(
            [
                fetch(x_ref.at[:, rows], x.at[:, rows], sems.at[i, 0]),
                fetch(wk_ref.at[rows], wk.at[rows], sems.at[i, 1]),
                fetch(wv_ref.at[rows], wv.at[rows], sems.at[i, 2]),
            ]
        )
    for i in range(parts):
        rows = slice(i * depth, (i + 1) * depth)
        for copy in copies[i]:
            copy.wait()
        left = x[:, rows]
        terms = mm(left, wk[rows, :]), mm(left, wv[rows, :])
        for j, term in enumerate(terms):
            columns = slice(j * width, (j + 1) * width)
            total = term if i == 0 else acc[:, columns] + term
            if i < parts - 1:
                acc[:, columns] = total
            else:
                out_ref[:, columns] = total.astype(out_ref.dtype)


def project_kv(x, wk, wv):
    tokens, depth = x.shape
    width = wk.shape[1]
    parts = 4
    return pl.pallas_call(
        functools.partial(kv_body, parts),
        in_specs=[pl.BlockSpec(memory_space=HBM)] * 3,
        out_specs=pl.BlockSpec(memory_space=VMEM),
        out_shape=jax.ShapeDtypeStruct((tokens, 2 * width), jnp.bfloat16),
        scratch_shapes=[
            VMEM(x.shape, x.dtype),
            VMEM(wk.shape, wk.dtype),
            VMEM(wv.shape, wv.dtype),
            VMEM((tokens, 2 * width), jnp.float32),
            pltpu.SemaphoreType.DMA((parts, 3)),
        ],
        compiler_params=params(),
        cost_estimate=cost(3.4),
        name="project_kv",
    )(in_hbm(x), in_hbm(wk), in_hbm(wv))


def project_body(parts, x_ref, w_ref, out_ref, x, w, acc, sems):
    depth = w.shape[0] // parts
    copies = []
    for i in range(parts):
        rows = slice(i * depth, (i + 1) * depth)
        copies.append(
            [
                fetch(x_ref.at[:, rows], x.at[:, rows], sems.at[i, 0]),
                fetch(w_ref.at[rows], w.at[rows], sems.at[i, 1]),
            ]
        )
    for i in range(parts):
        rows = slice(i * depth, (i + 1) * depth)
        for copy in copies[i]:
            copy.wait()
        total = mm(x[:, rows], w[rows, :])
        if i:
            total = acc[...] + total
        if i < parts - 1:
            acc[...] = total
        else:
            out_ref[...] = total.astype(out_ref.dtype)


def project(x, w):
    tokens, depth = x.shape
    width = w.shape[1]
    parts = 4
    return pl.pallas_call(
        functools.partial(project_body, parts),
        in_specs=[pl.BlockSpec(memory_space=HBM)] * 2,
        out_specs=pl.BlockSpec(memory_space=VMEM),
        out_shape=jax.ShapeDtypeStruct((tokens, width), jnp.bfloat16),
        scratch_shapes=[
            VMEM(x.shape, x.dtype),
            VMEM(w.shape, w.dtype),
            VMEM((tokens, width), jnp.float32),
            pltpu.SemaphoreType.DMA((parts, 2)),
        ],
        compiler_params=params(),
        cost_estimate=cost(4.9),
        name="project",
    )(in_hbm(x), in_hbm(w))


def back_body(places, given, rows, *refs):
    refs = list(refs)
    sems, w = refs.pop(), refs.pop()
    out_ref, w_ref = refs.pop(), refs.pop()
    me = lax.axis_index("head")
    depth = w.shape[2]
    copies = [
        fetch(w_ref.at[:, pl.ds(pl.multiple_of((me ^ k) * depth, depth), depth)], w.at[i], sems.at[i])
        for i, k in enumerate(places)
    ]
    total = refs.pop(0)[...] if given else None
    for i, copy in enumerate(copies):
        x = refs.pop(0)[...]
        if x.shape[0] < rows:
            x = jnp.concatenate([x, refs.pop(0)[...]], axis=0)
        copy.wait()
        term = mm_nt(x, w[i])
        total = term if total is None else total + term
    out_ref[...] = total.astype(out_ref.dtype)


def back_project(blocks, places, w, total, dtype):
    rows, depth = blocks[0][0].shape[0] * len(blocks[0]), blocks[0][0].shape[1]
    given = [] if total is None else [total]
    flat = [x for block in blocks for x in block]
    return pl.pallas_call(
        functools.partial(back_body, places, len(given), rows),
        in_specs=[pl.BlockSpec(memory_space=VMEM)] * (len(given) + len(flat))
        + [pl.BlockSpec(memory_space=HBM)],
        out_specs=pl.BlockSpec(memory_space=VMEM),
        out_shape=jax.ShapeDtypeStruct((rows, w.shape[0]), dtype),
        scratch_shapes=[
            VMEM((len(places), w.shape[0], depth), w.dtype),
            pltpu.SemaphoreType.DMA((len(places),)),
        ],
        compiler_params=params(),
        cost_estimate=cost(3.4),
        name="context_grad",
    )(*given, *flat, in_hbm(w))


def query_terms_body(places, upper_ref, lower_ref, w_ref, upper_out, lower_out, w, sems):
    me = lax.axis_index("head")
    share = w.shape[1]
    copies = [
        fetch(w_ref.at[pl.ds(pl.multiple_of((me ^ k) * share, share), share)], w.at[i], sems.at[i])
        for i, k in enumerate(places)
    ]
    half = upper_ref.shape[0]
    x = jnp.concatenate([upper_ref[...], lower_ref[...]], axis=0)
    for i, copy in enumerate(copies):
        copy.wait()
        total = mm_nt(x, w[i])
        upper_out[i] = total[:half]
        lower_out[i] = total[half:]


def query_terms(upper, lower, w, heads, places):
    rows, depth = upper.shape
    share = w.shape[0] // heads
    size = len(places)
    return pl.pallas_call(
        functools.partial(query_terms_body, places),
        in_specs=[pl.BlockSpec(memory_space=VMEM)] * 2 + [pl.BlockSpec(memory_space=HBM)],
        out_specs=[pl.BlockSpec(memory_space=VMEM)] * 2,
        out_shape=[jax.ShapeDtypeStruct((size, rows, share), jnp.float32)] * 2,
        scratch_shapes=[
            VMEM((size, share, depth), w.dtype),
            pltpu.SemaphoreType.DMA((size,)),
        ],
        compiler_params=params(),
        cost_estimate=cost(4.6),
        name="query_terms",
    )(upper, lower, in_hbm(w))


def all_terms_body(places, count, first_ref, *refs):
    terms, (wk_ref, wv_ref), refs = refs[:count], refs[count : count + 2], refs[count + 2 :]
    outs, (wk, wv, sems) = refs[:-3], refs[-3:]
    me = lax.axis_index("head")
    size, share, width = wk.shape
    copies = {}
    for i, k in enumerate(places):
        rows = pl.ds(pl.multiple_of((me ^ k) * share, share), share)
        copies[i] = [
            fetch(wk_ref.at[rows], wk.at[i], sems.at[i, 0]),
            fetch(wv_ref.at[rows], wv.at[i], sems.at[i, 1]),
        ]
    grads = terms[0][...].astype(jnp.float32)
    for term in terms[1:]:
        grads = grads + term[...].astype(jnp.float32)
    grads = grads.astype(jnp.bfloat16)
    for i, pair in copies.items():
        for copy in pair:
            copy.wait()
        total = first_ref[i] + mm_nt(grads[:, :width], wk[i])
        total = total + mm_nt(grads[:, width:], wv[i])
        if len(outs) == 1:
            outs[0][i] = total.astype(outs[0].dtype)
        else:
            outs[i][...] = total.astype(outs[i].dtype)


def all_terms(first, terms, wk, wv, places, stacked):
    size, rows, share = first.shape
    width = wk.shape[1]
    return pl.pallas_call(
        functools.partial(all_terms_body, places, len(terms)),
        in_specs=[pl.BlockSpec(memory_space=VMEM)] * (1 + len(terms))
        + [pl.BlockSpec(memory_space=HBM)] * 2,
        out_specs=[pl.BlockSpec(memory_space=VMEM)] * (1 if stacked else size),
        out_shape=[jax.ShapeDtypeStruct((size, rows, share), jnp.bfloat16)]
        if stacked
        else [jax.ShapeDtypeStruct((rows, share), jnp.bfloat16)] * size,
        scratch_shapes=[
            VMEM((size, share, width), wk.dtype),
            VMEM((size, share, width), wv.dtype),
            pltpu.SemaphoreType.DMA((size, 2)),
        ],
        compiler_params=params(),
        cost_estimate=cost(3.2),
        name="all_terms",
    )(first, *terms, in_hbm(wk), in_hbm(wv))


def part_of(ref, at):
    return (ref[...] if at is None else ref[at]).astype(jnp.float32)


def add_body(at, a_ref, b_ref, out_ref):
    out_ref[...] = (a_ref[...].astype(jnp.float32) + part_of(b_ref, at)).astype(out_ref.dtype)


def add(a, b, at):
    return pl.pallas_call(
        functools.partial(add_body, at),
        in_specs=[pl.BlockSpec(memory_space=VMEM)] * 2,
        out_specs=pl.BlockSpec(memory_space=VMEM),
        out_shape=jax.ShapeDtypeStruct(a.shape, a.dtype),
        compiler_params=params(),
        cost_estimate=cost(0.5),
        name="add",
    )(a, b)


def join_body(ats, order, *refs):
    refs, out_ref = list(refs[:-1]), refs[-1]
    half = out_ref.shape[0] // 2
    at = upper_half(order) * half
    for j, place in enumerate((at, half - at)):
        total = None
        for i in ats[j]:
            term = part_of(refs.pop(0), i)
            total = term if total is None else total + term
        out_ref[pl.ds(pl.multiple_of(place, half), half), :] = total.astype(out_ref.dtype)


def join_rows(upper, lower, span_order):
    rows, width = upper[0][0].shape
    ats = [[at for _, at in terms] for terms in (upper, lower)]
    blocks = [block for block, _ in upper + lower]
    return pl.pallas_call(
        functools.partial(join_body, ats),
        in_specs=[pl.BlockSpec(memory_space=pltpu.SMEM)]
        + [pl.BlockSpec(memory_space=VMEM)] * len(blocks),
        out_specs=pl.BlockSpec(memory_space=VMEM),
        out_shape=jax.ShapeDtypeStruct((2 * rows, width), jnp.bfloat16),
        compiler_params=params(),
        cost_estimate=cost(1.5),
        name="join_rows",
    )(span_order, *blocks)


def find_places(order, places, me, spans):
    for i in range(spans):
        k = (i // 2) ^ me
        places[order[i]] = (k % 2) * (spans // 2) + (k // 2) * 2 + (i % 2)


def own_span(order, lengths, docs, me, j, half):
    span = order[2 * me + j]
    position = span * half + lax.broadcasted_iota(jnp.int32, (1, half), 1)
    first, end = 0, 0
    start = jnp.zeros((1, half), jnp.int32)
    for k in range(docs):
        end = end + lengths[k]
        start = jnp.where(position >= end, end, start)
        first = jnp.where(span * half >= end, end, first)
    return span, position, start, first // half


def stack_heads(ref, rows, group, share, dim):
    base = group * share
    return jnp.concatenate(
        [ref[rows, (base + h) * dim : (base + h + 1) * dim] for h in range(share)], axis=0
    )


def load_blocks(refs, held):
    rows = refs[0].shape[0]
    for k, ref in enumerate(refs):
        held[k * rows : (k + 1) * rows, :] = ref[...]


def span_group(i, span, held, places, half):
    numbers = [span - AT_ONCE * i - j for j in range(AT_ONCE - 1, -1, -1)]
    known = [jnp.maximum(p, 0) for p in numbers]
    at = [pl.multiple_of(places[p] * half, half) for p in known]
    block = jnp.concatenate([held[pl.ds(place, half), :] for place in at], axis=0)
    key = numbers[0] * half + lax.broadcasted_iota(jnp.int32, (AT_ONCE * half, 1), 0)
    return known, block, key


def keep(allowed, x, other):
    width = allowed.shape[1]
    return jnp.concatenate(
        [
            jnp.where(allowed, x[:, i : i + width], other)
            for i in range(0, x.shape[1], width)
        ],
        axis=1,
    )


def stats_body(sizes, upper, order, lengths, q_ref, *refs):
    peers, half, groups, share, dim, docs = sizes
    blocks = refs[:peers]
    level_ref, mixed_ref, held, kept, places = refs[peers:]
    me = lax.axis_index("ctx")
    width = groups * dim
    factor = math.log2(math.e) / math.sqrt(dim)
    find_places(order, places, me, 2 * peers)
    load_blocks(blocks, held)
    columns = share * half
    at = upper_half(order)
    j = at if upper else 1 - at
    span, position, start, lowest = own_span(order, lengths, docs, me, j, half)
    rows = pl.ds(pl.multiple_of(j * half, half), half)
    queries = [stack_heads(q_ref, rows, g, share, dim) for g in range(groups)]

    deep = AT_ONCE * half
    steps = (span - lowest) // AT_ONCE + 1

    def score(i, carry):
        known, block, key = span_group(i, span, held, places, half)
        allowed = (key <= position) & (key >= start)
        fresh = []
        for g in range(groups):
            logits = keep(allowed, mm_nt(block[:, g * dim : (g + 1) * dim], queries[g]), masked_score)
            kept[g, pl.ds(pl.multiple_of(i * deep, deep), deep), :] = logits
            high = jnp.max(logits.reshape(deep // 8, 8, columns), axis=0)
            fresh.append(jnp.maximum(carry[g], high))
        return tuple(fresh)

    empty = jnp.full((8, columns), masked_score, jnp.float32)
    tops = lax.fori_loop(0, steps, score, (empty,) * groups)
    tops = [jnp.max(top, axis=0, keepdims=True) for top in tops]

    def mix(i, carry):
        known, block, key = span_group(i, span, held, places, half)
        fresh = []
        for g in range(groups):
            total, mixed = carry[g]
            values = block[:, width + g * dim : width + (g + 1) * dim]
            logits = kept[g, pl.ds(pl.multiple_of(i * deep, deep), deep), :]
            weights = jnp.exp2((logits - tops[g]) * factor)
            total = total + jnp.sum(weights.reshape(deep // 8, 8, columns), axis=0)
            mixed = mixed + mm_tn(values, weights.astype(jnp.bfloat16))
            fresh.append((total, mixed))
        return tuple(fresh)

    empty = (jnp.zeros((8, columns), jnp.float32), jnp.zeros((dim, columns), jnp.float32))
    done = lax.fori_loop(0, steps, mix, (empty,) * groups)
    for g in range(groups):
        top, (total, mixed) = tops[g], done[g]
        total = jnp.sum(total, axis=0, keepdims=True)
        level_ref[g] = top * factor + jnp.log2(total)
        mixed_ref[g] = mixed / total


def stats(upper, q, *args):
    *blocks, span_order, doc_lengths, sizes = args
    peers, half, groups, share, dim, docs = sizes
    columns = share * half
    return pl.pallas_call(
        functools.partial(stats_body, sizes, upper),
        in_specs=[pl.BlockSpec(memory_space=pltpu.SMEM)] * 2
        + [pl.BlockSpec(memory_space=VMEM)] * (1 + peers),
        out_specs=[pl.BlockSpec(memory_space=VMEM)] * 2,
        out_shape=[
            jax.ShapeDtypeStruct((groups, 1, columns), jnp.float32),
            jax.ShapeDtypeStruct((groups, dim, columns), jnp.float32),
        ],
        scratch_shapes=[
            VMEM((2 * peers * half, 2 * groups * dim), jnp.bfloat16),
            VMEM((groups, (2 * peers + AT_ONCE) * half, columns), jnp.float32),
            pltpu.SMEM((2 * peers,), jnp.int32),
        ],
        compiler_params=params(),
        cost_estimate=cost(2.4),
        name="upper_stats" if upper else "lower_stats",
    )(span_order, doc_lengths, q, *blocks)


def grads_body(sizes, upper, order, lengths, q_ref, g_ref, level_ref, mixed_ref, *refs):
    peers, half, groups, share, dim, docs = sizes
    spans = 2 * peers
    if upper:
        blocks = refs[:peers]
        dq_ref, even_ref, *odd_refs, rest_ref, held, sums, places = refs[peers:]
    else:
        rest_ref, blocks = refs[0], refs[1 : 1 + peers]
        dq_ref, even_ref, *odd_refs, held, sums, places = refs[1 + peers :]
    me = lax.axis_index("ctx")
    width = groups * dim
    scale = 1.0 / math.sqrt(dim)
    factor = math.log2(math.e) * scale
    find_places(order, places, me, spans)
    load_blocks(blocks, held)
    columns = share * half
    at = upper_half(order)
    j = at if upper else 1 - at
    span, position, start, lowest = own_span(order, lengths, docs, me, j, half)
    if upper:
        sums[...] = jnp.zeros_like(sums)
    else:
        sums[...] = rest_ref[...]
    rows = pl.ds(pl.multiple_of(j * half, half), half)
    queries = [stack_heads(q_ref, rows, g, share, dim) for g in range(groups)]
    outs = [stack_heads(g_ref, rows, g, share, dim) for g in range(groups)]
    levels = [level_ref[g] for g in range(groups)]
    deltas = []
    for g in range(groups):
        turned = jnp.concatenate(
            [outs[g][h * half : (h + 1) * half].astype(jnp.float32).T for h in range(share)],
            axis=1,
        )
        deltas.append(jnp.sum(turned * mixed_ref[g], axis=0, keepdims=True))

    def visit(i, carry):
        known, block, key = span_group(i, span, held, places, half)
        allowed = (key <= position) & (key >= start)
        targets = [pl.ds(pl.multiple_of(p * half, half), half) for p in known]
        fresh = []
        for g in range(groups):
            keys = block[:, g * dim : (g + 1) * dim]
            values = block[:, width + g * dim : width + (g + 1) * dim]
            logits = mm_nt(keys, queries[g]) * factor
            chance = keep(allowed, jnp.exp2(logits - levels[g]), 0.0)
            slopes = mm_nt(values, outs[g])
            score = (chance * (slopes - deltas[g])).astype(jnp.bfloat16)
            key_term = mm(score, queries[g])
            value_term = mm(chance.astype(jnp.bfloat16), outs[g])
            for j, target in enumerate(targets):
                part = slice(j * half, (j + 1) * half)
                sums[target, g * dim : (g + 1) * dim] += key_term[part]
                sums[target, width + g * dim : width + (g + 1) * dim] += value_term[part]
            fresh.append(carry[g] + mm_tn(keys, score))
        return tuple(fresh)

    empty = jnp.zeros((dim, columns), jnp.float32)
    done = lax.fori_loop(0, (span - lowest) // AT_ONCE + 1, visit, (empty,) * groups)
    for g in range(groups):
        for h in range(share):
            head = g * share + h
            dq_ref[:, head * dim : (head + 1) * dim] = (
                (done[g][:, h * half : (h + 1) * half].T * scale).astype(dq_ref.dtype)
            )
    for k in range(peers):
        out, slot = even_ref, k // 2
        if k % 2:
            out, slot = odd_refs[slot // odd_refs[0].shape[0]], slot % odd_refs[0].shape[0]
        first = order[2 * (me ^ k)]
        other = spans - 1 - first
        pick = jnp.maximum(first, other) if upper else jnp.minimum(first, other)
        part = pl.ds(pl.multiple_of(pick * half, half), half)
        out[slot, :, :width] = (sums[part, :width] * scale).astype(out.dtype)
        out[slot, :, width:] = sums[part, width:].astype(out.dtype)
    if upper:
        rest_ref[...] = sums[: peers * half, :]


def grads(upper, q, g, level, mixed, *args):
    *blocks, span_order, doc_lengths, sizes = args
    peers, half, groups, share, dim, docs = sizes
    tokens, width = 2 * half, groups * dim
    columns = share * half
    terms = jax.ShapeDtypeStruct((peers // 2, half, 2 * width), jnp.bfloat16)
    odds = jax.ShapeDtypeStruct((peers // 4, half, 2 * width), jnp.bfloat16)
    rests = jax.ShapeDtypeStruct((peers * half, 2 * width), jnp.float32)
    outs = [jax.ShapeDtypeStruct((half, g.shape[1]), jnp.bfloat16), terms, odds, odds] + [rests] * upper
    return pl.pallas_call(
        functools.partial(grads_body, sizes, upper),
        in_specs=[pl.BlockSpec(memory_space=pltpu.SMEM)] * 2
        + [pl.BlockSpec(memory_space=VMEM)] * (4 + len(blocks)),
        out_specs=[pl.BlockSpec(memory_space=VMEM)] * len(outs),
        out_shape=outs,
        scratch_shapes=[
            VMEM((peers * tokens, 2 * width), jnp.bfloat16),
            VMEM(((2 if upper else 1) * peers * half, 2 * width), jnp.float32),
            pltpu.SMEM((2 * peers,), jnp.int32),
        ],
        compiler_params=params(),
        cost_estimate=cost(3.0),
        name="upper_grads" if upper else "lower_grads",
    )(span_order, doc_lengths, q, g, level, mixed, *blocks)


def swap(x, k, axis):
    return lax.ppermute(x, axis, [(i, i ^ k) for i in range(lax.axis_size(axis))])


def gather_even(x, axis, held):
    size = lax.axis_size(axis)
    got, bit = {0: x}, 2
    while bit < size:
        passed = {k: block for k, block in got.items() if k}
        passed, held = lax.optimization_barrier((passed, held))
        got |= {bit: swap(x, bit, axis)}
        got |= {k ^ bit: swap(block, bit, axis) for k, block in passed.items()}
        bit *= 2
    return [got[k] for k in sorted(got)], held


def pair_body(even_ref, *refs):
    count = even_ref.shape[0]
    odd_refs, outs = refs[:-count], refs[-count:]
    part = odd_refs[0].shape[0]
    for k, out in enumerate(outs):
        total = even_ref[k].astype(jnp.float32) + odd_refs[k // part][k % part].astype(jnp.float32)
        out[...] = total.astype(out.dtype)


def pair_sums(even, *got):
    count, rows, width = even.shape
    return pl.pallas_call(
        pair_body,
        in_specs=[pl.BlockSpec(memory_space=VMEM)] * (1 + len(got)),
        out_specs=[pl.BlockSpec(memory_space=VMEM)] * count,
        out_shape=[jax.ShapeDtypeStruct((rows, width), jnp.bfloat16)] * count,
        compiler_params=params(),
        cost_estimate=cost(0.7),
        name="pair_sums",
    )(even, *got)


def scatter_ctx(pairs):
    return [part if k == 0 else swap(part, 2 * k, "ctx") for k, part in enumerate(pairs)]


def shards(inputs, out_grad, w_query, w_key, value_projection, w_out, doc_lengths, span_order):
    tokens = inputs.shape[0]
    share = ASKER_NUM // SHARED_KV_NUM
    half = tokens // 2
    sizes = (
        lax.axis_size("ctx"),
        tokens // 2,
        w_key.shape[1] // CHANNEL_DIM,
        share,
        CHANNEL_DIM,
        doc_lengths.shape[0],
    )
    heads = lax.axis_size("head")
    last = [span_order]

    def turn(call, *args):
        held, *args = lax.optimization_barrier((last[0], *args))
        out = call(*args)
        last[0] = out if hasattr(out, "shape") else out[0]
        return out

    def attend(upper, call, *args):
        return turn(lambda *a: call(upper, *a, span_order, doc_lengths, sizes), *args)

    def context(blocks, places, total, dtype):
        shape = jax.tree.structure((blocks, total))

        def call(*flat):
            parts, given = jax.tree.unflatten(shape, flat)
            return back_project(parts, places, w_out, given, dtype)

        return turn(call, *jax.tree.leaves((blocks, total)))

    def send_first(parts, stack):
        places = range(heads - 1, 0, -2)
        if stack is None:
            return {k ^ 1: (swap(parts[k], 1, "head"), None) for k in places}
        got = swap(stack, 1, "head")
        return {k ^ 1: (got, i) for i, k in enumerate(places)}

    def send_rest(parts, got):
        ends, bit = [(parts[0], None), got[0]], 2
        parts = {
            k: turn(lambda a, b, at=got[k][1]: add(a, b, at), parts[k], got[k][0])
            for k in range(2, heads, 2)
        }
        while bit < heads:
            moved = {k ^ bit: swap(parts[k], bit, "head") for k in parts if k & bit}
            ends.append((moved.pop(0), None))
            parts = {k: turn(lambda a, b: add(a, b, None), parts[k], moved[k]) for k in moved}
            bit *= 2
        return ends

    far = [{0: out_grad[:half]}, {0: out_grad[half:]}]
    bit = heads // 2
    while bit > 1:
        far = [got | {k ^ bit: swap(x, bit, "head") for k, x in got.items()} for got in far]
        bit //= 2
    near = swap(out_grad, 1, "head")
    own = turn(project_kv, inputs, w_key, value_projection)
    near_blocks, far[0] = gather_even(own, "ctx", far[0])
    query = turn(project, inputs, w_query)
    query, near_blocks = lax.optimization_barrier((query, near_blocks))
    blocks = (*near_blocks, *[swap(block, 1, "ctx") for block in near_blocks])
    query, far[1], near = lax.optimization_barrier((query, far[1], near))
    upper_stats = attend(True, stats, query, *blocks)
    lower_stats = attend(False, stats, query, *blocks)
    passed = [{k ^ 1: swap(x, 1, "head") for k, x in got.items() if k} for got in far]
    firsts = {0: (out_grad,), 1: (near,)}
    firsts |= {k: (far[0][k], far[1][k]) for k in range(2, heads, 2)}
    lasts = {k: (passed[0][k], passed[1][k]) for k in range(3, heads, 2)}
    total = context(list(firsts.values()), list(firsts), None, jnp.float32)
    context_grad = context(list(lasts.values()), list(lasts), total, jnp.bfloat16)
    upper_dq, even, *odd, rest = attend(True, grads, query, context_grad, *upper_stats, *blocks)
    upper = scatter_ctx(turn(pair_sums, even, *[swap(x, 1, "ctx") for x in odd]))
    lower_dq, even, *odd = attend(
        False, grads, query, context_grad, *lower_stats, rest, *blocks
    )
    sides = [list(range(heads - 1, 0, -2)), list(range(heads - 2, -1, -2))]

    def firsts_of(places):
        return turn(lambda a, b: query_terms(a, b, w_query, heads, places), upper_dq, lower_dq)

    def terms_of(first, terms, places, stacked=False):
        outs = turn(
            lambda a, *b: all_terms(a, b, w_key, value_projection, places, stacked), first, *terms
        )
        return outs[0] if stacked else dict(zip(places, outs))

    first = [firsts_of(sides[0])]
    lower_odd = [swap(x, 1, "ctx") for x in odd]
    upper_got = send_first(None, terms_of(first[0][0], upper, sides[0], True))
    lower = scatter_ctx(turn(pair_sums, even, *lower_odd))
    first.append(firsts_of(sides[1]))
    upper = send_rest(terms_of(first[1][0], upper, sides[1]), upper_got)
    lower_got = send_first(terms_of(first[0][1], lower, sides[0]), None)
    lower = send_rest(terms_of(first[1][1], lower, sides[1]), lower_got)
    return join_rows(upper, lower, span_order)


def solution(mesh):
    in_specs = (
        P("ctx", None),
        P("ctx", "head"),
        P(None, "head"),
        P(None, "head"),
        P(None, "head"),
        P("head", None),
        P(),
        P(),
    )
    out_specs = P("ctx", "head")
    return jax.shard_map(shards, mesh=mesh, in_specs=in_specs, out_specs=out_specs, check_vma=False)
```

```python
import functools
import math

import jax
import jax.numpy as jnp
from jax import lax
from jax.experimental import pallas as pl
from jax.experimental.pallas import tpu as pltpu
from jax.sharding import PartitionSpec as P

ASKER_NUM = 32
SHARED_KV_NUM = 8
CHANNEL_DIM = 128

masked_score = -1e30
MIB = 1 << 20
COST = 0
AT_ONCE = 4
PARTS = 2
VMEM = pltpu.VMEM
HBM = pltpu.HBM


def mm(a, b):
    return lax.dot_general(a, b, (((1,), (0,)), ((), ())), preferred_element_type=jnp.float32)


def mm_nt(a, b):
    return lax.dot_general(a, b, (((1,), (1,)), ((), ())), preferred_element_type=jnp.float32)


def mm_tn(a, b):
    return lax.dot_general(a, b, (((0,), (0,)), ((), ())), preferred_element_type=jnp.float32)


def params():
    return pltpu.CompilerParams(vmem_limit_bytes=24 * MIB)


def cost(micros):
    return pl.CostEstimate(flops=int(micros * COST), bytes_accessed=1, transcendentals=0)


def upper_half(order):
    first = order[2 * lax.axis_index("ctx")]
    return jnp.where(2 * first >= order.shape[0], 0, 1)


def in_hbm(x):
    return pltpu.with_memory_space_constraint(x, HBM)


def fetch(src, dst, sem):
    copy = pltpu.make_async_copy(src, dst, sem)
    copy.start()
    return copy


def kv_body(parts, x_ref, wk_ref, wv_ref, out_ref, x, wk, wv, acc, sems):
    width = wk.shape[1]
    depth = wk.shape[0] // parts
    copies = []
    for i in range(parts):
        rows = slice(i * depth, (i + 1) * depth)
        copies.append(
            [
                fetch(x_ref.at[:, rows], x.at[:, rows], sems.at[i, 0]),
                fetch(wk_ref.at[rows], wk.at[rows], sems.at[i, 1]),
                fetch(wv_ref.at[rows], wv.at[rows], sems.at[i, 2]),
            ]
        )
    for i in range(parts):
        rows = slice(i * depth, (i + 1) * depth)
        for copy in copies[i]:
            copy.wait()
        left = x[:, rows]
        terms = mm(left, wk[rows, :]), mm(left, wv[rows, :])
        for j, term in enumerate(terms):
            columns = slice(j * width, (j + 1) * width)
            total = term if i == 0 else acc[:, columns] + term
            if i < parts - 1:
                acc[:, columns] = total
            else:
                out_ref[:, columns] = total.astype(out_ref.dtype)


def project_kv(x, wk, wv):
    tokens, depth = x.shape
    width = wk.shape[1]
    parts = 4
    return pl.pallas_call(
        functools.partial(kv_body, parts),
        in_specs=[pl.BlockSpec(memory_space=HBM)] * 3,
        out_specs=pl.BlockSpec(memory_space=VMEM),
        out_shape=jax.ShapeDtypeStruct((tokens, 2 * width), jnp.bfloat16),
        scratch_shapes=[
            VMEM(x.shape, x.dtype),
            VMEM(wk.shape, wk.dtype),
            VMEM(wv.shape, wv.dtype),
            VMEM((tokens, 2 * width), jnp.float32),
            pltpu.SemaphoreType.DMA((parts, 3)),
        ],
        compiler_params=params(),
        cost_estimate=cost(3.4),
        name="project_kv",
    )(in_hbm(x), in_hbm(wk), in_hbm(wv))


def project_body(parts, x_ref, w_ref, out_ref, x, w, acc, sems):
    depth = w.shape[0] // parts
    copies = []
    for i in range(parts):
        rows = slice(i * depth, (i + 1) * depth)
        copies.append(
            [
                fetch(x_ref.at[:, rows], x.at[:, rows], sems.at[i, 0]),
                fetch(w_ref.at[rows], w.at[rows], sems.at[i, 1]),
            ]
        )
    for i in range(parts):
        rows = slice(i * depth, (i + 1) * depth)
        for copy in copies[i]:
            copy.wait()
        total = mm(x[:, rows], w[rows, :])
        if i:
            total = acc[...] + total
        if i < parts - 1:
            acc[...] = total
        else:
            out_ref[...] = total.astype(out_ref.dtype)


def project(x, w):
    tokens, depth = x.shape
    width = w.shape[1]
    parts = 4
    return pl.pallas_call(
        functools.partial(project_body, parts),
        in_specs=[pl.BlockSpec(memory_space=HBM)] * 2,
        out_specs=pl.BlockSpec(memory_space=VMEM),
        out_shape=jax.ShapeDtypeStruct((tokens, width), jnp.bfloat16),
        scratch_shapes=[
            VMEM(x.shape, x.dtype),
            VMEM(w.shape, w.dtype),
            VMEM((tokens, width), jnp.float32),
            pltpu.SemaphoreType.DMA((parts, 2)),
        ],
        compiler_params=params(),
        cost_estimate=cost(4.9),
        name="project",
    )(in_hbm(x), in_hbm(w))


def back_body(places, given, rows, *refs):
    refs = list(refs)
    sems, w = refs.pop(), refs.pop()
    out_ref, w_ref = refs.pop(), refs.pop()
    me = lax.axis_index("head")
    depth = w.shape[2]
    step = depth // PARTS
    copies = {}
    for i, k in enumerate(places):
        for j in range(PARTS):
            columns = pl.ds(pl.multiple_of((me ^ k) * depth + j * step, step), step)
            part = slice(j * step, (j + 1) * step)
            copies[i, j] = fetch(w_ref.at[:, columns], w.at[i, :, part], sems.at[i, j])
    total = refs.pop(0)[...] if given else None
    for i in range(len(places)):
        x = refs.pop(0)[...]
        if x.shape[0] < rows:
            x = jnp.concatenate([x, refs.pop(0)[...]], axis=0)
        for j in range(PARTS):
            copies[i, j].wait()
            part = slice(j * step, (j + 1) * step)
            term = mm_nt(x[:, part], w[i, :, part])
            total = term if total is None else total + term
    out_ref[...] = total.astype(out_ref.dtype)


def back_project(blocks, places, w, total, dtype):
    rows, depth = blocks[0][0].shape[0] * len(blocks[0]), blocks[0][0].shape[1]
    given = [] if total is None else [total]
    flat = [x for block in blocks for x in block]
    return pl.pallas_call(
        functools.partial(back_body, places, len(given), rows),
        in_specs=[pl.BlockSpec(memory_space=VMEM)] * (len(given) + len(flat))
        + [pl.BlockSpec(memory_space=HBM)],
        out_specs=pl.BlockSpec(memory_space=VMEM),
        out_shape=jax.ShapeDtypeStruct((rows, w.shape[0]), dtype),
        scratch_shapes=[
            VMEM((len(places), w.shape[0], depth), w.dtype),
            pltpu.SemaphoreType.DMA((len(places), PARTS)),
        ],
        compiler_params=params(),
        cost_estimate=cost(3.4),
        name="context_grad",
    )(*given, *flat, in_hbm(w))


def query_terms_body(places, upper_ref, lower_ref, w_ref, upper_out, lower_out, w, sems):
    me = lax.axis_index("head")
    share = w.shape[1]
    step = w.shape[2] // PARTS
    parts = [slice(j * step, (j + 1) * step) for j in range(PARTS)]
    copies = {}
    for i, k in enumerate(places):
        rows = pl.ds(pl.multiple_of((me ^ k) * share, share), share)
        for j, part in enumerate(parts):
            copies[i, j] = fetch(w_ref.at[rows, part], w.at[i, :, part], sems.at[i, j])
    half = upper_ref.shape[0]
    x = jnp.concatenate([upper_ref[...], lower_ref[...]], axis=0)
    for i in range(len(places)):
        total = None
        for j, part in enumerate(parts):
            copies[i, j].wait()
            term = mm_nt(x[:, part], w[i, :, part])
            total = term if total is None else total + term
        upper_out[i] = total[:half]
        lower_out[i] = total[half:]


def query_terms(upper, lower, w, heads, places):
    rows, depth = upper.shape
    share = w.shape[0] // heads
    size = len(places)
    return pl.pallas_call(
        functools.partial(query_terms_body, places),
        in_specs=[pl.BlockSpec(memory_space=VMEM)] * 2 + [pl.BlockSpec(memory_space=HBM)],
        out_specs=[pl.BlockSpec(memory_space=VMEM)] * 2,
        out_shape=[jax.ShapeDtypeStruct((size, rows, share), jnp.float32)] * 2,
        scratch_shapes=[
            VMEM((size, share, depth), w.dtype),
            pltpu.SemaphoreType.DMA((size, PARTS)),
        ],
        compiler_params=params(),
        cost_estimate=cost(4.6),
        name="query_terms",
    )(upper, lower, in_hbm(w))


def all_terms_body(places, count, first_ref, *refs):
    terms, (wk_ref, wv_ref), refs = refs[:count], refs[count : count + 2], refs[count + 2 :]
    outs, (wk, wv, sems) = refs[:-3], refs[-3:]
    me = lax.axis_index("head")
    size, share, width = wk.shape
    copies = {}
    for i, k in enumerate(places):
        rows = pl.ds(pl.multiple_of((me ^ k) * share, share), share)
        copies[i] = [
            fetch(wk_ref.at[rows], wk.at[i], sems.at[i, 0]),
            fetch(wv_ref.at[rows], wv.at[i], sems.at[i, 1]),
        ]
    grads = terms[0][...].astype(jnp.float32)
    for term in terms[1:]:
        grads = grads + term[...].astype(jnp.float32)
    grads = grads.astype(jnp.bfloat16)
    for i, pair in copies.items():
        for copy in pair:
            copy.wait()
        total = first_ref[i] + mm_nt(grads[:, :width], wk[i])
        total = total + mm_nt(grads[:, width:], wv[i])
        if len(outs) == 1:
            outs[0][i] = total.astype(outs[0].dtype)
        else:
            outs[i][...] = total.astype(outs[i].dtype)


def all_terms(first, terms, wk, wv, places, stacked):
    size, rows, share = first.shape
    width = wk.shape[1]
    return pl.pallas_call(
        functools.partial(all_terms_body, places, len(terms)),
        in_specs=[pl.BlockSpec(memory_space=VMEM)] * (1 + len(terms))
        + [pl.BlockSpec(memory_space=HBM)] * 2,
        out_specs=[pl.BlockSpec(memory_space=VMEM)] * (1 if stacked else size),
        out_shape=[jax.ShapeDtypeStruct((size, rows, share), jnp.bfloat16)]
        if stacked
        else [jax.ShapeDtypeStruct((rows, share), jnp.bfloat16)] * size,
        scratch_shapes=[
            VMEM((size, share, width), wk.dtype),
            VMEM((size, share, width), wv.dtype),
            pltpu.SemaphoreType.DMA((size, 2)),
        ],
        compiler_params=params(),
        cost_estimate=cost(3.2),
        name="all_terms",
    )(first, *terms, in_hbm(wk), in_hbm(wv))


def part_of(ref, at):
    return (ref[...] if at is None else ref[at]).astype(jnp.float32)


def add_body(at, a_ref, b_ref, out_ref):
    out_ref[...] = (a_ref[...].astype(jnp.float32) + part_of(b_ref, at)).astype(out_ref.dtype)


def add(a, b, at):
    return pl.pallas_call(
        functools.partial(add_body, at),
        in_specs=[pl.BlockSpec(memory_space=VMEM)] * 2,
        out_specs=pl.BlockSpec(memory_space=VMEM),
        out_shape=jax.ShapeDtypeStruct(a.shape, a.dtype),
        compiler_params=params(),
        cost_estimate=cost(0.5),
        name="add",
    )(a, b)


def join_body(ats, order, *refs):
    refs, out_ref = list(refs[:-1]), refs[-1]
    half = out_ref.shape[0] // 2
    at = upper_half(order) * half
    for j, place in enumerate((at, half - at)):
        total = None
        for i in ats[j]:
            term = part_of(refs.pop(0), i)
            total = term if total is None else total + term
        out_ref[pl.ds(pl.multiple_of(place, half), half), :] = total.astype(out_ref.dtype)


def join_rows(upper, lower, span_order):
    rows, width = upper[0][0].shape
    ats = [[at for _, at in terms] for terms in (upper, lower)]
    blocks = [block for block, _ in upper + lower]
    return pl.pallas_call(
        functools.partial(join_body, ats),
        in_specs=[pl.BlockSpec(memory_space=pltpu.SMEM)]
        + [pl.BlockSpec(memory_space=VMEM)] * len(blocks),
        out_specs=pl.BlockSpec(memory_space=VMEM),
        out_shape=jax.ShapeDtypeStruct((2 * rows, width), jnp.bfloat16),
        compiler_params=params(),
        cost_estimate=cost(1.5),
        name="join_rows",
    )(span_order, *blocks)


def find_places(order, places, me, spans):
    for i in range(spans):
        k = (i // 2) ^ me
        places[order[i]] = (k % 2) * (spans // 2) + (k // 2) * 2 + (i % 2)


def own_span(order, lengths, docs, me, j, half):
    span = order[2 * me + j]
    position = span * half + lax.broadcasted_iota(jnp.int32, (1, half), 1)
    first, end = 0, 0
    start = jnp.zeros((1, half), jnp.int32)
    for k in range(docs):
        end = end + lengths[k]
        start = jnp.where(position >= end, end, start)
        first = jnp.where(span * half >= end, end, first)
    return span, position, start, first // half


def stack_heads(ref, rows, group, share, dim):
    base = group * share
    return jnp.concatenate(
        [ref[rows, (base + h) * dim : (base + h + 1) * dim] for h in range(share)], axis=0
    )


def load_blocks(refs, held):
    rows = refs[0].shape[0]
    for k, ref in enumerate(refs):
        held[k * rows : (k + 1) * rows, :] = ref[...]


def span_group(i, span, held, places, half):
    numbers = [span - AT_ONCE * i - j for j in range(AT_ONCE - 1, -1, -1)]
    known = [jnp.maximum(p, 0) for p in numbers]
    at = [pl.multiple_of(places[p] * half, half) for p in known]
    block = jnp.concatenate([held[pl.ds(place, half), :] for place in at], axis=0)
    key = numbers[0] * half + lax.broadcasted_iota(jnp.int32, (AT_ONCE * half, 1), 0)
    return known, block, key


def keep(allowed, x, other):
    width = allowed.shape[1]
    return jnp.concatenate(
        [
            jnp.where(allowed, x[:, i : i + width], other)
            for i in range(0, x.shape[1], width)
        ],
        axis=1,
    )


def stats_body(sizes, upper, order, lengths, q_ref, *refs):
    peers, half, groups, share, dim, docs = sizes
    if upper:
        level_ref, mixed_ref, held, kept, places = refs[peers:]
        load_blocks(refs[:peers], held)
    else:
        held, level_ref, mixed_ref, kept, places = refs
    me = lax.axis_index("ctx")
    width = groups * dim
    factor = math.log2(math.e) / math.sqrt(dim)
    find_places(order, places, me, 2 * peers)
    columns = share * half
    at = upper_half(order)
    j = at if upper else 1 - at
    span, position, start, lowest = own_span(order, lengths, docs, me, j, half)
    rows = pl.ds(pl.multiple_of(j * half, half), half)
    queries = [stack_heads(q_ref, rows, g, share, dim) for g in range(groups)]

    deep = AT_ONCE * half
    steps = (span - lowest) // AT_ONCE + 1

    def score(i, carry):
        known, block, key = span_group(i, span, held, places, half)
        allowed = (key <= position) & (key >= start)
        fresh = []
        for g in range(groups):
            logits = keep(allowed, mm_nt(block[:, g * dim : (g + 1) * dim], queries[g]), masked_score)
            kept[g, pl.ds(pl.multiple_of(i * deep, deep), deep), :] = logits
            high = jnp.max(logits.reshape(deep // 8, 8, columns), axis=0)
            fresh.append(jnp.maximum(carry[g], high))
        return tuple(fresh)

    empty = jnp.full((8, columns), masked_score, jnp.float32)
    tops = lax.fori_loop(0, steps, score, (empty,) * groups)
    tops = [jnp.max(top, axis=0, keepdims=True) for top in tops]

    def mix(i, carry):
        known, block, key = span_group(i, span, held, places, half)
        fresh = []
        for g in range(groups):
            total, mixed = carry[g]
            values = block[:, width + g * dim : width + (g + 1) * dim]
            logits = kept[g, pl.ds(pl.multiple_of(i * deep, deep), deep), :]
            weights = jnp.exp2((logits - tops[g]) * factor)
            total = total + jnp.sum(weights.reshape(deep // 8, 8, columns), axis=0)
            mixed = mixed + mm_tn(values, weights.astype(jnp.bfloat16))
            fresh.append((total, mixed))
        return tuple(fresh)

    empty = (jnp.zeros((8, columns), jnp.float32), jnp.zeros((dim, columns), jnp.float32))
    done = lax.fori_loop(0, steps, mix, (empty,) * groups)
    for g in range(groups):
        top, (total, mixed) = tops[g], done[g]
        total = jnp.sum(total, axis=0, keepdims=True)
        level_ref[g] = top * factor + jnp.log2(total)
        mixed_ref[g] = mixed / total


def stats(upper, q, *args):
    *blocks, span_order, doc_lengths, sizes = args
    peers, half, groups, share, dim, docs = sizes
    columns = share * half
    return pl.pallas_call(
        functools.partial(stats_body, sizes, upper),
        in_specs=[pl.BlockSpec(memory_space=pltpu.SMEM)] * 2
        + [pl.BlockSpec(memory_space=VMEM)] * (1 + len(blocks)),
        out_specs=[pl.BlockSpec(memory_space=VMEM)] * (3 if upper else 2),
        out_shape=[
            jax.ShapeDtypeStruct((groups, 1, columns), jnp.float32),
            jax.ShapeDtypeStruct((groups, dim, columns), jnp.float32),
        ]
        + [jax.ShapeDtypeStruct((2 * peers * half, 2 * groups * dim), jnp.bfloat16)] * upper,
        scratch_shapes=[
            VMEM((groups, (2 * peers + AT_ONCE) * half, columns), jnp.float32),
            pltpu.SMEM((2 * peers,), jnp.int32),
        ],
        compiler_params=params(),
        cost_estimate=cost(2.4),
        name="upper_stats" if upper else "lower_stats",
    )(span_order, doc_lengths, q, *blocks)


def grads_body(sizes, upper, order, lengths, q_ref, g_ref, level_ref, mixed_ref, *refs):
    peers, half, groups, share, dim, docs = sizes
    spans = 2 * peers
    if upper:
        held, dq_ref, even_ref, *odd_refs, rest_ref, sums, places = refs
    else:
        rest_ref, held, dq_ref, even_ref, *odd_refs, sums, places = refs
    me = lax.axis_index("ctx")
    width = groups * dim
    scale = 1.0 / math.sqrt(dim)
    factor = math.log2(math.e) * scale
    find_places(order, places, me, spans)
    columns = share * half
    at = upper_half(order)
    j = at if upper else 1 - at
    span, position, start, lowest = own_span(order, lengths, docs, me, j, half)
    if upper:
        sums[...] = jnp.zeros_like(sums)
    else:
        sums[...] = rest_ref[...]
    rows = pl.ds(pl.multiple_of(j * half, half), half)
    queries = [stack_heads(q_ref, rows, g, share, dim) for g in range(groups)]
    outs = [stack_heads(g_ref, rows, g, share, dim) for g in range(groups)]
    levels = [level_ref[g] for g in range(groups)]
    deltas = []
    for g in range(groups):
        turned = jnp.concatenate(
            [outs[g][h * half : (h + 1) * half].astype(jnp.float32).T for h in range(share)],
            axis=1,
        )
        deltas.append(jnp.sum(turned * mixed_ref[g], axis=0, keepdims=True))

    def visit(i, carry):
        known, block, key = span_group(i, span, held, places, half)
        allowed = (key <= position) & (key >= start)
        targets = [pl.ds(pl.multiple_of(p * half, half), half) for p in known]
        fresh = []
        for g in range(groups):
            keys = block[:, g * dim : (g + 1) * dim]
            values = block[:, width + g * dim : width + (g + 1) * dim]
            logits = mm_nt(keys, queries[g]) * factor
            chance = keep(allowed, jnp.exp2(logits - levels[g]), 0.0)
            slopes = mm_nt(values, outs[g])
            score = (chance * (slopes - deltas[g])).astype(jnp.bfloat16)
            key_term = mm(score, queries[g])
            value_term = mm(chance.astype(jnp.bfloat16), outs[g])
            for j, target in enumerate(targets):
                part = slice(j * half, (j + 1) * half)
                sums[target, g * dim : (g + 1) * dim] += key_term[part]
                sums[target, width + g * dim : width + (g + 1) * dim] += value_term[part]
            fresh.append(carry[g] + mm_tn(keys, score))
        return tuple(fresh)

    empty = jnp.zeros((dim, columns), jnp.float32)
    done = lax.fori_loop(0, (span - lowest) // AT_ONCE + 1, visit, (empty,) * groups)
    for g in range(groups):
        for h in range(share):
            head = g * share + h
            dq_ref[:, head * dim : (head + 1) * dim] = (
                (done[g][:, h * half : (h + 1) * half].T * scale).astype(dq_ref.dtype)
            )
    for k in range(peers):
        out, slot = even_ref, k // 2
        if k % 2:
            out, slot = odd_refs[slot // odd_refs[0].shape[0]], slot % odd_refs[0].shape[0]
        first = order[2 * (me ^ k)]
        other = spans - 1 - first
        pick = jnp.maximum(first, other) if upper else jnp.minimum(first, other)
        part = pl.ds(pl.multiple_of(pick * half, half), half)
        out[slot, :, :width] = (sums[part, :width] * scale).astype(out.dtype)
        out[slot, :, width:] = sums[part, width:].astype(out.dtype)
    if upper:
        rest_ref[...] = sums[: peers * half, :]


def grads(upper, q, g, level, mixed, *args):
    *blocks, span_order, doc_lengths, sizes = args
    peers, half, groups, share, dim, docs = sizes
    tokens, width = 2 * half, groups * dim
    columns = share * half
    terms = jax.ShapeDtypeStruct((peers // 2, half, 2 * width), jnp.bfloat16)
    odds = jax.ShapeDtypeStruct((peers // 4, half, 2 * width), jnp.bfloat16)
    rests = jax.ShapeDtypeStruct((peers * half, 2 * width), jnp.float32)
    outs = [jax.ShapeDtypeStruct((half, g.shape[1]), jnp.bfloat16), terms, odds, odds] + [rests] * upper
    return pl.pallas_call(
        functools.partial(grads_body, sizes, upper),
        in_specs=[pl.BlockSpec(memory_space=pltpu.SMEM)] * 2
        + [pl.BlockSpec(memory_space=VMEM)] * (4 + len(blocks)),
        out_specs=[pl.BlockSpec(memory_space=VMEM)] * len(outs),
        out_shape=outs,
        scratch_shapes=[
            VMEM(((2 if upper else 1) * peers * half, 2 * width), jnp.float32),
            pltpu.SMEM((2 * peers,), jnp.int32),
        ],
        compiler_params=params(),
        cost_estimate=cost(3.0),
        name="upper_grads" if upper else "lower_grads",
    )(span_order, doc_lengths, q, g, level, mixed, *blocks)


def swap(x, k, axis):
    return lax.ppermute(x, axis, [(i, i ^ k) for i in range(lax.axis_size(axis))])


def gather_even(x, axis, held):
    size = lax.axis_size(axis)
    got, bit = {0: x}, 2
    while bit < size:
        passed = {k: block for k, block in got.items() if k}
        passed, held = lax.optimization_barrier((passed, held))
        got |= {bit: swap(x, bit, axis)}
        got |= {k ^ bit: swap(block, bit, axis) for k, block in passed.items()}
        bit *= 2
    return [got[k] for k in sorted(got)], held


def pair_body(even_ref, *refs):
    count = even_ref.shape[0]
    odd_refs, outs = refs[:-count], refs[-count:]
    part = odd_refs[0].shape[0]
    for k, out in enumerate(outs):
        total = even_ref[k].astype(jnp.float32) + odd_refs[k // part][k % part].astype(jnp.float32)
        out[...] = total.astype(out.dtype)


def pair_sums(even, *got):
    count, rows, width = even.shape
    return pl.pallas_call(
        pair_body,
        in_specs=[pl.BlockSpec(memory_space=VMEM)] * (1 + len(got)),
        out_specs=[pl.BlockSpec(memory_space=VMEM)] * count,
        out_shape=[jax.ShapeDtypeStruct((rows, width), jnp.bfloat16)] * count,
        compiler_params=params(),
        cost_estimate=cost(0.7),
        name="pair_sums",
    )(even, *got)


def scatter_ctx(pairs):
    return [part if k == 0 else swap(part, 2 * k, "ctx") for k, part in enumerate(pairs)]


def shards(inputs, out_grad, w_query, w_key, value_projection, w_out, doc_lengths, span_order):
    tokens = inputs.shape[0]
    share = ASKER_NUM // SHARED_KV_NUM
    half = tokens // 2
    sizes = (
        lax.axis_size("ctx"),
        tokens // 2,
        w_key.shape[1] // CHANNEL_DIM,
        share,
        CHANNEL_DIM,
        doc_lengths.shape[0],
    )
    heads = lax.axis_size("head")
    last = [span_order]

    def turn(call, *args):
        held, *args = lax.optimization_barrier((last[0], *args))
        out = call(*args)
        last[0] = out if hasattr(out, "shape") else out[0]
        return out

    def attend(upper, call, *args):
        return turn(lambda *a: call(upper, *a, span_order, doc_lengths, sizes), *args)

    def context(blocks, places, total, dtype):
        shape = jax.tree.structure((blocks, total))

        def call(*flat):
            parts, given = jax.tree.unflatten(shape, flat)
            return back_project(parts, places, w_out, given, dtype)

        return turn(call, *jax.tree.leaves((blocks, total)))

    def send_first(parts, stack):
        places = range(heads - 1, 0, -2)
        if stack is None:
            return {k ^ 1: (swap(parts[k], 1, "head"), None) for k in places}
        got = swap(stack, 1, "head")
        return {k ^ 1: (got, i) for i, k in enumerate(places)}

    def send_rest(parts, got):
        ends, bit = [(parts[0], None), got[0]], 2
        parts = {
            k: turn(lambda a, b, at=got[k][1]: add(a, b, at), parts[k], got[k][0])
            for k in range(2, heads, 2)
        }
        while bit < heads:
            moved = {k ^ bit: swap(parts[k], bit, "head") for k in parts if k & bit}
            ends.append((moved.pop(0), None))
            parts = {k: turn(lambda a, b: add(a, b, None), parts[k], moved[k]) for k in moved}
            bit *= 2
        return ends

    far = [{0: out_grad[:half]}, {0: out_grad[half:]}]
    bit = heads // 2
    while bit > 1:
        far = [got | {k ^ bit: swap(x, bit, "head") for k, x in got.items()} for got in far]
        bit //= 2
    near = [swap(out_grad[:half], 1, "head"), swap(out_grad[half:], 1, "head")]
    own = turn(project_kv, inputs, w_key, value_projection)
    near_blocks, (far[0], near[0]) = gather_even(own, "ctx", (far[0], near[0]))
    query = turn(project, inputs, w_query)
    query, near_blocks = lax.optimization_barrier((query, near_blocks))
    blocks = (*near_blocks, *[swap(block, 1, "ctx") for block in near_blocks])
    query, far[1], near[1] = lax.optimization_barrier((query, far[1], near[1]))
    *upper_stats, held = attend(True, stats, query, *blocks)
    lower_stats = attend(False, stats, query, held)
    passed = [{k ^ 1: swap(x, 1, "head") for k, x in got.items() if k} for got in far]
    firsts = {0: (out_grad,), 1: tuple(near)}
    firsts |= {k: (far[0][k], far[1][k]) for k in range(2, heads, 2)}
    lasts = {k: (passed[0][k], passed[1][k]) for k in range(3, heads, 2)}
    total = context(list(firsts.values()), list(firsts), None, jnp.float32)
    context_grad = context(list(lasts.values()), list(lasts), total, jnp.bfloat16)
    upper_dq, even, *odd, rest = attend(True, grads, query, context_grad, *upper_stats, held)
    upper = scatter_ctx(turn(pair_sums, even, *[swap(x, 1, "ctx") for x in odd]))
    lower_dq, even, *odd = attend(
        False, grads, query, context_grad, *lower_stats, rest, held
    )
    sides = [list(range(heads - 1, 0, -2)), list(range(heads - 2, -1, -2))]

    def firsts_of(places):
        return turn(lambda a, b: query_terms(a, b, w_query, heads, places), upper_dq, lower_dq)

    def terms_of(first, terms, places, stacked=False):
        outs = turn(
            lambda a, *b: all_terms(a, b, w_key, value_projection, places, stacked), first, *terms
        )
        return outs[0] if stacked else dict(zip(places, outs))

    first = [firsts_of(sides[0])]
    lower_odd = [swap(x, 1, "ctx") for x in odd]
    upper_got = send_first(None, terms_of(first[0][0], upper, sides[0], True))
    lower = scatter_ctx(turn(pair_sums, even, *lower_odd))
    first.append(firsts_of(sides[1]))
    lower_got = send_first(terms_of(first[0][1], lower, sides[0]), None)
    upper = send_rest(terms_of(first[1][0], upper, sides[1]), upper_got)
    lower = send_rest(terms_of(first[1][1], lower, sides[1]), lower_got)
    return join_rows(upper, lower, span_order)


def solution(mesh):
    in_specs = (
        P("ctx", None),
        P("ctx", "head"),
        P(None, "head"),
        P(None, "head"),
        P(None, "head"),
        P("head", None),
        P(),
        P(),
    )
    out_specs = P("ctx", "head")
    return jax.shard_map(shards, mesh=mesh, in_specs=in_specs, out_specs=out_specs, check_vma=False)
```

```python
import functools
import math

import jax
import jax.numpy as jnp
from jax import lax
from jax.experimental import pallas as pl
from jax.experimental.pallas import tpu as pltpu
from jax.sharding import PartitionSpec as P

ASKER_NUM = 32
SHARED_KV_NUM = 8
CHANNEL_DIM = 128

masked_score = -1e30
MIB = 1 << 20
COST = 0
AT_ONCE = 4
PARTS = 2
VMEM = pltpu.VMEM
HBM = pltpu.HBM


def mm(a, b):
    return lax.dot_general(a, b, (((1,), (0,)), ((), ())), preferred_element_type=jnp.float32)


def mm_nt(a, b):
    return lax.dot_general(a, b, (((1,), (1,)), ((), ())), preferred_element_type=jnp.float32)


def mm_tn(a, b):
    return lax.dot_general(a, b, (((0,), (0,)), ((), ())), preferred_element_type=jnp.float32)


def params():
    return pltpu.CompilerParams(vmem_limit_bytes=24 * MIB)


def cost(micros):
    return pl.CostEstimate(flops=int(micros * COST), bytes_accessed=1, transcendentals=0)


def upper_half(order):
    first = order[2 * lax.axis_index("ctx")]
    return jnp.where(2 * first >= order.shape[0], 0, 1)


def in_hbm(x):
    return pltpu.with_memory_space_constraint(x, HBM)


def fetch(src, dst, sem):
    copy = pltpu.make_async_copy(src, dst, sem)
    copy.start()
    return copy


def kv_body(parts, x_ref, wk_ref, wv_ref, out_ref, x, wk, wv, acc, sems):
    width = wk.shape[1]
    depth = wk.shape[0] // parts
    copies = []
    for i in range(parts):
        rows = slice(i * depth, (i + 1) * depth)
        copies.append(
            [
                fetch(x_ref.at[:, rows], x.at[:, rows], sems.at[i, 0]),
                fetch(wk_ref.at[rows], wk.at[rows], sems.at[i, 1]),
                fetch(wv_ref.at[rows], wv.at[rows], sems.at[i, 2]),
            ]
        )
    for i in range(parts):
        rows = slice(i * depth, (i + 1) * depth)
        for copy in copies[i]:
            copy.wait()
        left = x[:, rows]
        terms = mm(left, wk[rows, :]), mm(left, wv[rows, :])
        for j, term in enumerate(terms):
            columns = slice(j * width, (j + 1) * width)
            total = term if i == 0 else acc[:, columns] + term
            if i < parts - 1:
                acc[:, columns] = total
            else:
                out_ref[:, columns] = total.astype(out_ref.dtype)


def project_kv(x, wk, wv):
    tokens, depth = x.shape
    width = wk.shape[1]
    parts = 4
    return pl.pallas_call(
        functools.partial(kv_body, parts),
        in_specs=[pl.BlockSpec(memory_space=HBM)] * 3,
        out_specs=pl.BlockSpec(memory_space=VMEM),
        out_shape=jax.ShapeDtypeStruct((tokens, 2 * width), jnp.bfloat16),
        scratch_shapes=[
            VMEM(x.shape, x.dtype),
            VMEM(wk.shape, wk.dtype),
            VMEM(wv.shape, wv.dtype),
            VMEM((tokens, 2 * width), jnp.float32),
            pltpu.SemaphoreType.DMA((parts, 3)),
        ],
        compiler_params=params(),
        cost_estimate=cost(3.4),
        name="project_kv",
    )(in_hbm(x), in_hbm(wk), in_hbm(wv))


def project_body(parts, x_ref, w_ref, out_ref, x, w, acc, sems):
    depth = w.shape[0] // parts
    copies = []
    for i in range(parts):
        rows = slice(i * depth, (i + 1) * depth)
        copies.append(
            [
                fetch(x_ref.at[:, rows], x.at[:, rows], sems.at[i, 0]),
                fetch(w_ref.at[rows], w.at[rows], sems.at[i, 1]),
            ]
        )
    for i in range(parts):
        rows = slice(i * depth, (i + 1) * depth)
        for copy in copies[i]:
            copy.wait()
        total = mm(x[:, rows], w[rows, :])
        if i:
            total = acc[...] + total
        if i < parts - 1:
            acc[...] = total
        else:
            out_ref[...] = total.astype(out_ref.dtype)


def project(x, w):
    tokens, depth = x.shape
    width = w.shape[1]
    parts = 4
    return pl.pallas_call(
        functools.partial(project_body, parts),
        in_specs=[pl.BlockSpec(memory_space=HBM)] * 2,
        out_specs=pl.BlockSpec(memory_space=VMEM),
        out_shape=jax.ShapeDtypeStruct((tokens, width), jnp.bfloat16),
        scratch_shapes=[
            VMEM(x.shape, x.dtype),
            VMEM(w.shape, w.dtype),
            VMEM((tokens, width), jnp.float32),
            pltpu.SemaphoreType.DMA((parts, 2)),
        ],
        compiler_params=params(),
        cost_estimate=cost(4.9),
        name="project",
    )(in_hbm(x), in_hbm(w))


def back_body(given, rows, spans, *refs):
    refs, out_ref = list(refs[:-1]), refs[-1]
    total = refs.pop(0)[...] if given else None
    stacks = [refs.pop() for _ in spans][::-1]
    for w, (low, high) in zip(stacks, spans):
        for i in range(low, high):
            x = refs.pop(0)[...]
            if x.shape[0] < rows:
                x = jnp.concatenate([x, refs.pop(0)[...]], axis=0)
            term = mm_nt(x, w[i])
            total = term if total is None else total + term
    out_ref[...] = total.astype(out_ref.dtype)


def back_project(blocks, stacks, spans, total, dtype):
    rows = blocks[0][0].shape[0] * len(blocks[0])
    given = [] if total is None else [total]
    flat = [x for block in blocks for x in block]
    operands = (*given, *flat, *stacks)
    return pl.pallas_call(
        functools.partial(back_body, len(given), rows, spans),
        in_specs=[pl.BlockSpec(memory_space=VMEM)] * len(operands),
        out_specs=pl.BlockSpec(memory_space=VMEM),
        out_shape=jax.ShapeDtypeStruct((rows, stacks[0].shape[1]), dtype),
        compiler_params=params(),
        cost_estimate=cost(3),
        name="context_grad",
    )(*operands)


def fetch_columns(places, ref, out, sems):
    me = lax.axis_index("head")
    depth = out.shape[2]
    return [
        fetch(ref.at[:, pl.ds(pl.multiple_of((me ^ k) * depth, depth), depth)], out.at[i], sems.at[i])
        for i, k in enumerate(places)
    ]


def fetch_rows(places, ref, out, sems, at):
    me = lax.axis_index("head")
    share = out.shape[1]
    return [
        fetch(ref.at[pl.ds(pl.multiple_of((me ^ k) * share, share), share)], out.at[i], sems.at[i, at])
        for i, k in enumerate(places)
    ]


def rows_shape(places, w, heads):
    return jax.ShapeDtypeStruct((len(places), w.shape[0] // heads, w.shape[1]), w.dtype)


def query_terms_body(places, upper_ref, lower_ref, w_ref, *refs):
    upper_out, lower_out = refs[:2]
    copies, w = [], w_ref
    if places is not None:
        w, sems = refs[2:]
        copies = fetch_rows(places, w_ref, w, sems, 0)
    half = upper_ref.shape[0]
    x = jnp.concatenate([upper_ref[...], lower_ref[...]], axis=0)
    for i in range(w.shape[0]):
        if copies:
            copies[i].wait()
        total = mm_nt(x, w[i])
        upper_out[i] = total[:half]
        lower_out[i] = total[half:]


def query_terms(upper, lower, w, heads, places):
    rows, depth = upper.shape
    scratch = []
    shape = w
    if w.ndim == 2:
        shape = rows_shape(places, w, heads)
        scratch = [VMEM(shape.shape, w.dtype), pltpu.SemaphoreType.DMA((len(places), 1))]
        w = in_hbm(w)
    else:
        places = None
    size, share = shape.shape[:2]
    return pl.pallas_call(
        functools.partial(query_terms_body, places),
        in_specs=[pl.BlockSpec(memory_space=VMEM)] * 2
        + [pl.BlockSpec(memory_space=HBM if scratch else VMEM)],
        out_specs=[pl.BlockSpec(memory_space=VMEM)] * 2,
        out_shape=[jax.ShapeDtypeStruct((size, rows, share), jnp.float32)] * 2,
        scratch_shapes=scratch,
        compiler_params=params(),
        cost_estimate=cost(3),
        name="query_terms",
    )(upper, lower, w)


def all_terms_body(places, count, first_ref, *refs):
    terms, (wk_ref, wv_ref), refs = refs[:count], refs[count : count + 2], refs[count + 2 :]
    wk, wv, copies = wk_ref, wv_ref, []
    if places is not None:
        refs, (wk, wv, sems) = refs[:-3], refs[-3:]
        copies = [fetch_rows(places, wk_ref, wk, sems, 0), fetch_rows(places, wv_ref, wv, sems, 1)]
    outs = refs
    width = wk.shape[2]
    grads = terms[0][...].astype(jnp.float32)
    for term in terms[1:]:
        grads = grads + term[...].astype(jnp.float32)
    grads = grads.astype(jnp.bfloat16)
    for i in range(wk.shape[0]):
        for some in copies:
            some[i].wait()
        total = first_ref[i] + mm_nt(grads[:, :width], wk[i])
        total = total + mm_nt(grads[:, width:], wv[i])
        if len(outs) == 1:
            outs[0][i] = total.astype(outs[0].dtype)
        else:
            outs[i][...] = total.astype(outs[i].dtype)


def all_terms(first, terms, wk, wv, heads, places, stacked):
    size, rows, share = first.shape
    scratch = []
    if wk.ndim == 2:
        shape = rows_shape(places, wk, heads).shape
        scratch = [
            VMEM(shape, wk.dtype),
            VMEM(shape, wv.dtype),
            pltpu.SemaphoreType.DMA((size, 2)),
        ]
        wk, wv = in_hbm(wk), in_hbm(wv)
    else:
        places = None
    return pl.pallas_call(
        functools.partial(all_terms_body, places, len(terms)),
        in_specs=[pl.BlockSpec(memory_space=VMEM)] * (1 + len(terms))
        + [pl.BlockSpec(memory_space=HBM if scratch else VMEM)] * 2,
        out_specs=[pl.BlockSpec(memory_space=VMEM)] * (1 if stacked else size),
        out_shape=[jax.ShapeDtypeStruct((size, rows, share), jnp.bfloat16)]
        if stacked
        else [jax.ShapeDtypeStruct((rows, share), jnp.bfloat16)] * size,
        scratch_shapes=scratch,
        compiler_params=params(),
        cost_estimate=cost(2),
        name="all_terms",
    )(first, *terms, wk, wv)


def part_of(ref, at):
    return (ref[...] if at is None else ref[at]).astype(jnp.float32)


def add_body(at, a_ref, b_ref, out_ref):
    out_ref[...] = (a_ref[...].astype(jnp.float32) + part_of(b_ref, at)).astype(out_ref.dtype)


def add(a, b, at):
    return pl.pallas_call(
        functools.partial(add_body, at),
        in_specs=[pl.BlockSpec(memory_space=VMEM)] * 2,
        out_specs=pl.BlockSpec(memory_space=VMEM),
        out_shape=jax.ShapeDtypeStruct(a.shape, a.dtype),
        compiler_params=params(),
        cost_estimate=cost(0.5),
        name="add",
    )(a, b)


def merge_body(at, a_ref, b_ref, out_ref):
    out_ref[...] = a_ref[...].astype(jnp.float32) + part_of(b_ref, at)


def merge(a, b, at):
    return pl.pallas_call(
        functools.partial(merge_body, at),
        in_specs=[pl.BlockSpec(memory_space=VMEM)] * 2,
        out_specs=pl.BlockSpec(memory_space=VMEM),
        out_shape=jax.ShapeDtypeStruct(a.shape, jnp.float32),
        compiler_params=params(),
        cost_estimate=cost(0.5),
        name="merge",
    )(a, b)


def join_body(ats, order, *refs):
    refs, out_ref = list(refs[:-1]), refs[-1]
    half = out_ref.shape[0] // 2
    at = upper_half(order) * half
    for j, place in enumerate((at, half - at)):
        total = None
        for i in ats[j]:
            term = part_of(refs.pop(0), i)
            total = term if total is None else total + term
        out_ref[pl.ds(pl.multiple_of(place, half), half), :] = total.astype(out_ref.dtype)


def join_rows(upper, lower, span_order):
    rows, width = upper[0][0].shape
    ats = [[at for _, at in terms] for terms in (upper, lower)]
    blocks = [block for block, _ in upper + lower]
    return pl.pallas_call(
        functools.partial(join_body, ats),
        in_specs=[pl.BlockSpec(memory_space=pltpu.SMEM)]
        + [pl.BlockSpec(memory_space=VMEM)] * len(blocks),
        out_specs=pl.BlockSpec(memory_space=VMEM),
        out_shape=jax.ShapeDtypeStruct((2 * rows, width), jnp.bfloat16),
        compiler_params=params(),
        cost_estimate=cost(1.5),
        name="join_rows",
    )(span_order, *blocks)


def find_places(order, places, me, spans):
    for i in range(spans):
        k = (i // 2) ^ me
        places[order[i]] = (k % 2) * (spans // 2) + (k // 2) * 2 + (i % 2)


def own_span(order, lengths, docs, me, j, half):
    span = order[2 * me + j]
    position = span * half + lax.broadcasted_iota(jnp.int32, (1, half), 1)
    first, end = 0, 0
    start = jnp.zeros((1, half), jnp.int32)
    for k in range(docs):
        end = end + lengths[k]
        start = jnp.where(position >= end, end, start)
        first = jnp.where(span * half >= end, end, first)
    return span, position, start, first // half


def stack_heads(ref, rows, group, share, dim):
    base = group * share
    return jnp.concatenate(
        [ref[rows, (base + h) * dim : (base + h + 1) * dim] for h in range(share)], axis=0
    )


def load_blocks(refs, held):
    rows = refs[0].shape[0]
    for k, ref in enumerate(refs):
        held[k * rows : (k + 1) * rows, :] = ref[...]


def span_group(i, span, held, places, half):
    numbers = [span - AT_ONCE * i - j for j in range(AT_ONCE - 1, -1, -1)]
    known = [jnp.maximum(p, 0) for p in numbers]
    at = [pl.multiple_of(places[p] * half, half) for p in known]
    block = jnp.concatenate([held[pl.ds(place, half), :] for place in at], axis=0)
    key = numbers[0] * half + lax.broadcasted_iota(jnp.int32, (AT_ONCE * half, 1), 0)
    return known, block, key


def keep(allowed, x, other):
    width = allowed.shape[1]
    return jnp.concatenate(
        [
            jnp.where(allowed, x[:, i : i + width], other)
            for i in range(0, x.shape[1], width)
        ],
        axis=1,
    )


def stats_body(sizes, upper, spare, order, lengths, q_ref, *refs):
    peers, half, groups, share, dim, docs = sizes
    if upper:
        w_ref, level_ref, mixed_ref, w, held, kept, places, sems = refs[peers:]
    else:
        held, w_ref, level_ref, mixed_ref, w, kept, places, sems = refs
    copies = fetch_columns(spare, w_ref, w, sems)
    if upper:
        load_blocks(refs[:peers], held)
    me = lax.axis_index("ctx")
    width = groups * dim
    factor = math.log2(math.e) / math.sqrt(dim)
    find_places(order, places, me, 2 * peers)
    columns = share * half
    at = upper_half(order)
    j = at if upper else 1 - at
    span, position, start, lowest = own_span(order, lengths, docs, me, j, half)
    rows = pl.ds(pl.multiple_of(j * half, half), half)
    queries = [stack_heads(q_ref, rows, g, share, dim) for g in range(groups)]

    deep = AT_ONCE * half
    steps = (span - lowest) // AT_ONCE + 1

    def score(i, carry):
        known, block, key = span_group(i, span, held, places, half)
        allowed = (key <= position) & (key >= start)
        fresh = []
        for g in range(groups):
            logits = keep(allowed, mm_nt(block[:, g * dim : (g + 1) * dim], queries[g]), masked_score)
            kept[g, pl.ds(pl.multiple_of(i * deep, deep), deep), :] = logits
            high = jnp.max(logits.reshape(deep // 8, 8, columns), axis=0)
            fresh.append(jnp.maximum(carry[g], high))
        return tuple(fresh)

    empty = jnp.full((8, columns), masked_score, jnp.float32)
    tops = lax.fori_loop(0, steps, score, (empty,) * groups)
    tops = [jnp.max(top, axis=0, keepdims=True) for top in tops]

    def mix(i, carry):
        known, block, key = span_group(i, span, held, places, half)
        fresh = []
        for g in range(groups):
            total, mixed = carry[g]
            values = block[:, width + g * dim : width + (g + 1) * dim]
            logits = kept[g, pl.ds(pl.multiple_of(i * deep, deep), deep), :]
            weights = jnp.exp2((logits - tops[g]) * factor)
            total = total + jnp.sum(weights.reshape(deep // 8, 8, columns), axis=0)
            mixed = mixed + mm_tn(values, weights.astype(jnp.bfloat16))
            fresh.append((total, mixed))
        return tuple(fresh)

    empty = (jnp.zeros((8, columns), jnp.float32), jnp.zeros((dim, columns), jnp.float32))
    done = lax.fori_loop(0, steps, mix, (empty,) * groups)
    for g in range(groups):
        top, (total, mixed) = tops[g], done[g]
        total = jnp.sum(total, axis=0, keepdims=True)
        level_ref[g] = top * factor + jnp.log2(total)
        mixed_ref[g] = mixed / total
    for copy in copies:
        copy.wait()


def stats(upper, q, *args):
    *blocks, w, span_order, doc_lengths, sizes = args
    heads = lax.axis_size("head")
    spare = list(range(heads))[: heads // 2] if upper else list(range(heads))[heads // 2 :]
    peers, half, groups, share, dim, docs = sizes
    columns = share * half
    return pl.pallas_call(
        functools.partial(stats_body, sizes, upper, spare),
        in_specs=[pl.BlockSpec(memory_space=pltpu.SMEM)] * 2
        + [pl.BlockSpec(memory_space=VMEM)] * (1 + len(blocks))
        + [pl.BlockSpec(memory_space=HBM)],
        out_specs=[pl.BlockSpec(memory_space=VMEM)] * (4 if upper else 3),
        out_shape=[
            jax.ShapeDtypeStruct((groups, 1, columns), jnp.float32),
            jax.ShapeDtypeStruct((groups, dim, columns), jnp.float32),
            jax.ShapeDtypeStruct((len(spare), w.shape[0], w.shape[1] // heads), w.dtype),
        ]
        + [jax.ShapeDtypeStruct((2 * peers * half, 2 * groups * dim), jnp.bfloat16)] * upper,
        scratch_shapes=[
            VMEM((groups, (2 * peers + AT_ONCE) * half, columns), jnp.float32),
            pltpu.SMEM((2 * peers,), jnp.int32),
            pltpu.SemaphoreType.DMA((len(spare),)),
        ],
        compiler_params=params(),
        cost_estimate=cost(2.4),
        name="upper_stats" if upper else "lower_stats",
    )(span_order, doc_lengths, q, *blocks, in_hbm(w))


def grads_body(sizes, upper, spare, order, lengths, q_ref, g_ref, level_ref, mixed_ref, *refs):
    peers, half, groups, share, dim, docs = sizes
    spans = 2 * peers
    if upper:
        held, dq_ref, even_ref, *odd_refs, sums, places = refs
    else:
        rest_ref, held, wq_ref, wk_ref, wv_ref, dq_ref, even_ref, *odd_refs, wq, wk, wv, sums, places, sems = refs
        copies = []
        for i, (w_ref, w) in enumerate(((wq_ref, wq), (wk_ref, wk), (wv_ref, wv))):
            copies += fetch_rows(spare, w_ref, w, sems, i)
    me = lax.axis_index("ctx")
    width = groups * dim
    scale = 1.0 / math.sqrt(dim)
    factor = math.log2(math.e) * scale
    find_places(order, places, me, spans)
    columns = share * half
    at = upper_half(order)
    j = at if upper else 1 - at
    span, position, start, lowest = own_span(order, lengths, docs, me, j, half)
    steps = (span - lowest) // AT_ONCE + 1

    def fill(p, carry):
        target = pl.ds(pl.multiple_of(p * half, half), half)
        if upper:
            sums[target, :] = jnp.zeros((half, 2 * width), jnp.float32)
        else:
            sums[target, :] = rest_ref[target, :]
        return carry

    lax.fori_loop(0, jnp.maximum(span - AT_ONCE * steps + 1, 0), fill, 0)
    lax.fori_loop(span + 1, sums.shape[0] // half, fill, 0)
    rows = pl.ds(pl.multiple_of(j * half, half), half)
    queries = [stack_heads(q_ref, rows, g, share, dim) for g in range(groups)]
    outs = [stack_heads(g_ref, rows, g, share, dim) for g in range(groups)]
    levels = [level_ref[g] for g in range(groups)]
    deltas = []
    for g in range(groups):
        turned = jnp.concatenate(
            [outs[g][h * half : (h + 1) * half].astype(jnp.float32).T for h in range(share)],
            axis=1,
        )
        deltas.append(jnp.sum(turned * mixed_ref[g], axis=0, keepdims=True))

    def visit(i, carry):
        known, block, key = span_group(i, span, held, places, half)
        allowed = (key <= position) & (key >= start)
        targets = [pl.ds(pl.multiple_of(p * half, half), half) for p in known]
        fresh = []
        for g in range(groups):
            keys = block[:, g * dim : (g + 1) * dim]
            values = block[:, width + g * dim : width + (g + 1) * dim]
            logits = mm_nt(keys, queries[g]) * factor
            chance = keep(allowed, jnp.exp2(logits - levels[g]), 0.0)
            slopes = mm_nt(values, outs[g])
            score = (chance * (slopes - deltas[g])).astype(jnp.bfloat16)
            key_term = mm(score, queries[g])
            value_term = mm(chance.astype(jnp.bfloat16), outs[g])
            for j, target in enumerate(targets):
                part = slice(j * half, (j + 1) * half)
                for at, term in ((g * dim, key_term[part]), (width + g * dim, value_term[part])):
                    columns_at = slice(at, at + dim)
                    if not upper:
                        term = term + rest_ref[target, columns_at]
                    sums[target, columns_at] = term
            fresh.append(carry[g] + mm_tn(keys, score))
        return tuple(fresh)

    empty = jnp.zeros((dim, columns), jnp.float32)
    done = lax.fori_loop(0, steps, visit, (empty,) * groups)
    for g in range(groups):
        for h in range(share):
            head = g * share + h
            dq_ref[:, head * dim : (head + 1) * dim] = (
                (done[g][:, h * half : (h + 1) * half].T * scale).astype(dq_ref.dtype)
            )
    for k in range(peers):
        out, slot = even_ref, k // 2
        if k % 2:
            out, slot = odd_refs[slot // odd_refs[0].shape[0]], slot % odd_refs[0].shape[0]
        first = order[2 * (me ^ k)]
        other = spans - 1 - first
        pick = jnp.maximum(first, other) if upper else jnp.minimum(first, other)
        part = pl.ds(pl.multiple_of(pick * half, half), half)
        out[slot, :, :width] = (sums[part, :width] * scale).astype(out.dtype)
        out[slot, :, width:] = sums[part, width:].astype(out.dtype)
    if not upper:
        for copy in copies:
            copy.wait()


def grads(upper, q, g, level, mixed, *args):
    *blocks, span_order, doc_lengths, sizes = args
    weights, spare, scratch = [], [], []
    if not upper:
        heads = lax.axis_size("head")
        spare = list(range(heads - 1, 0, -2))
        weights, blocks = [in_hbm(w) for w in blocks[-3:]], blocks[:-3]
        scratch = [pltpu.SemaphoreType.DMA((len(spare), 3))]
    peers, half, groups, share, dim, docs = sizes
    tokens, width = 2 * half, groups * dim
    columns = share * half
    terms = jax.ShapeDtypeStruct((peers // 2, half, 2 * width), jnp.bfloat16)
    odds = jax.ShapeDtypeStruct((peers // 4, half, 2 * width), jnp.bfloat16)
    rests = jax.ShapeDtypeStruct((peers * tokens, 2 * width), jnp.float32)
    outs = [jax.ShapeDtypeStruct((half, g.shape[1]), jnp.bfloat16), terms, odds, odds] + [rests] * upper
    outs += [rows_shape(spare, w, heads) for w in weights]
    return pl.pallas_call(
        functools.partial(grads_body, sizes, upper, spare),
        in_specs=[pl.BlockSpec(memory_space=pltpu.SMEM)] * 2
        + [pl.BlockSpec(memory_space=VMEM)] * (4 + len(blocks))
        + [pl.BlockSpec(memory_space=HBM)] * len(weights),
        out_specs=[pl.BlockSpec(memory_space=VMEM)] * len(outs),
        out_shape=outs,
        scratch_shapes=[VMEM((peers * half, 2 * width), jnp.float32)] * (not upper)
        + [
            pltpu.SMEM((2 * peers,), jnp.int32),
        ]
        + scratch,
        compiler_params=params(),
        cost_estimate=cost(3.0),
        name="upper_grads" if upper else "lower_grads",
    )(span_order, doc_lengths, q, g, level, mixed, *blocks, *weights)


def swap(x, k, axis):
    return lax.ppermute(x, axis, [(i, i ^ k) for i in range(lax.axis_size(axis))])


def gather_even(x, axis, held):
    size = lax.axis_size(axis)
    got, bit = {0: x}, 2
    while bit < size:
        passed = {k: block for k, block in got.items() if k}
        passed, held = lax.optimization_barrier((passed, held))
        got |= {bit: swap(x, bit, axis)}
        got |= {k ^ bit: swap(block, bit, axis) for k, block in passed.items()}
        bit *= 2
    return [got[k] for k in sorted(got)], held


def pair_body(even_ref, *refs):
    count = even_ref.shape[0]
    odd_refs, outs = refs[:-count], refs[-count:]
    part = odd_refs[0].shape[0]
    for k, out in enumerate(outs):
        total = even_ref[k].astype(jnp.float32) + odd_refs[k // part][k % part].astype(jnp.float32)
        out[...] = total.astype(out.dtype)


def pair_sums(even, *got):
    count, rows, width = even.shape
    return pl.pallas_call(
        pair_body,
        in_specs=[pl.BlockSpec(memory_space=VMEM)] * (1 + len(got)),
        out_specs=[pl.BlockSpec(memory_space=VMEM)] * count,
        out_shape=[jax.ShapeDtypeStruct((rows, width), jnp.bfloat16)] * count,
        compiler_params=params(),
        cost_estimate=cost(0.7),
        name="pair_sums",
    )(even, *got)


def scatter_ctx(pairs):
    return [part if k == 0 else swap(part, 2 * k, "ctx") for k, part in enumerate(pairs)]


def shards(inputs, out_grad, w_query, w_key, value_projection, w_out, doc_lengths, span_order):
    tokens = inputs.shape[0]
    share = ASKER_NUM // SHARED_KV_NUM
    half = tokens // 2
    sizes = (
        lax.axis_size("ctx"),
        tokens // 2,
        w_key.shape[1] // CHANNEL_DIM,
        share,
        CHANNEL_DIM,
        doc_lengths.shape[0],
    )
    heads = lax.axis_size("head")
    last = [span_order]

    def turn(call, *args):
        held, *args = lax.optimization_barrier((last[0], *args))
        out = call(*args)
        last[0] = out if hasattr(out, "shape") else out[0]
        return out

    def attend(upper, call, *args):
        return turn(lambda *a: call(upper, *a, span_order, doc_lengths, sizes), *args)

    def context(blocks, stacks, spans, total, dtype):
        shape = jax.tree.structure((blocks, stacks, total))

        def call(*flat):
            parts, weights, given = jax.tree.unflatten(shape, flat)
            return back_project(parts, weights, spans, given, dtype)

        return turn(call, *jax.tree.leaves((blocks, stacks, total)))

    def send_first(parts, stack, places=None):
        if stack is None:
            return {k ^ 1: (swap(parts[k], 1, "head"), None) for k in places} | {0: None}
        places = range(heads - 1, 0, -2)
        got = swap(stack, 1, "head")
        return {k ^ 1: (got, i) for i, k in enumerate(places)}

    def send_rest(parts, got):
        ends, bit = [(parts[0], None), got[0]], 2
        parts = {
            k: turn(lambda a, b, at=got[k][1]: add(a, b, at), parts[k], got[k][0])
            for k in range(2, heads, 2)
        }
        while bit < heads:
            moved = {k ^ bit: swap(parts[k], bit, "head") for k in parts if k & bit}
            ends.append((moved.pop(0), None))
            parts = {k: turn(lambda a, b: add(a, b, None), parts[k], moved[k]) for k in moved}
            bit *= 2
        return ends

    far = [{0: out_grad[:half]}, {0: out_grad[half:]}]
    bit = heads // 2
    while bit > 1:
        far = [got | {k ^ bit: swap(x, bit, "head") for k, x in got.items()} for got in far]
        bit //= 2
    near = [swap(out_grad[:half], 1, "head"), swap(out_grad[half:], 1, "head")]
    own = turn(project_kv, inputs, w_key, value_projection)
    near_blocks, (far[0], near[0]) = gather_even(own, "ctx", (far[0], near[0]))
    query = turn(project, inputs, w_query)
    query, near_blocks = lax.optimization_barrier((query, near_blocks))
    blocks = (*near_blocks, *[swap(block, 1, "ctx") for block in near_blocks])
    query, far[1], near[1] = lax.optimization_barrier((query, far[1], near[1]))
    *upper_stats, w_first, held = attend(True, stats, query, *blocks, w_out)
    *lower_stats, w_second = attend(False, stats, query, held, w_out)
    passed = [{k ^ 1: swap(x, 1, "head") for k, x in got.items() if k} for got in far]
    come = {0: (out_grad,), 1: tuple(near)}
    come |= {k: (far[0][k], far[1][k]) for k in range(2, heads, 2)}
    come |= {k: (passed[0][k], passed[1][k]) for k in range(3, heads, 2)}
    blocks = [come[k] for k in range(heads)]
    mid = heads // 2
    total = context(
        blocks[:-1], (w_first, w_second), [(0, mid), (0, mid - 1)], None, jnp.float32
    )
    context_grad = context(blocks[-1:], (w_second,), [(mid - 1, mid)], total, jnp.bfloat16)
    upper_dq, even, *odd, rest = attend(True, grads, query, context_grad, *upper_stats, held)
    upper = scatter_ctx(turn(pair_sums, even, *[swap(x, 1, "ctx") for x in odd]))
    weights = (w_query, w_key, value_projection)
    lower_dq, even, *odd, wq, wk, wv = attend(
        False, grads, query, context_grad, *lower_stats, rest, held, *weights
    )
    sides = [list(range(heads - 1, 0, -2)), list(range(heads - 2, -1, -2))]
    weights = [(wq, wk, wv), weights]

    def firsts_of(side):
        return turn(
            lambda a, b, w: query_terms(a, b, w, heads, sides[side]),
            upper_dq,
            lower_dq,
            weights[side][0],
        )

    def terms_of(first, terms, side, stacked=False):
        outs = turn(
            lambda a, k, v, *b: all_terms(a, b, k, v, heads, sides[side], stacked),
            first,
            *weights[side][1:],
            *terms,
        )
        return outs[0] if stacked else dict(zip(sides[side], outs))

    first = [firsts_of(0)]
    lower_odd = [swap(x, 1, "ctx") for x in odd]
    upper_got = send_first(None, terms_of(first[0][0], upper, 0, True))
    lower = scatter_ctx(turn(pair_sums, even, *lower_odd))
    first.append(firsts_of(1))
    upper = terms_of(first[1][0], upper, 1)
    parts = terms_of(first[0][1], lower, 0)
    lower_got = send_first(parts, None, sides[0][:-1])
    upper = send_rest(upper, upper_got)
    lower = terms_of(first[1][1], lower, 1)
    lower = send_rest(lower, lower_got)
    stack, at = upper[1]
    upper = [(turn(lambda a, b: merge(a, b, at), upper[0][0], stack), None)] + upper[2:]
    last_part, held = lax.optimization_barrier((parts[1], last[0]))
    last_part = (swap(last_part, 1, "head"), None)
    total = upper[0][0]
    for block, at in upper[1:]:
        total = turn(lambda a, b: merge(a, b, None), total, block)
    upper = [(total, None)]
    total = lower[0][0]
    for block, at in lower[2:]:
        total = turn(lambda a, b: merge(a, b, None), total, block)
    lower = [(total, None), last_part]
    return join_rows(upper, lower, span_order)


def solution(mesh):
    in_specs = (
        P("ctx", None),
        P("ctx", "head"),
        P(None, "head"),
        P(None, "head"),
        P(None, "head"),
        P("head", None),
        P(),
        P(),
    )
    out_specs = P("ctx", "head")
    return jax.shard_map(shards, mesh=mesh, in_specs=in_specs, out_specs=out_specs, check_vma=False)
```

```python
import functools
import math

import jax
import jax.numpy as jnp
from jax import lax
from jax.experimental import pallas as pl
from jax.experimental.pallas import tpu as pltpu
from jax.sharding import PartitionSpec as P

ASKER_NUM = 32
SHARED_KV_NUM = 8
CHANNEL_DIM = 128

masked_score = -1e30
MIB = 1 << 20
COST = 0
AT_ONCE = 4
PARTS = 2
VMEM = pltpu.VMEM
HBM = pltpu.HBM


def mm(a, b):
    return lax.dot_general(a, b, (((1,), (0,)), ((), ())), preferred_element_type=jnp.float32)


def mm_nt(a, b):
    return lax.dot_general(a, b, (((1,), (1,)), ((), ())), preferred_element_type=jnp.float32)


def mm_tn(a, b):
    return lax.dot_general(a, b, (((0,), (0,)), ((), ())), preferred_element_type=jnp.float32)


def params():
    return pltpu.CompilerParams(vmem_limit_bytes=24 * MIB)


def cost(micros):
    return pl.CostEstimate(flops=int(micros * COST), bytes_accessed=1, transcendentals=0)


def upper_half(order):
    first = order[2 * lax.axis_index("ctx")]
    return jnp.where(2 * first >= order.shape[0], 0, 1)


def in_hbm(x):
    return pltpu.with_memory_space_constraint(x, HBM)


def fetch(src, dst, sem):
    copy = pltpu.make_async_copy(src, dst, sem)
    copy.start()
    return copy


def kv_body(parts, x_ref, wk_ref, wv_ref, out_ref, x, wk, wv, acc, sems):
    width = wk.shape[1]
    depth = wk.shape[0] // parts
    copies = []
    for i in range(parts):
        rows = slice(i * depth, (i + 1) * depth)
        copies.append(
            [
                fetch(x_ref.at[:, rows], x.at[:, rows], sems.at[i, 0]),
                fetch(wk_ref.at[rows], wk.at[rows], sems.at[i, 1]),
                fetch(wv_ref.at[rows], wv.at[rows], sems.at[i, 2]),
            ]
        )
    for i in range(parts):
        rows = slice(i * depth, (i + 1) * depth)
        for copy in copies[i]:
            copy.wait()
        left = x[:, rows]
        terms = mm(left, wk[rows, :]), mm(left, wv[rows, :])
        for j, term in enumerate(terms):
            columns = slice(j * width, (j + 1) * width)
            total = term if i == 0 else acc[:, columns] + term
            if i < parts - 1:
                acc[:, columns] = total
            else:
                out_ref[:, columns] = total.astype(out_ref.dtype)


def project_kv(x, wk, wv):
    tokens, depth = x.shape
    width = wk.shape[1]
    parts = 4
    return pl.pallas_call(
        functools.partial(kv_body, parts),
        in_specs=[pl.BlockSpec(memory_space=HBM)] * 3,
        out_specs=pl.BlockSpec(memory_space=VMEM),
        out_shape=jax.ShapeDtypeStruct((tokens, 2 * width), jnp.bfloat16),
        scratch_shapes=[
            VMEM(x.shape, x.dtype),
            VMEM(wk.shape, wk.dtype),
            VMEM(wv.shape, wv.dtype),
            VMEM((tokens, 2 * width), jnp.float32),
            pltpu.SemaphoreType.DMA((parts, 3)),
        ],
        compiler_params=params(),
        cost_estimate=cost(3.4),
        name="project_kv",
    )(in_hbm(x), in_hbm(wk), in_hbm(wv))


def project_body(parts, x_ref, w_ref, out_ref, x, w, acc, sems):
    depth = w.shape[0] // parts
    copies = []
    for i in range(parts):
        rows = slice(i * depth, (i + 1) * depth)
        copies.append(
            [
                fetch(x_ref.at[:, rows], x.at[:, rows], sems.at[i, 0]),
                fetch(w_ref.at[rows], w.at[rows], sems.at[i, 1]),
            ]
        )
    for i in range(parts):
        rows = slice(i * depth, (i + 1) * depth)
        for copy in copies[i]:
            copy.wait()
        total = mm(x[:, rows], w[rows, :])
        if i:
            total = acc[...] + total
        if i < parts - 1:
            acc[...] = total
        else:
            out_ref[...] = total.astype(out_ref.dtype)


def project(x, w):
    tokens, depth = x.shape
    width = w.shape[1]
    parts = 4
    return pl.pallas_call(
        functools.partial(project_body, parts),
        in_specs=[pl.BlockSpec(memory_space=HBM)] * 2,
        out_specs=pl.BlockSpec(memory_space=VMEM),
        out_shape=jax.ShapeDtypeStruct((tokens, width), jnp.bfloat16),
        scratch_shapes=[
            VMEM(x.shape, x.dtype),
            VMEM(w.shape, w.dtype),
            VMEM((tokens, width), jnp.float32),
            pltpu.SemaphoreType.DMA((parts, 2)),
        ],
        compiler_params=params(),
        cost_estimate=cost(4.9),
        name="project",
    )(in_hbm(x), in_hbm(w))


def back_body(given, rows, spans, *refs):
    refs, out_ref = list(refs[:-1]), refs[-1]
    total = refs.pop(0)[...] if given else None
    stacks = [refs.pop() for _ in spans][::-1]
    for w, (low, high) in zip(stacks, spans):
        for i in range(low, high):
            x = refs.pop(0)[...]
            if x.shape[0] < rows:
                x = jnp.concatenate([x, refs.pop(0)[...]], axis=0)
            term = mm_nt(x, w[i])
            total = term if total is None else total + term
    out_ref[...] = total.astype(out_ref.dtype)


def back_project(blocks, stacks, spans, total, dtype):
    rows = blocks[0][0].shape[0] * len(blocks[0])
    given = [] if total is None else [total]
    flat = [x for block in blocks for x in block]
    operands = (*given, *flat, *stacks)
    return pl.pallas_call(
        functools.partial(back_body, len(given), rows, spans),
        in_specs=[pl.BlockSpec(memory_space=VMEM)] * len(operands),
        out_specs=pl.BlockSpec(memory_space=VMEM),
        out_shape=jax.ShapeDtypeStruct((rows, stacks[0].shape[1]), dtype),
        compiler_params=params(),
        cost_estimate=cost(3),
        name="context_grad",
    )(*operands)


def fetch_columns(places, ref, out, sems):
    me = lax.axis_index("head")
    depth = out.shape[2]
    return [
        fetch(ref.at[:, pl.ds(pl.multiple_of((me ^ k) * depth, depth), depth)], out.at[i], sems.at[i])
        for i, k in enumerate(places)
    ]


def fetch_rows(places, ref, out, sems, at):
    me = lax.axis_index("head")
    share = out.shape[1]
    return [
        fetch(ref.at[pl.ds(pl.multiple_of((me ^ k) * share, share), share)], out.at[i], sems.at[i, at])
        for i, k in enumerate(places)
    ]


def rows_shape(places, w, heads):
    return jax.ShapeDtypeStruct((len(places), w.shape[0] // heads, w.shape[1]), w.dtype)


def query_terms_body(places, upper_ref, lower_ref, w_ref, *refs):
    upper_out, lower_out = refs[:2]
    copies, w = [], w_ref
    if places is not None:
        w, sems = refs[2:]
        copies = fetch_rows(places, w_ref, w, sems, 0)
    half = upper_ref.shape[0]
    x = jnp.concatenate([upper_ref[...], lower_ref[...]], axis=0)
    for i in range(w.shape[0]):
        if copies:
            copies[i].wait()
        total = mm_nt(x, w[i])
        upper_out[i] = total[:half]
        lower_out[i] = total[half:]


def query_terms(upper, lower, w, heads, places):
    rows, depth = upper.shape
    scratch = []
    shape = w
    if w.ndim == 2:
        shape = rows_shape(places, w, heads)
        scratch = [VMEM(shape.shape, w.dtype), pltpu.SemaphoreType.DMA((len(places), 1))]
        w = in_hbm(w)
    else:
        places = None
    size, share = shape.shape[:2]
    return pl.pallas_call(
        functools.partial(query_terms_body, places),
        in_specs=[pl.BlockSpec(memory_space=VMEM)] * 2
        + [pl.BlockSpec(memory_space=HBM if scratch else VMEM)],
        out_specs=[pl.BlockSpec(memory_space=VMEM)] * 2,
        out_shape=[jax.ShapeDtypeStruct((size, rows, share), jnp.float32)] * 2,
        scratch_shapes=scratch,
        compiler_params=params(),
        cost_estimate=cost(3),
        name="query_terms",
    )(upper, lower, w)


def all_terms_body(places, count, first_ref, *refs):
    terms, (wk_ref, wv_ref), refs = refs[:count], refs[count : count + 2], refs[count + 2 :]
    wk, wv, copies = wk_ref, wv_ref, []
    if places is not None:
        refs, (wk, wv, sems) = refs[:-3], refs[-3:]
        copies = [fetch_rows(places, wk_ref, wk, sems, 0), fetch_rows(places, wv_ref, wv, sems, 1)]
    outs = refs
    width = wk.shape[2]
    grads = terms[0][...].astype(jnp.float32)
    for term in terms[1:]:
        grads = grads + term[...].astype(jnp.float32)
    grads = grads.astype(jnp.bfloat16)
    for i in range(wk.shape[0]):
        for some in copies:
            some[i].wait()
        total = first_ref[i] + mm_nt(grads[:, :width], wk[i])
        total = total + mm_nt(grads[:, width:], wv[i])
        if len(outs) == 1:
            outs[0][i] = total.astype(outs[0].dtype)
        else:
            outs[i][...] = total.astype(outs[i].dtype)


def all_terms(first, terms, wk, wv, heads, places, stacked):
    size, rows, share = first.shape
    scratch = []
    if wk.ndim == 2:
        shape = rows_shape(places, wk, heads).shape
        scratch = [
            VMEM(shape, wk.dtype),
            VMEM(shape, wv.dtype),
            pltpu.SemaphoreType.DMA((size, 2)),
        ]
        wk, wv = in_hbm(wk), in_hbm(wv)
    else:
        places = None
    return pl.pallas_call(
        functools.partial(all_terms_body, places, len(terms)),
        in_specs=[pl.BlockSpec(memory_space=VMEM)] * (1 + len(terms))
        + [pl.BlockSpec(memory_space=HBM if scratch else VMEM)] * 2,
        out_specs=[pl.BlockSpec(memory_space=VMEM)] * (1 if stacked else size),
        out_shape=[jax.ShapeDtypeStruct((size, rows, share), jnp.bfloat16)]
        if stacked
        else [jax.ShapeDtypeStruct((rows, share), jnp.bfloat16)] * size,
        scratch_shapes=scratch,
        compiler_params=params(),
        cost_estimate=cost(2),
        name="all_terms",
    )(first, *terms, wk, wv)


def part_of(ref, at):
    return (ref[...] if at is None else ref[at]).astype(jnp.float32)


def add_body(at, a_ref, b_ref, out_ref):
    out_ref[...] = (a_ref[...].astype(jnp.float32) + part_of(b_ref, at)).astype(out_ref.dtype)


def add(a, b, at):
    return pl.pallas_call(
        functools.partial(add_body, at),
        in_specs=[pl.BlockSpec(memory_space=VMEM)] * 2,
        out_specs=pl.BlockSpec(memory_space=VMEM),
        out_shape=jax.ShapeDtypeStruct(a.shape, a.dtype),
        compiler_params=params(),
        cost_estimate=cost(0.5),
        name="add",
    )(a, b)


def merge_body(at, a_ref, b_ref, out_ref):
    out_ref[...] = a_ref[...].astype(jnp.float32) + part_of(b_ref, at)


def merge(a, b, at):
    return pl.pallas_call(
        functools.partial(merge_body, at),
        in_specs=[pl.BlockSpec(memory_space=VMEM)] * 2,
        out_specs=pl.BlockSpec(memory_space=VMEM),
        out_shape=jax.ShapeDtypeStruct(a.shape, jnp.float32),
        compiler_params=params(),
        cost_estimate=cost(0.5),
        name="merge",
    )(a, b)


def join_body(ats, order, *refs):
    refs, out_ref = list(refs[:-1]), refs[-1]
    half = out_ref.shape[0] // 2
    at = upper_half(order) * half
    for j, place in enumerate((at, half - at)):
        total = None
        for i in ats[j]:
            term = part_of(refs.pop(0), i)
            total = term if total is None else total + term
        out_ref[pl.ds(pl.multiple_of(place, half), half), :] = total.astype(out_ref.dtype)


def join_rows(upper, lower, span_order):
    rows, width = upper[0][0].shape
    ats = [[at for _, at in terms] for terms in (upper, lower)]
    blocks = [block for block, _ in upper + lower]
    return pl.pallas_call(
        functools.partial(join_body, ats),
        in_specs=[pl.BlockSpec(memory_space=pltpu.SMEM)]
        + [pl.BlockSpec(memory_space=VMEM)] * len(blocks),
        out_specs=pl.BlockSpec(memory_space=VMEM),
        out_shape=jax.ShapeDtypeStruct((2 * rows, width), jnp.bfloat16),
        compiler_params=params(),
        cost_estimate=cost(1.5),
        name="join_rows",
    )(span_order, *blocks)


def find_places(order, places, me, spans):
    for i in range(spans):
        k = (i // 2) ^ me
        places[order[i]] = (k % 2) * (spans // 2) + (k // 2) * 2 + (i % 2)


def own_span(order, lengths, docs, me, j, half):
    span = order[2 * me + j]
    position = span * half + lax.broadcasted_iota(jnp.int32, (1, half), 1)
    first, end = 0, 0
    start = jnp.zeros((1, half), jnp.int32)
    for k in range(docs):
        end = end + lengths[k]
        start = jnp.where(position >= end, end, start)
        first = jnp.where(span * half >= end, end, first)
    return span, position, start, first // half


def stack_heads(ref, rows, group, share, dim):
    base = group * share
    return jnp.concatenate(
        [ref[rows, (base + h) * dim : (base + h + 1) * dim] for h in range(share)], axis=0
    )


def load_blocks(refs, held):
    rows = refs[0].shape[0]
    for k, ref in enumerate(refs):
        held[k * rows : (k + 1) * rows, :] = ref[...]


def span_group(i, span, held, places, half, count):
    numbers = [span - count * i - j for j in range(count - 1, -1, -1)]
    known = [jnp.maximum(p, 0) for p in numbers]
    at = [pl.multiple_of(places[p] * half, half) for p in known]
    block = jnp.concatenate([held[pl.ds(place, half), :] for place in at], axis=0)
    key = numbers[0] * half + lax.broadcasted_iota(jnp.int32, (count * half, 1), 0)
    return known, block, key


def keep(allowed, x, other):
    width = allowed.shape[1]
    return jnp.concatenate(
        [
            jnp.where(allowed, x[:, i : i + width], other)
            for i in range(0, x.shape[1], width)
        ],
        axis=1,
    )


def stats_body(sizes, upper, spare, order, lengths, q_ref, *refs):
    peers, half, groups, share, dim, docs = sizes
    if upper:
        w_ref, level_ref, mixed_ref, w, held, kept, places, sems = refs[peers:]
    else:
        held, w_ref, level_ref, mixed_ref, w, kept, places, sems = refs
    copies = fetch_columns(spare, w_ref, w, sems)
    if upper:
        load_blocks(refs[:peers], held)
    me = lax.axis_index("ctx")
    width = groups * dim
    factor = math.log2(math.e) / math.sqrt(dim)
    find_places(order, places, me, 2 * peers)
    columns = share * half
    at = upper_half(order)
    j = at if upper else 1 - at
    span, position, start, lowest = own_span(order, lengths, docs, me, j, half)
    rows = pl.ds(pl.multiple_of(j * half, half), half)
    queries = [stack_heads(q_ref, rows, g, share, dim) for g in range(groups)]

    deep = AT_ONCE * half
    steps = (span - lowest) // AT_ONCE + 1

    def score(i, carry):
        known, block, key = span_group(i, span, held, places, half, AT_ONCE)
        allowed = (key <= position) & (key >= start)
        fresh = []
        for g in range(groups):
            logits = keep(allowed, mm_nt(block[:, g * dim : (g + 1) * dim], queries[g]), masked_score)
            kept[g, pl.ds(pl.multiple_of(i * deep, deep), deep), :] = logits
            high = jnp.max(logits.reshape(deep // 8, 8, columns), axis=0)
            fresh.append(jnp.maximum(carry[g], high))
        return tuple(fresh)

    empty = jnp.full((8, columns), masked_score, jnp.float32)
    tops = lax.fori_loop(0, steps, score, (empty,) * groups)
    tops = [jnp.max(top, axis=0, keepdims=True) for top in tops]

    def mix(i, carry):
        known, block, key = span_group(i, span, held, places, half, AT_ONCE)
        fresh = []
        for g in range(groups):
            total, mixed = carry[g]
            values = block[:, width + g * dim : width + (g + 1) * dim]
            logits = kept[g, pl.ds(pl.multiple_of(i * deep, deep), deep), :]
            weights = jnp.exp2((logits - tops[g]) * factor)
            total = total + jnp.sum(weights.reshape(deep // 8, 8, columns), axis=0)
            mixed = mixed + mm_tn(values, weights.astype(jnp.bfloat16))
            fresh.append((total, mixed))
        return tuple(fresh)

    empty = (jnp.zeros((8, columns), jnp.float32), jnp.zeros((dim, columns), jnp.float32))
    done = lax.fori_loop(0, steps, mix, (empty,) * groups)
    for g in range(groups):
        top, (total, mixed) = tops[g], done[g]
        total = jnp.sum(total, axis=0, keepdims=True)
        level_ref[g] = top * factor + jnp.log2(total)
        mixed_ref[g] = mixed / total
    for copy in copies:
        copy.wait()


def stats(upper, q, *args):
    *blocks, w, span_order, doc_lengths, sizes = args
    heads = lax.axis_size("head")
    spare = list(range(heads))[: heads // 2] if upper else list(range(heads))[heads // 2 :]
    peers, half, groups, share, dim, docs = sizes
    columns = share * half
    return pl.pallas_call(
        functools.partial(stats_body, sizes, upper, spare),
        in_specs=[pl.BlockSpec(memory_space=pltpu.SMEM)] * 2
        + [pl.BlockSpec(memory_space=VMEM)] * (1 + len(blocks))
        + [pl.BlockSpec(memory_space=HBM)],
        out_specs=[pl.BlockSpec(memory_space=VMEM)] * (4 if upper else 3),
        out_shape=[
            jax.ShapeDtypeStruct((groups, 1, columns), jnp.float32),
            jax.ShapeDtypeStruct((groups, dim, columns), jnp.float32),
            jax.ShapeDtypeStruct((len(spare), w.shape[0], w.shape[1] // heads), w.dtype),
        ]
        + [jax.ShapeDtypeStruct((2 * peers * half, 2 * groups * dim), jnp.bfloat16)] * upper,
        scratch_shapes=[
            VMEM((groups, (2 * peers + AT_ONCE) * half, columns), jnp.float32),
            pltpu.SMEM((2 * peers,), jnp.int32),
            pltpu.SemaphoreType.DMA((len(spare),)),
        ],
        compiler_params=params(),
        cost_estimate=cost(2.4),
        name="upper_stats" if upper else "lower_stats",
    )(span_order, doc_lengths, q, *blocks, in_hbm(w))


def grads_body(sizes, upper, spare, order, lengths, q_ref, g_ref, level_ref, mixed_ref, *refs):
    peers, half, groups, share, dim, docs = sizes
    spans = 2 * peers
    count = 3 if upper else AT_ONCE
    if upper:
        held, dq_ref, even_ref, *odd_refs, sums, places = refs
    else:
        rest_ref, held, wq_ref, wk_ref, wv_ref, dq_ref, even_ref, *odd_refs, wq, wk, wv, sums, places, sems = refs
        copies = []
        for i, (w_ref, w) in enumerate(((wq_ref, wq), (wk_ref, wk), (wv_ref, wv))):
            copies += fetch_rows(spare, w_ref, w, sems, i)
    me = lax.axis_index("ctx")
    width = groups * dim
    scale = 1.0 / math.sqrt(dim)
    factor = math.log2(math.e) * scale
    find_places(order, places, me, spans)
    columns = share * half
    at = upper_half(order)
    j = at if upper else 1 - at
    span, position, start, lowest = own_span(order, lengths, docs, me, j, half)
    steps = (span - lowest) // count + 1

    def fill(p, carry):
        target = pl.ds(pl.multiple_of(p * half, half), half)
        if upper:
            sums[target, :] = jnp.zeros((half, 2 * width), jnp.float32)
        else:
            sums[target, :] = rest_ref[target, :]
        return carry

    lax.fori_loop(0, jnp.maximum(span - count * steps + 1, 0), fill, 0)
    lax.fori_loop(span + 1, sums.shape[0] // half, fill, 0)
    rows = pl.ds(pl.multiple_of(j * half, half), half)
    queries = [stack_heads(q_ref, rows, g, share, dim) for g in range(groups)]
    outs = [stack_heads(g_ref, rows, g, share, dim) for g in range(groups)]
    levels = [level_ref[g] for g in range(groups)]
    deltas = []
    for g in range(groups):
        turned = jnp.concatenate(
            [outs[g][h * half : (h + 1) * half].astype(jnp.float32).T for h in range(share)],
            axis=1,
        )
        deltas.append(jnp.sum(turned * mixed_ref[g], axis=0, keepdims=True))

    def visit(i, carry):
        known, block, key = span_group(i, span, held, places, half, count)
        allowed = (key <= position) & (key >= start)
        targets = [pl.ds(pl.multiple_of(p * half, half), half) for p in known]
        fresh = []
        for g in range(groups):
            keys = block[:, g * dim : (g + 1) * dim]
            values = block[:, width + g * dim : width + (g + 1) * dim]
            logits = mm_nt(keys, queries[g]) * factor
            chance = keep(allowed, jnp.exp2(logits - levels[g]), 0.0)
            slopes = mm_nt(values, outs[g])
            score = (chance * (slopes - deltas[g])).astype(jnp.bfloat16)
            key_term = mm(score, queries[g])
            value_term = mm(chance.astype(jnp.bfloat16), outs[g])
            for j, target in enumerate(targets):
                part = slice(j * half, (j + 1) * half)
                for at, term in ((g * dim, key_term[part]), (width + g * dim, value_term[part])):
                    columns_at = slice(at, at + dim)
                    if not upper:
                        term = term + rest_ref[target, columns_at]
                    sums[target, columns_at] = term
            fresh.append(carry[g] + mm_tn(keys, score))
        return tuple(fresh)

    empty = jnp.zeros((dim, columns), jnp.float32)
    done = lax.fori_loop(0, steps, visit, (empty,) * groups)
    for g in range(groups):
        for h in range(share):
            head = g * share + h
            dq_ref[:, head * dim : (head + 1) * dim] = (
                (done[g][:, h * half : (h + 1) * half].T * scale).astype(dq_ref.dtype)
            )
    for k in range(peers):
        out, slot = even_ref, k // 2
        if k % 2:
            out, slot = odd_refs[slot // odd_refs[0].shape[0]], slot % odd_refs[0].shape[0]
        first = order[2 * (me ^ k)]
        other = spans - 1 - first
        pick = jnp.maximum(first, other) if upper else jnp.minimum(first, other)
        part = pl.ds(pl.multiple_of(pick * half, half), half)
        out[slot, :, :width] = (sums[part, :width] * scale).astype(out.dtype)
        out[slot, :, width:] = sums[part, width:].astype(out.dtype)
    if not upper:
        for copy in copies:
            copy.wait()


def grads(upper, q, g, level, mixed, *args):
    *blocks, span_order, doc_lengths, sizes = args
    weights, spare, scratch = [], [], []
    if not upper:
        heads = lax.axis_size("head")
        spare = list(range(heads - 1, 0, -2))
        weights, blocks = [in_hbm(w) for w in blocks[-3:]], blocks[:-3]
        scratch = [pltpu.SemaphoreType.DMA((len(spare), 3))]
    peers, half, groups, share, dim, docs = sizes
    tokens, width = 2 * half, groups * dim
    columns = share * half
    terms = jax.ShapeDtypeStruct((peers // 2, half, 2 * width), jnp.bfloat16)
    odds = jax.ShapeDtypeStruct((peers // 4, half, 2 * width), jnp.bfloat16)
    rests = jax.ShapeDtypeStruct((peers * tokens, 2 * width), jnp.float32)
    outs = [jax.ShapeDtypeStruct((half, g.shape[1]), jnp.bfloat16), terms, odds, odds] + [rests] * upper
    outs += [rows_shape(spare, w, heads) for w in weights]
    return pl.pallas_call(
        functools.partial(grads_body, sizes, upper, spare),
        in_specs=[pl.BlockSpec(memory_space=pltpu.SMEM)] * 2
        + [pl.BlockSpec(memory_space=VMEM)] * (4 + len(blocks))
        + [pl.BlockSpec(memory_space=HBM)] * len(weights),
        out_specs=[pl.BlockSpec(memory_space=VMEM)] * len(outs),
        out_shape=outs,
        scratch_shapes=[VMEM((peers * half, 2 * width), jnp.float32)] * (not upper)
        + [
            pltpu.SMEM((2 * peers,), jnp.int32),
        ]
        + scratch,
        compiler_params=params(),
        cost_estimate=cost(3.0),
        name="upper_grads" if upper else "lower_grads",
    )(span_order, doc_lengths, q, g, level, mixed, *blocks, *weights)


def swap(x, k, axis):
    return lax.ppermute(x, axis, [(i, i ^ k) for i in range(lax.axis_size(axis))])


def gather_even(x, axis, held):
    size = lax.axis_size(axis)
    got, bit = {0: x}, 2
    while bit < size:
        passed = {k: block for k, block in got.items() if k}
        passed, held = lax.optimization_barrier((passed, held))
        got |= {bit: swap(x, bit, axis)}
        got |= {k ^ bit: swap(block, bit, axis) for k, block in passed.items()}
        bit *= 2
    return [got[k] for k in sorted(got)], held


def pair_body(even_ref, *refs):
    count = even_ref.shape[0]
    odd_refs, outs = refs[:-count], refs[-count:]
    part = odd_refs[0].shape[0]
    for k, out in enumerate(outs):
        total = even_ref[k].astype(jnp.float32) + odd_refs[k // part][k % part].astype(jnp.float32)
        out[...] = total.astype(out.dtype)


def pair_sums(even, *got):
    count, rows, width = even.shape
    return pl.pallas_call(
        pair_body,
        in_specs=[pl.BlockSpec(memory_space=VMEM)] * (1 + len(got)),
        out_specs=[pl.BlockSpec(memory_space=VMEM)] * count,
        out_shape=[jax.ShapeDtypeStruct((rows, width), jnp.bfloat16)] * count,
        compiler_params=params(),
        cost_estimate=cost(0.7),
        name="pair_sums",
    )(even, *got)


def scatter_ctx(pairs):
    return [part if k == 0 else swap(part, 2 * k, "ctx") for k, part in enumerate(pairs)]


def shards(inputs, out_grad, w_query, w_key, value_projection, w_out, doc_lengths, span_order):
    tokens = inputs.shape[0]
    share = ASKER_NUM // SHARED_KV_NUM
    half = tokens // 2
    sizes = (
        lax.axis_size("ctx"),
        tokens // 2,
        w_key.shape[1] // CHANNEL_DIM,
        share,
        CHANNEL_DIM,
        doc_lengths.shape[0],
    )
    heads = lax.axis_size("head")
    last = [span_order]

    def turn(call, *args):
        held, *args = lax.optimization_barrier((last[0], *args))
        out = call(*args)
        last[0] = out if hasattr(out, "shape") else out[0]
        return out

    def attend(upper, call, *args):
        return turn(lambda *a: call(upper, *a, span_order, doc_lengths, sizes), *args)

    def context(blocks, stacks, spans, total, dtype):
        shape = jax.tree.structure((blocks, stacks, total))

        def call(*flat):
            parts, weights, given = jax.tree.unflatten(shape, flat)
            return back_project(parts, weights, spans, given, dtype)

        return turn(call, *jax.tree.leaves((blocks, stacks, total)))

    def send_first(parts, stack, places=None):
        if stack is None:
            return {k ^ 1: (swap(parts[k], 1, "head"), None) for k in places} | {0: None}
        places = range(heads - 1, 0, -2)
        got = swap(stack, 1, "head")
        return {k ^ 1: (got, i) for i, k in enumerate(places)}

    def send_rest(parts, got):
        ends, bit = [(parts[0], None), got[0]], 2
        parts = {
            k: turn(lambda a, b, at=got[k][1]: add(a, b, at), parts[k], got[k][0])
            for k in range(2, heads, 2)
        }
        while bit < heads:
            moved = {k ^ bit: swap(parts[k], bit, "head") for k in parts if k & bit}
            ends.append((moved.pop(0), None))
            parts = {k: turn(lambda a, b: add(a, b, None), parts[k], moved[k]) for k in moved}
            bit *= 2
        return ends

    far = [{0: out_grad[:half]}, {0: out_grad[half:]}]
    bit = heads // 2
    while bit > 1:
        far = [got | {k ^ bit: swap(x, bit, "head") for k, x in got.items()} for got in far]
        bit //= 2
    near = [swap(out_grad[:half], 1, "head"), swap(out_grad[half:], 1, "head")]
    own = turn(project_kv, inputs, w_key, value_projection)
    near_blocks, (far[0], near[0]) = gather_even(own, "ctx", (far[0], near[0]))
    query = turn(project, inputs, w_query)
    query, near_blocks = lax.optimization_barrier((query, near_blocks))
    blocks = (*near_blocks, *[swap(block, 1, "ctx") for block in near_blocks])
    query, far[1], near[1] = lax.optimization_barrier((query, far[1], near[1]))
    *upper_stats, w_first, held = attend(True, stats, query, *blocks, w_out)
    *lower_stats, w_second = attend(False, stats, query, held, w_out)
    passed = [{k ^ 1: swap(x, 1, "head") for k, x in got.items() if k} for got in far]
    come = {0: (out_grad,), 1: tuple(near)}
    come |= {k: (far[0][k], far[1][k]) for k in range(2, heads, 2)}
    come |= {k: (passed[0][k], passed[1][k]) for k in range(3, heads, 2)}
    blocks = [come[k] for k in range(heads)]
    mid = heads // 2
    total = context(
        blocks[:-1], (w_first, w_second), [(0, mid), (0, mid - 1)], None, jnp.float32
    )
    context_grad = context(blocks[-1:], (w_second,), [(mid - 1, mid)], total, jnp.bfloat16)
    upper_dq, even, *odd, rest = attend(True, grads, query, context_grad, *upper_stats, held)
    upper = scatter_ctx(turn(pair_sums, even, *[swap(x, 1, "ctx") for x in odd]))
    weights = (w_query, w_key, value_projection)
    lower_dq, even, *odd, wq, wk, wv = attend(
        False, grads, query, context_grad, *lower_stats, rest, held, *weights
    )
    sides = [list(range(heads - 1, 0, -2)), list(range(heads - 2, -1, -2))]
    weights = [(wq, wk, wv), weights]

    def firsts_of(side):
        return turn(
            lambda a, b, w: query_terms(a, b, w, heads, sides[side]),
            upper_dq,
            lower_dq,
            weights[side][0],
        )

    def terms_of(first, terms, side, stacked=False):
        outs = turn(
            lambda a, k, v, *b: all_terms(a, b, k, v, heads, sides[side], stacked),
            first,
            *weights[side][1:],
            *terms,
        )
        return outs[0] if stacked else dict(zip(sides[side], outs))

    first = [firsts_of(0)]
    lower_odd = [swap(x, 1, "ctx") for x in odd]
    upper_got = send_first(None, terms_of(first[0][0], upper, 0, True))
    lower = scatter_ctx(turn(pair_sums, even, *lower_odd))
    first.append(firsts_of(1))
    upper = terms_of(first[1][0], upper, 1)
    parts = terms_of(first[0][1], lower, 0)
    lower_got = send_first(parts, None, sides[0][:-1])
    upper = send_rest(upper, upper_got)
    lower = terms_of(first[1][1], lower, 1)
    lower = send_rest(lower, lower_got)
    stack, at = upper[1]
    upper = [(turn(lambda a, b: merge(a, b, at), upper[0][0], stack), None)] + upper[2:]
    last_part, held = lax.optimization_barrier((parts[1], last[0]))
    last_part = (swap(last_part, 1, "head"), None)
    total = upper[0][0]
    for block, at in upper[1:]:
        total = turn(lambda a, b: merge(a, b, None), total, block)
    upper = [(total, None)]
    total = lower[0][0]
    for block, at in lower[2:]:
        total = turn(lambda a, b: merge(a, b, None), total, block)
    lower = [(total, None), last_part]
    return join_rows(upper, lower, span_order)


def solution(mesh):
    in_specs = (
        P("ctx", None),
        P("ctx", "head"),
        P(None, "head"),
        P(None, "head"),
        P(None, "head"),
        P("head", None),
        P(),
        P(),
    )
    out_specs = P("ctx", "head")
    return jax.shard_map(shards, mesh=mesh, in_specs=in_specs, out_specs=out_specs, check_vma=False)
```

```python
import functools
import math

import jax
import jax.numpy as jnp
from jax import lax
from jax.experimental import pallas as pl
from jax.experimental.pallas import tpu as pltpu
from jax.sharding import PartitionSpec as P

ASKER_NUM = 32
SHARED_KV_NUM = 8
CHANNEL_DIM = 128

masked_score = -1e30
MIB = 1 << 20
AT_ONCE = 4
VMEM = pltpu.VMEM
HBM = pltpu.HBM


def mm(a, b):
    return lax.dot_general(a, b, (((1,), (0,)), ((), ())), preferred_element_type=jnp.float32)


def mm_nt(a, b):
    return lax.dot_general(a, b, (((1,), (1,)), ((), ())), preferred_element_type=jnp.float32)


def mm_tn(a, b):
    return lax.dot_general(a, b, (((0,), (0,)), ((), ())), preferred_element_type=jnp.float32)


def params():
    return pltpu.CompilerParams(vmem_limit_bytes=24 * MIB)


def cost():
    return pl.CostEstimate(flops=0, bytes_accessed=1, transcendentals=0)


def upper_half(order):
    first = order[2 * lax.axis_index("ctx")]
    return jnp.where(2 * first >= order.shape[0], 0, 1)


def in_hbm(x):
    return pltpu.with_memory_space_constraint(x, HBM)


def fetch(src, dst, sem):
    copy = pltpu.make_async_copy(src, dst, sem)
    copy.start()
    return copy


def kv_body(parts, x_ref, wk_ref, wv_ref, out_ref, x, wk, wv, acc, sems):
    width = wk.shape[1]
    depth = wk.shape[0] // parts
    copies = []
    for i in range(parts):
        rows = slice(i * depth, (i + 1) * depth)
        copies.append(
            [
                fetch(x_ref.at[:, rows], x.at[:, rows], sems.at[i, 0]),
                fetch(wk_ref.at[rows], wk.at[rows], sems.at[i, 1]),
                fetch(wv_ref.at[rows], wv.at[rows], sems.at[i, 2]),
            ]
        )
    for i in range(parts):
        rows = slice(i * depth, (i + 1) * depth)
        for copy in copies[i]:
            copy.wait()
        left = x[:, rows]
        terms = mm(left, wk[rows, :]), mm(left, wv[rows, :])
        for j, term in enumerate(terms):
            columns = slice(j * width, (j + 1) * width)
            total = term if i == 0 else acc[:, columns] + term
            if i < parts - 1:
                acc[:, columns] = total
            else:
                out_ref[:, columns] = total.astype(out_ref.dtype)


def project_kv(x, wk, wv):
    tokens, depth = x.shape
    width = wk.shape[1]
    parts = 4
    return pl.pallas_call(
        functools.partial(kv_body, parts),
        in_specs=[pl.BlockSpec(memory_space=HBM)] * 3,
        out_specs=pl.BlockSpec(memory_space=VMEM),
        out_shape=jax.ShapeDtypeStruct((tokens, 2 * width), jnp.bfloat16),
        scratch_shapes=[
            VMEM(x.shape, x.dtype),
            VMEM(wk.shape, wk.dtype),
            VMEM(wv.shape, wv.dtype),
            VMEM((tokens, 2 * width), jnp.float32),
            pltpu.SemaphoreType.DMA((parts, 3)),
        ],
        compiler_params=params(),
        cost_estimate=cost(),
        name="project_kv",
    )(in_hbm(x), in_hbm(wk), in_hbm(wv))


def project_body(parts, x_ref, w_ref, out_ref, x, w, acc, sems):
    depth = w.shape[0] // parts
    copies = []
    for i in range(parts):
        rows = slice(i * depth, (i + 1) * depth)
        copies.append(
            [
                fetch(x_ref.at[:, rows], x.at[:, rows], sems.at[i, 0]),
                fetch(w_ref.at[rows], w.at[rows], sems.at[i, 1]),
            ]
        )
    for i in range(parts):
        rows = slice(i * depth, (i + 1) * depth)
        for copy in copies[i]:
            copy.wait()
        total = mm(x[:, rows], w[rows, :])
        if i:
            total = acc[...] + total
        if i < parts - 1:
            acc[...] = total
        else:
            out_ref[...] = total.astype(out_ref.dtype)


def project(x, w):
    tokens, depth = x.shape
    width = w.shape[1]
    parts = 4
    return pl.pallas_call(
        functools.partial(project_body, parts),
        in_specs=[pl.BlockSpec(memory_space=HBM)] * 2,
        out_specs=pl.BlockSpec(memory_space=VMEM),
        out_shape=jax.ShapeDtypeStruct((tokens, width), jnp.bfloat16),
        scratch_shapes=[
            VMEM(x.shape, x.dtype),
            VMEM(w.shape, w.dtype),
            VMEM((tokens, width), jnp.float32),
            pltpu.SemaphoreType.DMA((parts, 2)),
        ],
        compiler_params=params(),
        cost_estimate=cost(),
        name="project",
    )(in_hbm(x), in_hbm(w))


def back_body(given, rows, spans, *refs):
    refs, out_ref = list(refs[:-1]), refs[-1]
    total = refs.pop(0)[...] if given else None
    stacks = [refs.pop() for _ in spans][::-1]
    for w, (low, high) in zip(stacks, spans):
        for i in range(low, high):
            x = refs.pop(0)[...]
            if x.shape[0] < rows:
                x = jnp.concatenate([x, refs.pop(0)[...]], axis=0)
            term = mm_nt(x, w[i])
            total = term if total is None else total + term
    out_ref[...] = total.astype(out_ref.dtype)


def back_project(blocks, stacks, spans, total, dtype):
    rows = blocks[0][0].shape[0] * len(blocks[0])
    given = [] if total is None else [total]
    flat = [x for block in blocks for x in block]
    operands = (*given, *flat, *stacks)
    return pl.pallas_call(
        functools.partial(back_body, len(given), rows, spans),
        in_specs=[pl.BlockSpec(memory_space=VMEM)] * len(operands),
        out_specs=pl.BlockSpec(memory_space=VMEM),
        out_shape=jax.ShapeDtypeStruct((rows, stacks[0].shape[1]), dtype),
        compiler_params=params(),
        cost_estimate=cost(),
        name="context_grad",
    )(*operands)


def fetch_columns(places, ref, out, sems):
    me = lax.axis_index("head")
    depth = out.shape[2]
    return [
        fetch(ref.at[:, pl.ds(pl.multiple_of((me ^ k) * depth, depth), depth)], out.at[i], sems.at[i])
        for i, k in enumerate(places)
    ]


def fetch_rows(places, ref, out, sems, at):
    me = lax.axis_index("head")
    share = out.shape[1]
    return [
        fetch(ref.at[pl.ds(pl.multiple_of((me ^ k) * share, share), share)], out.at[i], sems.at[i, at])
        for i, k in enumerate(places)
    ]


def rows_shape(places, w, heads):
    return jax.ShapeDtypeStruct((len(places), w.shape[0] // heads, w.shape[1]), w.dtype)


def query_terms_body(places, upper_ref, lower_ref, w_ref, *refs):
    upper_out, lower_out = refs[:2]
    copies, w = [], w_ref
    if places is not None:
        w, sems = refs[2:]
        copies = fetch_rows(places, w_ref, w, sems, 0)
    half = upper_ref.shape[0]
    x = jnp.concatenate([upper_ref[...], lower_ref[...]], axis=0)
    for i in range(w.shape[0]):
        if copies:
            copies[i].wait()
        total = mm_nt(x, w[i])
        upper_out[i] = total[:half]
        lower_out[i] = total[half:]


def query_terms(upper, lower, w, heads, places):
    rows, depth = upper.shape
    scratch = []
    shape = w
    if w.ndim == 2:
        shape = rows_shape(places, w, heads)
        scratch = [VMEM(shape.shape, w.dtype), pltpu.SemaphoreType.DMA((len(places), 1))]
        w = in_hbm(w)
    else:
        places = None
    size, share = shape.shape[:2]
    return pl.pallas_call(
        functools.partial(query_terms_body, places),
        in_specs=[pl.BlockSpec(memory_space=VMEM)] * 2
        + [pl.BlockSpec(memory_space=HBM if scratch else VMEM)],
        out_specs=[pl.BlockSpec(memory_space=VMEM)] * 2,
        out_shape=[jax.ShapeDtypeStruct((size, rows, share), jnp.float32)] * 2,
        scratch_shapes=scratch,
        compiler_params=params(),
        cost_estimate=cost(),
        name="query_terms",
    )(upper, lower, w)


def all_terms_body(places, count, first_ref, *refs):
    terms, (wk_ref, wv_ref), refs = refs[:count], refs[count : count + 2], refs[count + 2 :]
    wk, wv, copies = wk_ref, wv_ref, []
    if places is not None:
        refs, (wk, wv, sems) = refs[:-3], refs[-3:]
        copies = [fetch_rows(places, wk_ref, wk, sems, 0), fetch_rows(places, wv_ref, wv, sems, 1)]
    outs = refs
    width = wk.shape[2]
    grads = terms[0][...].astype(jnp.float32)
    for term in terms[1:]:
        grads = grads + term[...].astype(jnp.float32)
    grads = grads.astype(jnp.bfloat16)
    for i in range(wk.shape[0]):
        for some in copies:
            some[i].wait()
        total = first_ref[i] + mm_nt(grads[:, :width], wk[i])
        total = total + mm_nt(grads[:, width:], wv[i])
        if len(outs) == 1:
            outs[0][i] = total.astype(outs[0].dtype)
        else:
            outs[i][...] = total.astype(outs[i].dtype)


def all_terms(first, terms, wk, wv, heads, places, stacked):
    size, rows, share = first.shape
    scratch = []
    if wk.ndim == 2:
        shape = rows_shape(places, wk, heads).shape
        scratch = [
            VMEM(shape, wk.dtype),
            VMEM(shape, wv.dtype),
            pltpu.SemaphoreType.DMA((size, 2)),
        ]
        wk, wv = in_hbm(wk), in_hbm(wv)
    else:
        places = None
    return pl.pallas_call(
        functools.partial(all_terms_body, places, len(terms)),
        in_specs=[pl.BlockSpec(memory_space=VMEM)] * (1 + len(terms))
        + [pl.BlockSpec(memory_space=HBM if scratch else VMEM)] * 2,
        out_specs=[pl.BlockSpec(memory_space=VMEM)] * (1 if stacked else size),
        out_shape=[jax.ShapeDtypeStruct((size, rows, share), jnp.bfloat16)]
        if stacked
        else [jax.ShapeDtypeStruct((rows, share), jnp.bfloat16)] * size,
        scratch_shapes=scratch,
        compiler_params=params(),
        cost_estimate=cost(),
        name="all_terms",
    )(first, *terms, wk, wv)


def part_of(ref, at):
    return (ref[...] if at is None else ref[at]).astype(jnp.float32)


def add_body(at, a_ref, b_ref, out_ref):
    out_ref[...] = (a_ref[...].astype(jnp.float32) + part_of(b_ref, at)).astype(out_ref.dtype)


def add(a, b, at):
    return pl.pallas_call(
        functools.partial(add_body, at),
        in_specs=[pl.BlockSpec(memory_space=VMEM)] * 2,
        out_specs=pl.BlockSpec(memory_space=VMEM),
        out_shape=jax.ShapeDtypeStruct(a.shape, a.dtype),
        compiler_params=params(),
        cost_estimate=cost(),
        name="add",
    )(a, b)


def merge_body(at, a_ref, b_ref, out_ref):
    out_ref[...] = a_ref[...].astype(jnp.float32) + part_of(b_ref, at)


def merge(a, b, at):
    return pl.pallas_call(
        functools.partial(merge_body, at),
        in_specs=[pl.BlockSpec(memory_space=VMEM)] * 2,
        out_specs=pl.BlockSpec(memory_space=VMEM),
        out_shape=jax.ShapeDtypeStruct(a.shape, jnp.float32),
        compiler_params=params(),
        cost_estimate=cost(),
        name="merge",
    )(a, b)


def join_body(ats, order, *refs):
    refs, out_ref = list(refs[:-1]), refs[-1]
    half = out_ref.shape[0] // 2
    at = upper_half(order) * half
    for j, place in enumerate((at, half - at)):
        total = None
        for i in ats[j]:
            term = part_of(refs.pop(0), i)
            total = term if total is None else total + term
        out_ref[pl.ds(pl.multiple_of(place, half), half), :] = total.astype(out_ref.dtype)


def join_rows(upper, lower, span_order):
    rows, width = upper[0][0].shape
    ats = [[at for _, at in terms] for terms in (upper, lower)]
    blocks = [block for block, _ in upper + lower]
    return pl.pallas_call(
        functools.partial(join_body, ats),
        in_specs=[pl.BlockSpec(memory_space=pltpu.SMEM)]
        + [pl.BlockSpec(memory_space=VMEM)] * len(blocks),
        out_specs=pl.BlockSpec(memory_space=VMEM),
        out_shape=jax.ShapeDtypeStruct((2 * rows, width), jnp.bfloat16),
        compiler_params=params(),
        cost_estimate=cost(),
        name="join_rows",
    )(span_order, *blocks)


def find_places(order, places, me, spans):
    for i in range(spans):
        k = (i // 2) ^ me
        places[order[i]] = (k % 2) * (spans // 2) + (k // 2) * 2 + (i % 2)


def own_span(order, lengths, docs, me, j, half):
    span = order[2 * me + j]
    position = span * half + lax.broadcasted_iota(jnp.int32, (1, half), 1)
    first, end = 0, 0
    start = jnp.zeros((1, half), jnp.int32)
    for k in range(docs):
        end = end + lengths[k]
        start = jnp.where(position >= end, end, start)
        first = jnp.where(span * half >= end, end, first)
    return span, position, start, first // half


def stack_heads(ref, rows, group, share, dim):
    base = group * share
    return jnp.concatenate(
        [ref[rows, (base + h) * dim : (base + h + 1) * dim] for h in range(share)], axis=0
    )


def load_blocks(refs, held):
    rows = refs[0].shape[0]
    for k, ref in enumerate(refs):
        held[k * rows : (k + 1) * rows, :] = ref[...]


def span_group(i, span, held, places, half, count):
    numbers = [span - count * i - j for j in range(count - 1, -1, -1)]
    known = [jnp.maximum(p, 0) for p in numbers]
    at = [pl.multiple_of(places[p] * half, half) for p in known]
    block = jnp.concatenate([held[pl.ds(place, half), :] for place in at], axis=0)
    key = numbers[0] * half + lax.broadcasted_iota(jnp.int32, (count * half, 1), 0)
    return known, block, key


def keep(allowed, x, other):
    width = allowed.shape[1]
    return jnp.concatenate(
        [
            jnp.where(allowed, x[:, i : i + width], other)
            for i in range(0, x.shape[1], width)
        ],
        axis=1,
    )


def stats_body(sizes, upper, spare, order, lengths, q_ref, *refs):
    peers, half, groups, share, dim, docs = sizes
    if upper:
        w_ref, level_ref, mixed_ref, w, held, kept, places, sems = refs[peers:]
    else:
        held, w_ref, level_ref, mixed_ref, w, kept, places, sems = refs
    copies = fetch_columns(spare, w_ref, w, sems)
    if upper:
        load_blocks(refs[:peers], held)
    me = lax.axis_index("ctx")
    width = groups * dim
    factor = math.log2(math.e) / math.sqrt(dim)
    find_places(order, places, me, 2 * peers)
    columns = share * half
    at = upper_half(order)
    j = at if upper else 1 - at
    span, position, start, lowest = own_span(order, lengths, docs, me, j, half)
    rows = pl.ds(pl.multiple_of(j * half, half), half)
    queries = [stack_heads(q_ref, rows, g, share, dim) for g in range(groups)]

    deep = AT_ONCE * half
    steps = (span - lowest) // AT_ONCE + 1

    def score(i, carry):
        known, block, key = span_group(i, span, held, places, half, AT_ONCE)
        allowed = (key <= position) & (key >= start)
        fresh = []
        for g in range(groups):
            logits = keep(allowed, mm_nt(block[:, g * dim : (g + 1) * dim], queries[g]), masked_score)
            kept[g, pl.ds(pl.multiple_of(i * deep, deep), deep), :] = logits
            high = jnp.max(logits.reshape(deep // 8, 8, columns), axis=0)
            fresh.append(jnp.maximum(carry[g], high))
        return tuple(fresh)

    empty = jnp.full((8, columns), masked_score, jnp.float32)
    tops = lax.fori_loop(0, steps, score, (empty,) * groups)
    tops = [jnp.max(top, axis=0, keepdims=True) for top in tops]

    def mix(i, carry):
        known, block, key = span_group(i, span, held, places, half, AT_ONCE)
        fresh = []
        for g in range(groups):
            total, mixed = carry[g]
            values = block[:, width + g * dim : width + (g + 1) * dim]
            logits = kept[g, pl.ds(pl.multiple_of(i * deep, deep), deep), :]
            weights = jnp.exp2((logits - tops[g]) * factor)
            total = total + jnp.sum(weights.reshape(deep // 8, 8, columns), axis=0)
            mixed = mixed + mm_tn(values, weights.astype(jnp.bfloat16))
            fresh.append((total, mixed))
        return tuple(fresh)

    empty = (jnp.zeros((8, columns), jnp.float32), jnp.zeros((dim, columns), jnp.float32))
    done = lax.fori_loop(0, steps, mix, (empty,) * groups)
    for g in range(groups):
        top, (total, mixed) = tops[g], done[g]
        total = jnp.sum(total, axis=0, keepdims=True)
        level_ref[g, 0:1] = top
        level_ref[g, 1:2] = jnp.log2(total)
        mixed_ref[g] = mixed / total
    for copy in copies:
        copy.wait()


def stats(upper, q, *args):
    *blocks, w, span_order, doc_lengths, sizes = args
    heads = lax.axis_size("head")
    spare = list(range(heads))[: heads // 2] if upper else list(range(heads))[heads // 2 :]
    peers, half, groups, share, dim, docs = sizes
    columns = share * half
    return pl.pallas_call(
        functools.partial(stats_body, sizes, upper, spare),
        in_specs=[pl.BlockSpec(memory_space=pltpu.SMEM)] * 2
        + [pl.BlockSpec(memory_space=VMEM)] * (1 + len(blocks))
        + [pl.BlockSpec(memory_space=HBM)],
        out_specs=[pl.BlockSpec(memory_space=VMEM)] * (4 if upper else 3),
        out_shape=[
            jax.ShapeDtypeStruct((groups, 2, columns), jnp.float32),
            jax.ShapeDtypeStruct((groups, dim, columns), jnp.float32),
            jax.ShapeDtypeStruct((len(spare), w.shape[0], w.shape[1] // heads), w.dtype),
        ]
        + [jax.ShapeDtypeStruct((2 * peers * half, 2 * groups * dim), jnp.bfloat16)] * upper,
        scratch_shapes=[
            VMEM((groups, (2 * peers + AT_ONCE) * half, columns), jnp.float32),
            pltpu.SMEM((2 * peers,), jnp.int32),
            pltpu.SemaphoreType.DMA((len(spare),)),
        ],
        compiler_params=params(),
        cost_estimate=cost(),
        name="upper_stats" if upper else "lower_stats",
    )(span_order, doc_lengths, q, *blocks, in_hbm(w))


def grads_body(sizes, upper, spare, order, lengths, q_ref, g_ref, level_ref, mixed_ref, *refs):
    peers, half, groups, share, dim, docs = sizes
    spans = 2 * peers
    count = 3 if upper else AT_ONCE
    if upper:
        held, dq_ref, even_ref, *odd_refs, sums, places = refs
    else:
        rest_ref, held, wq_ref, wk_ref, wv_ref, dq_ref, even_ref, *odd_refs, wq, wk, wv, sums, places, sems = refs
        copies = []
        for i, (w_ref, w) in enumerate(((wq_ref, wq), (wk_ref, wk), (wv_ref, wv))):
            copies += fetch_rows(spare, w_ref, w, sems, i)
    me = lax.axis_index("ctx")
    width = groups * dim
    scale = 1.0 / math.sqrt(dim)
    factor = math.log2(math.e) * scale
    find_places(order, places, me, spans)
    columns = share * half
    at = upper_half(order)
    j = at if upper else 1 - at
    span, position, start, lowest = own_span(order, lengths, docs, me, j, half)
    steps = (span - lowest) // count + 1

    def fill(p, carry):
        target = pl.ds(pl.multiple_of(p * half, half), half)
        if upper:
            sums[target, :] = jnp.zeros((half, 2 * width), jnp.float32)
        else:
            sums[target, :] = rest_ref[target, :]
        return carry

    lax.fori_loop(0, jnp.maximum(span - count * steps + 1, 0), fill, 0)
    lax.fori_loop(span + 1, sums.shape[0] // half, fill, 0)
    rows = pl.ds(pl.multiple_of(j * half, half), half)
    queries = [stack_heads(q_ref, rows, g, share, dim) for g in range(groups)]
    outs = [stack_heads(g_ref, rows, g, share, dim) for g in range(groups)]
    tops = [level_ref[g, 0:1] for g in range(groups)]
    levels = [level_ref[g, 1:2] for g in range(groups)]
    deltas = []
    for g in range(groups):
        turned = jnp.concatenate(
            [outs[g][h * half : (h + 1) * half].astype(jnp.float32).T for h in range(share)],
            axis=1,
        )
        deltas.append(jnp.sum(turned * mixed_ref[g], axis=0, keepdims=True))

    def visit(i, carry):
        known, block, key = span_group(i, span, held, places, half, count)
        allowed = (key <= position) & (key >= start)
        targets = [pl.ds(pl.multiple_of(p * half, half), half) for p in known]
        fresh = []
        for g in range(groups):
            keys = block[:, g * dim : (g + 1) * dim]
            values = block[:, width + g * dim : width + (g + 1) * dim]
            logits = mm_nt(keys, queries[g])
            chance = keep(allowed, jnp.exp2((logits - tops[g]) * factor - levels[g]), 0.0)
            slopes = mm_nt(values, outs[g])
            score = (chance * (slopes - deltas[g])).astype(jnp.bfloat16)
            key_term = mm(score, queries[g])
            value_term = mm(chance.astype(jnp.bfloat16), outs[g])
            for j, target in enumerate(targets):
                part = slice(j * half, (j + 1) * half)
                for at, term in ((g * dim, key_term[part]), (width + g * dim, value_term[part])):
                    columns_at = slice(at, at + dim)
                    if not upper:
                        term = term + rest_ref[target, columns_at]
                    sums[target, columns_at] = term
            fresh.append(carry[g] + mm_tn(keys, score))
        return tuple(fresh)

    empty = jnp.zeros((dim, columns), jnp.float32)
    done = lax.fori_loop(0, steps, visit, (empty,) * groups)
    for g in range(groups):
        for h in range(share):
            head = g * share + h
            dq_ref[:, head * dim : (head + 1) * dim] = (
                (done[g][:, h * half : (h + 1) * half].T * scale).astype(dq_ref.dtype)
            )
    for k in range(peers):
        out, slot = even_ref, k // 2
        if k % 2:
            out, slot = odd_refs[slot // odd_refs[0].shape[0]], slot % odd_refs[0].shape[0]
        first = order[2 * (me ^ k)]
        other = spans - 1 - first
        pick = jnp.maximum(first, other) if upper else jnp.minimum(first, other)
        part = pl.ds(pl.multiple_of(pick * half, half), half)
        out[slot, :, :width] = (sums[part, :width] * scale).astype(out.dtype)
        out[slot, :, width:] = sums[part, width:].astype(out.dtype)
    if not upper:
        for copy in copies:
            copy.wait()


def grads(upper, q, g, level, mixed, *args):
    *blocks, span_order, doc_lengths, sizes = args
    weights, spare, scratch = [], [], []
    if not upper:
        heads = lax.axis_size("head")
        spare = list(range(heads - 1, 0, -2))
        weights, blocks = [in_hbm(w) for w in blocks[-3:]], blocks[:-3]
        scratch = [pltpu.SemaphoreType.DMA((len(spare), 3))]
    peers, half, groups, share, dim, docs = sizes
    tokens, width = 2 * half, groups * dim
    columns = share * half
    terms = jax.ShapeDtypeStruct((peers // 2, half, 2 * width), jnp.bfloat16)
    odds = jax.ShapeDtypeStruct((peers // 4, half, 2 * width), jnp.bfloat16)
    rests = jax.ShapeDtypeStruct((peers * tokens, 2 * width), jnp.float32)
    outs = [jax.ShapeDtypeStruct((half, g.shape[1]), jnp.bfloat16), terms, odds, odds] + [rests] * upper
    outs += [rows_shape(spare, w, heads) for w in weights]
    return pl.pallas_call(
        functools.partial(grads_body, sizes, upper, spare),
        in_specs=[pl.BlockSpec(memory_space=pltpu.SMEM)] * 2
        + [pl.BlockSpec(memory_space=VMEM)] * (4 + len(blocks))
        + [pl.BlockSpec(memory_space=HBM)] * len(weights),
        out_specs=[pl.BlockSpec(memory_space=VMEM)] * len(outs),
        out_shape=outs,
        scratch_shapes=[VMEM((peers * half, 2 * width), jnp.float32)] * (not upper)
        + [
            pltpu.SMEM((2 * peers,), jnp.int32),
        ]
        + scratch,
        compiler_params=params(),
        cost_estimate=cost(),
        name="upper_grads" if upper else "lower_grads",
    )(span_order, doc_lengths, q, g, level, mixed, *blocks, *weights)


def swap(x, k, axis):
    return lax.ppermute(x, axis, [(i, i ^ k) for i in range(lax.axis_size(axis))])


def gather_even(x, axis, held):
    size = lax.axis_size(axis)
    got, bit = {0: x}, 2
    while bit < size:
        passed = {k: block for k, block in got.items() if k}
        passed, held = lax.optimization_barrier((passed, held))
        got |= {bit: swap(x, bit, axis)}
        got |= {k ^ bit: swap(block, bit, axis) for k, block in passed.items()}
        bit *= 2
    return [got[k] for k in sorted(got)], held


def pair_body(even_ref, *refs):
    count = even_ref.shape[0]
    odd_refs, outs = refs[:-count], refs[-count:]
    part = odd_refs[0].shape[0]
    for k, out in enumerate(outs):
        total = even_ref[k].astype(jnp.float32) + odd_refs[k // part][k % part].astype(jnp.float32)
        out[...] = total.astype(out.dtype)


def pair_sums(even, *got):
    count, rows, width = even.shape
    return pl.pallas_call(
        pair_body,
        in_specs=[pl.BlockSpec(memory_space=VMEM)] * (1 + len(got)),
        out_specs=[pl.BlockSpec(memory_space=VMEM)] * count,
        out_shape=[jax.ShapeDtypeStruct((rows, width), jnp.bfloat16)] * count,
        compiler_params=params(),
        cost_estimate=cost(),
        name="pair_sums",
    )(even, *got)


def scatter_ctx(pairs):
    return [part if k == 0 else swap(part, 2 * k, "ctx") for k, part in enumerate(pairs)]


def shards(inputs, out_grad, w_query, w_key, value_projection, w_out, doc_lengths, span_order):
    tokens = inputs.shape[0]
    share = ASKER_NUM // SHARED_KV_NUM
    half = tokens // 2
    sizes = (
        lax.axis_size("ctx"),
        tokens // 2,
        w_key.shape[1] // CHANNEL_DIM,
        share,
        CHANNEL_DIM,
        doc_lengths.shape[0],
    )
    heads = lax.axis_size("head")
    last = [span_order]

    def turn(call, *args):
        held, *args = lax.optimization_barrier((last[0], *args))
        out = call(*args)
        last[0] = out if hasattr(out, "shape") else out[0]
        return out

    def attend(upper, call, *args):
        return turn(lambda *a: call(upper, *a, span_order, doc_lengths, sizes), *args)

    def context(blocks, stacks, spans, total, dtype):
        shape = jax.tree.structure((blocks, stacks, total))

        def call(*flat):
            parts, weights, given = jax.tree.unflatten(shape, flat)
            return back_project(parts, weights, spans, given, dtype)

        return turn(call, *jax.tree.leaves((blocks, stacks, total)))

    def send_first(parts, stack, places=None):
        if stack is None:
            return {k ^ 1: (swap(parts[k], 1, "head"), None) for k in places} | {0: None}
        places = range(heads - 1, 0, -2)
        got = swap(stack, 1, "head")
        return {k ^ 1: (got, i) for i, k in enumerate(places)}

    def send_rest(parts, got):
        ends, bit = [(parts[0], None), got[0]], 2
        parts = {
            k: turn(lambda a, b, at=got[k][1]: add(a, b, at), parts[k], got[k][0])
            for k in range(2, heads, 2)
        }
        while bit < heads:
            moved = {k ^ bit: swap(parts[k], bit, "head") for k in parts if k & bit}
            ends.append((moved.pop(0), None))
            parts = {k: turn(lambda a, b: add(a, b, None), parts[k], moved[k]) for k in moved}
            bit *= 2
        return ends

    far = [{0: out_grad[:half]}, {0: out_grad[half:]}]
    bit = heads // 2
    while bit > 1:
        far = [got | {k ^ bit: swap(x, bit, "head") for k, x in got.items()} for got in far]
        bit //= 2
    near = [swap(out_grad[:half], 1, "head"), swap(out_grad[half:], 1, "head")]
    own = turn(project_kv, inputs, w_key, value_projection)
    near_blocks, (far[0], near[0]) = gather_even(own, "ctx", (far[0], near[0]))
    query = turn(project, inputs, w_query)
    query, near_blocks = lax.optimization_barrier((query, near_blocks))
    blocks = (*near_blocks, *[swap(block, 1, "ctx") for block in near_blocks])
    query, far[1], near[1] = lax.optimization_barrier((query, far[1], near[1]))
    *upper_stats, w_first, held = attend(True, stats, query, *blocks, w_out)
    *lower_stats, w_second = attend(False, stats, query, held, w_out)
    passed = [{k ^ 1: swap(x, 1, "head") for k, x in got.items() if k} for got in far]
    come = {0: (out_grad,), 1: tuple(near)}
    come |= {k: (far[0][k], far[1][k]) for k in range(2, heads, 2)}
    come |= {k: (passed[0][k], passed[1][k]) for k in range(3, heads, 2)}
    blocks = [come[k] for k in range(heads)]
    mid = heads // 2
    total = context(
        blocks[:-1], (w_first, w_second), [(0, mid), (0, mid - 1)], None, jnp.float32
    )
    context_grad = context(blocks[-1:], (w_second,), [(mid - 1, mid)], total, jnp.bfloat16)
    upper_dq, even, *odd, rest = attend(True, grads, query, context_grad, *upper_stats, held)
    upper = scatter_ctx(turn(pair_sums, even, *[swap(x, 1, "ctx") for x in odd]))
    weights = (w_query, w_key, value_projection)
    lower_dq, even, *odd, wq, wk, wv = attend(
        False, grads, query, context_grad, *lower_stats, rest, held, *weights
    )
    sides = [list(range(heads - 1, 0, -2)), list(range(heads - 2, -1, -2))]
    weights = [(wq, wk, wv), weights]

    def firsts_of(side):
        return turn(
            lambda a, b, w: query_terms(a, b, w, heads, sides[side]),
            upper_dq,
            lower_dq,
            weights[side][0],
        )

    def terms_of(first, terms, side, stacked=False):
        outs = turn(
            lambda a, k, v, *b: all_terms(a, b, k, v, heads, sides[side], stacked),
            first,
            *weights[side][1:],
            *terms,
        )
        return outs[0] if stacked else dict(zip(sides[side], outs))

    first = [firsts_of(0)]
    lower_odd = [swap(x, 1, "ctx") for x in odd]
    upper_got = send_first(None, terms_of(first[0][0], upper, 0, True))
    lower = scatter_ctx(turn(pair_sums, even, *lower_odd))
    first.append(firsts_of(1))
    upper = terms_of(first[1][0], upper, 1)
    parts = terms_of(first[0][1], lower, 0)
    lower_got = send_first(parts, None, sides[0][:-1])
    upper = send_rest(upper, upper_got)
    lower = terms_of(first[1][1], lower, 1)
    lower = send_rest(lower, lower_got)
    stack, at = upper[1]
    upper = [(turn(lambda a, b: merge(a, b, at), upper[0][0], stack), None)] + upper[2:]
    last_part, held = lax.optimization_barrier((parts[1], last[0]))
    last_part = (swap(last_part, 1, "head"), None)
    total = upper[0][0]
    for block, at in upper[1:]:
        total = turn(lambda a, b: merge(a, b, None), total, block)
    upper = [(total, None)]
    total = lower[0][0]
    for block, at in lower[2:]:
        total = turn(lambda a, b: merge(a, b, None), total, block)
    lower = [(total, None), last_part]
    return join_rows(upper, lower, span_order)


def solution(mesh):
    in_specs = (
        P("ctx", None),
        P("ctx", "head"),
        P(None, "head"),
        P(None, "head"),
        P(None, "head"),
        P("head", None),
        P(),
        P(),
    )
    out_specs = P("ctx", "head")
    return jax.shard_map(shards, mesh=mesh, in_specs=in_specs, out_specs=out_specs, check_vma=False)
```

```python
import functools
import math

import jax
import jax.numpy as jnp
from jax import lax
from jax.experimental import pallas as pl
from jax.experimental.pallas import tpu as pltpu
from jax.sharding import PartitionSpec as P

ASKER_NUM = 32
SHARED_KV_NUM = 8
CHANNEL_DIM = 128

masked_score = -1e30
MIB = 1 << 20
AT_ONCE = 4
VMEM = pltpu.VMEM
HBM = pltpu.HBM


def mm(a, b):
    return lax.dot_general(a, b, (((1,), (0,)), ((), ())), preferred_element_type=jnp.float32)


def mm_nt(a, b):
    return lax.dot_general(a, b, (((1,), (1,)), ((), ())), preferred_element_type=jnp.float32)


def mm_tn(a, b):
    return lax.dot_general(a, b, (((0,), (0,)), ((), ())), preferred_element_type=jnp.float32)


def params():
    return pltpu.CompilerParams(vmem_limit_bytes=24 * MIB)


def cost():
    return pl.CostEstimate(flops=0, bytes_accessed=1, transcendentals=0)


def upper_half(order):
    first = order[2 * lax.axis_index("ctx")]
    return jnp.where(2 * first >= order.shape[0], 0, 1)


def in_hbm(x):
    return pltpu.with_memory_space_constraint(x, HBM)


def fetch(src, dst, sem):
    copy = pltpu.make_async_copy(src, dst, sem)
    copy.start()
    return copy


def kv_body(parts, x_ref, wk_ref, wv_ref, out_ref, x, wk, wv, acc, sems):
    width = wk.shape[1]
    depth = wk.shape[0] // parts
    copies = []
    for i in range(parts):
        rows = slice(i * depth, (i + 1) * depth)
        copies.append(
            [
                fetch(x_ref.at[:, rows], x.at[:, rows], sems.at[i, 0]),
                fetch(wk_ref.at[rows], wk.at[rows], sems.at[i, 1]),
                fetch(wv_ref.at[rows], wv.at[rows], sems.at[i, 2]),
            ]
        )
    for i in range(parts):
        rows = slice(i * depth, (i + 1) * depth)
        for copy in copies[i]:
            copy.wait()
        left = x[:, rows]
        terms = mm(left, wk[rows, :]), mm(left, wv[rows, :])
        for j, term in enumerate(terms):
            columns = slice(j * width, (j + 1) * width)
            total = term if i == 0 else acc[:, columns] + term
            if i < parts - 1:
                acc[:, columns] = total
            else:
                out_ref[:, columns] = total.astype(out_ref.dtype)


def project_kv(x, wk, wv):
    tokens, depth = x.shape
    width = wk.shape[1]
    parts = 4
    return pl.pallas_call(
        functools.partial(kv_body, parts),
        in_specs=[pl.BlockSpec(memory_space=HBM)] * 3,
        out_specs=pl.BlockSpec(memory_space=VMEM),
        out_shape=jax.ShapeDtypeStruct((tokens, 2 * width), jnp.bfloat16),
        scratch_shapes=[
            VMEM(x.shape, x.dtype),
            VMEM(wk.shape, wk.dtype),
            VMEM(wv.shape, wv.dtype),
            VMEM((tokens, 2 * width), jnp.float32),
            pltpu.SemaphoreType.DMA((parts, 3)),
        ],
        compiler_params=params(),
        cost_estimate=cost(),
        name="project_kv",
    )(in_hbm(x), in_hbm(wk), in_hbm(wv))


def project_body(parts, x_ref, w_ref, out_ref, x, w, acc, sems):
    depth = w.shape[0] // parts
    copies = []
    for i in range(parts):
        rows = slice(i * depth, (i + 1) * depth)
        copies.append(
            [
                fetch(x_ref.at[:, rows], x.at[:, rows], sems.at[i, 0]),
                fetch(w_ref.at[rows], w.at[rows], sems.at[i, 1]),
            ]
        )
    for i in range(parts):
        rows = slice(i * depth, (i + 1) * depth)
        for copy in copies[i]:
            copy.wait()
        total = mm(x[:, rows], w[rows, :])
        if i:
            total = acc[...] + total
        if i < parts - 1:
            acc[...] = total
        else:
            out_ref[...] = total.astype(out_ref.dtype)


def project(x, w):
    tokens, depth = x.shape
    width = w.shape[1]
    parts = 4
    return pl.pallas_call(
        functools.partial(project_body, parts),
        in_specs=[pl.BlockSpec(memory_space=HBM)] * 2,
        out_specs=pl.BlockSpec(memory_space=VMEM),
        out_shape=jax.ShapeDtypeStruct((tokens, width), jnp.bfloat16),
        scratch_shapes=[
            VMEM(x.shape, x.dtype),
            VMEM(w.shape, w.dtype),
            VMEM((tokens, width), jnp.float32),
            pltpu.SemaphoreType.DMA((parts, 2)),
        ],
        compiler_params=params(),
        cost_estimate=cost(),
        name="project",
    )(in_hbm(x), in_hbm(w))


def back_body(given, rows, spans, *refs):
    refs, out_ref = list(refs[:-1]), refs[-1]
    total = refs.pop(0)[...] if given else None
    stacks = [refs.pop() for _ in spans][::-1]
    for w, (low, high) in zip(stacks, spans):
        for i in range(low, high):
            x = refs.pop(0)[...]
            if x.shape[0] < rows:
                x = jnp.concatenate([x, refs.pop(0)[...]], axis=0)
            term = mm_nt(x, w[i])
            total = term if total is None else total + term
    out_ref[...] = total.astype(out_ref.dtype)


def back_project(blocks, stacks, spans, total, dtype):
    rows = blocks[0][0].shape[0] * len(blocks[0])
    given = [] if total is None else [total]
    flat = [x for block in blocks for x in block]
    operands = (*given, *flat, *stacks)
    return pl.pallas_call(
        functools.partial(back_body, len(given), rows, spans),
        in_specs=[pl.BlockSpec(memory_space=VMEM)] * len(operands),
        out_specs=pl.BlockSpec(memory_space=VMEM),
        out_shape=jax.ShapeDtypeStruct((rows, stacks[0].shape[1]), dtype),
        compiler_params=params(),
        cost_estimate=cost(),
        name="context_grad",
    )(*operands)


def fetch_columns(places, ref, out, sems):
    me = lax.axis_index("head")
    depth = out.shape[2]
    return [
        fetch(ref.at[:, pl.ds(pl.multiple_of((me ^ k) * depth, depth), depth)], out.at[i], sems.at[i])
        for i, k in enumerate(places)
    ]


def fetch_rows(places, ref, out, sems, at):
    me = lax.axis_index("head")
    share = out.shape[1]
    return [
        fetch(ref.at[pl.ds(pl.multiple_of((me ^ k) * share, share), share)], out.at[i], sems.at[i, at])
        for i, k in enumerate(places)
    ]


def rows_shape(places, w, heads):
    return jax.ShapeDtypeStruct((len(places), w.shape[0] // heads, w.shape[1]), w.dtype)


def query_terms_body(places, upper_ref, lower_ref, w_ref, *refs):
    upper_out, lower_out = refs[:2]
    copies, w = [], w_ref
    if places is not None:
        w, sems = refs[2:]
        copies = fetch_rows(places, w_ref, w, sems, 0)
    half = upper_ref.shape[0]
    x = jnp.concatenate([upper_ref[...], lower_ref[...]], axis=0)
    for i in range(w.shape[0]):
        if copies:
            copies[i].wait()
        total = mm_nt(x, w[i])
        upper_out[i] = total[:half]
        lower_out[i] = total[half:]


def query_terms(upper, lower, w, heads, places):
    rows, depth = upper.shape
    scratch = []
    shape = w
    if w.ndim == 2:
        shape = rows_shape(places, w, heads)
        scratch = [VMEM(shape.shape, w.dtype), pltpu.SemaphoreType.DMA((len(places), 1))]
        w = in_hbm(w)
    else:
        places = None
    size, share = shape.shape[:2]
    return pl.pallas_call(
        functools.partial(query_terms_body, places),
        in_specs=[pl.BlockSpec(memory_space=VMEM)] * 2
        + [pl.BlockSpec(memory_space=HBM if scratch else VMEM)],
        out_specs=[pl.BlockSpec(memory_space=VMEM)] * 2,
        out_shape=[jax.ShapeDtypeStruct((size, rows, share), jnp.float32)] * 2,
        scratch_shapes=scratch,
        compiler_params=params(),
        cost_estimate=cost(),
        name="query_terms",
    )(upper, lower, w)


def all_terms_body(places, count, first_ref, *refs):
    terms, (wk_ref, wv_ref), refs = refs[:count], refs[count : count + 2], refs[count + 2 :]
    wk, wv, copies = wk_ref, wv_ref, []
    if places is not None:
        refs, (wk, wv, sems) = refs[:-3], refs[-3:]
        copies = [fetch_rows(places, wk_ref, wk, sems, 0), fetch_rows(places, wv_ref, wv, sems, 1)]
    outs = refs
    width = wk.shape[2]
    grads = terms[0][...].astype(jnp.float32)
    for term in terms[1:]:
        grads = grads + term[...].astype(jnp.float32)
    grads = grads.astype(jnp.bfloat16)
    for i in range(wk.shape[0]):
        for some in copies:
            some[i].wait()
        total = first_ref[i] + mm_nt(grads[:, :width], wk[i])
        total = total + mm_nt(grads[:, width:], wv[i])
        if len(outs) == 1:
            outs[0][i] = total.astype(outs[0].dtype)
        else:
            outs[i][...] = total.astype(outs[i].dtype)


def all_terms(first, terms, wk, wv, heads, places, stacked):
    size, rows, share = first.shape
    scratch = []
    if wk.ndim == 2:
        shape = rows_shape(places, wk, heads).shape
        scratch = [
            VMEM(shape, wk.dtype),
            VMEM(shape, wv.dtype),
            pltpu.SemaphoreType.DMA((size, 2)),
        ]
        wk, wv = in_hbm(wk), in_hbm(wv)
    else:
        places = None
    return pl.pallas_call(
        functools.partial(all_terms_body, places, len(terms)),
        in_specs=[pl.BlockSpec(memory_space=VMEM)] * (1 + len(terms))
        + [pl.BlockSpec(memory_space=HBM if scratch else VMEM)] * 2,
        out_specs=[pl.BlockSpec(memory_space=VMEM)] * (1 if stacked else size),
        out_shape=[jax.ShapeDtypeStruct((size, rows, share), jnp.bfloat16)]
        if stacked
        else [jax.ShapeDtypeStruct((rows, share), jnp.bfloat16)] * size,
        scratch_shapes=scratch,
        compiler_params=params(),
        cost_estimate=cost(),
        name="all_terms",
    )(first, *terms, wk, wv)


def part_of(ref, at):
    return (ref[...] if at is None else ref[at]).astype(jnp.float32)


def add_body(at, a_ref, b_ref, out_ref):
    out_ref[...] = (a_ref[...].astype(jnp.float32) + part_of(b_ref, at)).astype(out_ref.dtype)


def add(a, b, at):
    return pl.pallas_call(
        functools.partial(add_body, at),
        in_specs=[pl.BlockSpec(memory_space=VMEM)] * 2,
        out_specs=pl.BlockSpec(memory_space=VMEM),
        out_shape=jax.ShapeDtypeStruct(a.shape, a.dtype),
        compiler_params=params(),
        cost_estimate=cost(),
        name="add",
    )(a, b)


def merge_body(at, a_ref, b_ref, out_ref):
    out_ref[...] = a_ref[...].astype(jnp.float32) + part_of(b_ref, at)


def merge(a, b, at):
    return pl.pallas_call(
        functools.partial(merge_body, at),
        in_specs=[pl.BlockSpec(memory_space=VMEM)] * 2,
        out_specs=pl.BlockSpec(memory_space=VMEM),
        out_shape=jax.ShapeDtypeStruct(a.shape, jnp.float32),
        compiler_params=params(),
        cost_estimate=cost(),
        name="merge",
    )(a, b)


def join_body(ats, order, *refs):
    refs, out_ref = list(refs[:-1]), refs[-1]
    half = out_ref.shape[0] // 2
    at = upper_half(order) * half
    for j, place in enumerate((at, half - at)):
        total = None
        for i in ats[j]:
            term = part_of(refs.pop(0), i)
            total = term if total is None else total + term
        out_ref[pl.ds(pl.multiple_of(place, half), half), :] = total.astype(out_ref.dtype)


def join_rows(upper, lower, span_order):
    rows, width = upper[0][0].shape
    ats = [[at for _, at in terms] for terms in (upper, lower)]
    blocks = [block for block, _ in upper + lower]
    return pl.pallas_call(
        functools.partial(join_body, ats),
        in_specs=[pl.BlockSpec(memory_space=pltpu.SMEM)]
        + [pl.BlockSpec(memory_space=VMEM)] * len(blocks),
        out_specs=pl.BlockSpec(memory_space=VMEM),
        out_shape=jax.ShapeDtypeStruct((2 * rows, width), jnp.bfloat16),
        compiler_params=params(),
        cost_estimate=cost(),
        name="join_rows",
    )(span_order, *blocks)


def find_places(order, places, me, spans):
    for i in range(spans):
        k = (i // 2) ^ me
        places[order[i]] = (k % 2) * (spans // 2) + (k // 2) * 2 + (i % 2)


def own_span(order, lengths, docs, me, j, half):
    span = order[2 * me + j]
    position = span * half + lax.broadcasted_iota(jnp.int32, (1, half), 1)
    first, end = 0, 0
    start = jnp.zeros((1, half), jnp.int32)
    for k in range(docs):
        end = end + lengths[k]
        start = jnp.where(position >= end, end, start)
        first = jnp.where(span * half >= end, end, first)
    return span, position, start, first // half


def stack_heads(ref, rows, group, share, dim):
    base = group * share
    return jnp.concatenate(
        [ref[rows, (base + h) * dim : (base + h + 1) * dim] for h in range(share)], axis=0
    )


def load_blocks(refs, held):
    rows = refs[0].shape[0]
    for k, ref in enumerate(refs):
        held[k * rows : (k + 1) * rows, :] = ref[...]


def span_group(i, span, held, places, half, count):
    numbers = [span - count * i - j for j in range(count - 1, -1, -1)]
    known = [jnp.maximum(p, 0) for p in numbers]
    at = [pl.multiple_of(places[p] * half, half) for p in known]
    block = jnp.concatenate([held[pl.ds(place, half), :] for place in at], axis=0)
    key = numbers[0] * half + lax.broadcasted_iota(jnp.int32, (count * half, 1), 0)
    return known, block, key


def keep(allowed, x, other):
    width = allowed.shape[1]
    return jnp.concatenate(
        [
            jnp.where(allowed, x[:, i : i + width], other)
            for i in range(0, x.shape[1], width)
        ],
        axis=1,
    )


def stats_body(sizes, upper, spare, order, lengths, q_ref, *refs):
    peers, half, groups, share, dim, docs = sizes
    if upper:
        w_ref, level_ref, mixed_ref, w, held, kept, places, sems = refs[peers:]
    else:
        held, w_ref, level_ref, mixed_ref, w, kept, places, sems = refs
    copies = fetch_columns(spare, w_ref, w, sems)
    if upper:
        load_blocks(refs[:peers], held)
    me = lax.axis_index("ctx")
    width = groups * dim
    factor = math.log2(math.e) / math.sqrt(dim)
    find_places(order, places, me, 2 * peers)
    columns = share * half
    at = upper_half(order)
    j = at if upper else 1 - at
    span, position, start, lowest = own_span(order, lengths, docs, me, j, half)
    rows = pl.ds(pl.multiple_of(j * half, half), half)
    queries = [stack_heads(q_ref, rows, g, share, dim) for g in range(groups)]

    deep = AT_ONCE * half
    steps = (span - lowest) // AT_ONCE + 1

    def score(i, carry):
        known, block, key = span_group(i, span, held, places, half, AT_ONCE)
        allowed = (key <= position) & (key >= start)
        fresh = []
        for g in range(groups):
            logits = keep(allowed, mm_nt(block[:, g * dim : (g + 1) * dim], queries[g]), masked_score)
            kept[g, pl.ds(pl.multiple_of(i * deep, deep), deep), :] = logits
            high = jnp.max(logits.reshape(deep // 8, 8, columns), axis=0)
            fresh.append(jnp.maximum(carry[g], high))
        return tuple(fresh)

    empty = jnp.full((8, columns), masked_score, jnp.float32)
    tops = lax.fori_loop(0, steps, score, (empty,) * groups)
    tops = [jnp.max(top, axis=0, keepdims=True) for top in tops]

    def mix(i, carry):
        known, block, key = span_group(i, span, held, places, half, AT_ONCE)
        fresh = []
        for g in range(groups):
            total, mixed = carry[g]
            values = block[:, width + g * dim : width + (g + 1) * dim]
            logits = kept[g, pl.ds(pl.multiple_of(i * deep, deep), deep), :]
            weights = jnp.exp2((logits - tops[g]) * factor)
            total = total + jnp.sum(weights.reshape(deep // 8, 8, columns), axis=0)
            mixed = mixed + mm_tn(values, weights.astype(jnp.bfloat16))
            fresh.append((total, mixed))
        return tuple(fresh)

    empty = (jnp.zeros((8, columns), jnp.float32), jnp.zeros((dim, columns), jnp.float32))
    done = lax.fori_loop(0, steps, mix, (empty,) * groups)
    for g in range(groups):
        top, (total, mixed) = tops[g], done[g]
        total = jnp.sum(total, axis=0, keepdims=True)
        level_ref[g, 0:1] = top
        level_ref[g, 1:2] = jnp.log2(total)
        mixed_ref[g] = mixed / total
    for copy in copies:
        copy.wait()


def stats(upper, q, *args):
    *blocks, w, span_order, doc_lengths, sizes = args
    heads = lax.axis_size("head")
    spare = list(range(heads))[: heads // 2] if upper else list(range(heads))[heads // 2 :]
    peers, half, groups, share, dim, docs = sizes
    columns = share * half
    return pl.pallas_call(
        functools.partial(stats_body, sizes, upper, spare),
        in_specs=[pl.BlockSpec(memory_space=pltpu.SMEM)] * 2
        + [pl.BlockSpec(memory_space=VMEM)] * (1 + len(blocks))
        + [pl.BlockSpec(memory_space=HBM)],
        out_specs=[pl.BlockSpec(memory_space=VMEM)] * (4 if upper else 3),
        out_shape=[
            jax.ShapeDtypeStruct((groups, 2, columns), jnp.float32),
            jax.ShapeDtypeStruct((groups, dim, columns), jnp.float32),
            jax.ShapeDtypeStruct((len(spare), w.shape[0], w.shape[1] // heads), w.dtype),
        ]
        + [jax.ShapeDtypeStruct((2 * peers * half, 2 * groups * dim), jnp.bfloat16)] * upper,
        scratch_shapes=[
            VMEM((groups, (2 * peers + AT_ONCE) * half, columns), jnp.float32),
            pltpu.SMEM((2 * peers,), jnp.int32),
            pltpu.SemaphoreType.DMA((len(spare),)),
        ],
        compiler_params=params(),
        cost_estimate=cost(),
        name="upper_stats" if upper else "lower_stats",
    )(span_order, doc_lengths, q, *blocks, in_hbm(w))


def grads_body(sizes, upper, spare, order, lengths, q_ref, g_ref, level_ref, mixed_ref, *refs):
    peers, half, groups, share, dim, docs = sizes
    spans = 2 * peers
    count = 3 if upper else AT_ONCE
    if upper:
        held, wq_ref, wk_ref, wv_ref, dq_ref, even_ref, *odd_refs, sums, wq, wk, wv, places, sems = refs
    else:
        rest_ref, held, wq_ref, wk_ref, wv_ref, dq_ref, even_ref, *odd_refs, wq, wk, wv, sums, places, sems = refs
    copies = []
    for i, (w_ref, w) in enumerate(((wq_ref, wq), (wk_ref, wk), (wv_ref, wv))):
        copies += fetch_rows(spare, w_ref, w, sems, i)
    me = lax.axis_index("ctx")
    width = groups * dim
    scale = 1.0 / math.sqrt(dim)
    factor = math.log2(math.e) * scale
    find_places(order, places, me, spans)
    columns = share * half
    at = upper_half(order)
    j = at if upper else 1 - at
    span, position, start, lowest = own_span(order, lengths, docs, me, j, half)
    steps = (span - lowest) // count + 1

    def fill(p, carry):
        target = pl.ds(pl.multiple_of(p * half, half), half)
        if upper:
            sums[target, :] = jnp.zeros((half, 2 * width), jnp.float32)
        else:
            sums[target, :] = rest_ref[target, :]
        return carry

    lax.fori_loop(0, jnp.maximum(span - count * steps + 1, 0), fill, 0)
    lax.fori_loop(span + 1, sums.shape[0] // half, fill, 0)
    rows = pl.ds(pl.multiple_of(j * half, half), half)
    queries = [stack_heads(q_ref, rows, g, share, dim) for g in range(groups)]
    outs = [stack_heads(g_ref, rows, g, share, dim) for g in range(groups)]
    tops = [level_ref[g, 0:1] for g in range(groups)]
    levels = [level_ref[g, 1:2] for g in range(groups)]
    deltas = []
    for g in range(groups):
        turned = jnp.concatenate(
            [outs[g][h * half : (h + 1) * half].astype(jnp.float32).T for h in range(share)],
            axis=1,
        )
        deltas.append(jnp.sum(turned * mixed_ref[g], axis=0, keepdims=True))

    def visit(i, carry):
        known, block, key = span_group(i, span, held, places, half, count)
        allowed = (key <= position) & (key >= start)
        targets = [pl.ds(pl.multiple_of(p * half, half), half) for p in known]
        fresh = []
        for g in range(groups):
            keys = block[:, g * dim : (g + 1) * dim]
            values = block[:, width + g * dim : width + (g + 1) * dim]
            logits = mm_nt(keys, queries[g])
            chance = keep(allowed, jnp.exp2((logits - tops[g]) * factor - levels[g]), 0.0)
            slopes = mm_nt(values, outs[g])
            score = (chance * (slopes - deltas[g])).astype(jnp.bfloat16)
            key_term = mm(score, queries[g])
            value_term = mm(chance.astype(jnp.bfloat16), outs[g])
            for j, target in enumerate(targets):
                part = slice(j * half, (j + 1) * half)
                for at, term in ((g * dim, key_term[part]), (width + g * dim, value_term[part])):
                    columns_at = slice(at, at + dim)
                    if not upper:
                        term = term + rest_ref[target, columns_at]
                    sums[target, columns_at] = term
            fresh.append(carry[g] + mm_tn(keys, score))
        return tuple(fresh)

    empty = jnp.zeros((dim, columns), jnp.float32)
    done = lax.fori_loop(0, steps, visit, (empty,) * groups)
    for g in range(groups):
        for h in range(share):
            head = g * share + h
            dq_ref[:, head * dim : (head + 1) * dim] = (
                (done[g][:, h * half : (h + 1) * half].T * scale).astype(dq_ref.dtype)
            )
    for k in range(peers):
        out, slot = even_ref, k // 2
        if k % 2:
            out, slot = odd_refs[slot // odd_refs[0].shape[0]], slot % odd_refs[0].shape[0]
        first = order[2 * (me ^ k)]
        other = spans - 1 - first
        pick = jnp.maximum(first, other) if upper else jnp.minimum(first, other)
        part = pl.ds(pl.multiple_of(pick * half, half), half)
        out[slot, :, :width] = (sums[part, :width] * scale).astype(out.dtype)
        out[slot, :, width:] = sums[part, width:].astype(out.dtype)
    for copy in copies:
        copy.wait()


def grads(upper, q, g, level, mixed, *args):
    *blocks, span_order, doc_lengths, sizes = args
    heads = lax.axis_size("head")
    spare = list(range(heads - (2 if upper else 1), -1, -2))
    weights, blocks = [in_hbm(w) for w in blocks[-3:]], blocks[:-3]
    scratch = [pltpu.SemaphoreType.DMA((len(spare), 3))]
    peers, half, groups, share, dim, docs = sizes
    tokens, width = 2 * half, groups * dim
    columns = share * half
    terms = jax.ShapeDtypeStruct((peers // 2, half, 2 * width), jnp.bfloat16)
    odds = jax.ShapeDtypeStruct((peers // 4, half, 2 * width), jnp.bfloat16)
    rests = jax.ShapeDtypeStruct((peers * tokens, 2 * width), jnp.float32)
    outs = [jax.ShapeDtypeStruct((half, g.shape[1]), jnp.bfloat16), terms, odds, odds] + [rests] * upper
    outs += [rows_shape(spare, w, heads) for w in weights]
    return pl.pallas_call(
        functools.partial(grads_body, sizes, upper, spare),
        in_specs=[pl.BlockSpec(memory_space=pltpu.SMEM)] * 2
        + [pl.BlockSpec(memory_space=VMEM)] * (4 + len(blocks))
        + [pl.BlockSpec(memory_space=HBM)] * len(weights),
        out_specs=[pl.BlockSpec(memory_space=VMEM)] * len(outs),
        out_shape=outs,
        scratch_shapes=[VMEM((peers * half, 2 * width), jnp.float32)] * (not upper)
        + [
            pltpu.SMEM((2 * peers,), jnp.int32),
        ]
        + scratch,
        compiler_params=params(),
        cost_estimate=cost(),
        name="upper_grads" if upper else "lower_grads",
    )(span_order, doc_lengths, q, g, level, mixed, *blocks, *weights)


def swap(x, k, axis):
    return lax.ppermute(x, axis, [(i, i ^ k) for i in range(lax.axis_size(axis))])


def gather_even(x, axis, held):
    size = lax.axis_size(axis)
    got, bit = {0: x}, 2
    while bit < size:
        passed = {k: block for k, block in got.items() if k}
        passed, held = lax.optimization_barrier((passed, held))
        got |= {bit: swap(x, bit, axis)}
        got |= {k ^ bit: swap(block, bit, axis) for k, block in passed.items()}
        bit *= 2
    return [got[k] for k in sorted(got)], held


def pair_body(even_ref, *refs):
    count = even_ref.shape[0]
    odd_refs, outs = refs[:-count], refs[-count:]
    part = odd_refs[0].shape[0]
    for k, out in enumerate(outs):
        total = even_ref[k].astype(jnp.float32) + odd_refs[k // part][k % part].astype(jnp.float32)
        out[...] = total.astype(out.dtype)


def pair_sums(even, *got):
    count, rows, width = even.shape
    return pl.pallas_call(
        pair_body,
        in_specs=[pl.BlockSpec(memory_space=VMEM)] * (1 + len(got)),
        out_specs=[pl.BlockSpec(memory_space=VMEM)] * count,
        out_shape=[jax.ShapeDtypeStruct((rows, width), jnp.bfloat16)] * count,
        compiler_params=params(),
        cost_estimate=cost(),
        name="pair_sums",
    )(even, *got)


def scatter_ctx(pairs):
    return [part if k == 0 else swap(part, 2 * k, "ctx") for k, part in enumerate(pairs)]


def shards(inputs, out_grad, w_query, w_key, value_projection, w_out, doc_lengths, span_order):
    tokens = inputs.shape[0]
    share = ASKER_NUM // SHARED_KV_NUM
    half = tokens // 2
    sizes = (
        lax.axis_size("ctx"),
        tokens // 2,
        w_key.shape[1] // CHANNEL_DIM,
        share,
        CHANNEL_DIM,
        doc_lengths.shape[0],
    )
    heads = lax.axis_size("head")
    last = [span_order]

    def turn(call, *args):
        held, *args = lax.optimization_barrier((last[0], *args))
        out = call(*args)
        last[0] = out if hasattr(out, "shape") else out[0]
        return out

    def attend(upper, call, *args):
        return turn(lambda *a: call(upper, *a, span_order, doc_lengths, sizes), *args)

    def context(blocks, stacks, spans, total, dtype):
        shape = jax.tree.structure((blocks, stacks, total))

        def call(*flat):
            parts, weights, given = jax.tree.unflatten(shape, flat)
            return back_project(parts, weights, spans, given, dtype)

        return turn(call, *jax.tree.leaves((blocks, stacks, total)))

    def send_first(parts, stack, places=None):
        if stack is None:
            return {k ^ 1: (swap(parts[k], 1, "head"), None) for k in places} | {0: None}
        places = range(heads - 1, 0, -2)
        got = swap(stack, 1, "head")
        return {k ^ 1: (got, i) for i, k in enumerate(places)}

    def send_rest(parts, got):
        ends, bit = [(parts[0], None), got[0]], 2
        parts = {
            k: turn(lambda a, b, at=got[k][1]: add(a, b, at), parts[k], got[k][0])
            for k in range(2, heads, 2)
        }
        while bit < heads:
            moved = {k ^ bit: swap(parts[k], bit, "head") for k in parts if k & bit}
            ends.append((moved.pop(0), None))
            parts = {k: turn(lambda a, b: add(a, b, None), parts[k], moved[k]) for k in moved}
            bit *= 2
        return ends

    far = [{0: out_grad[:half]}, {0: out_grad[half:]}]
    bit = heads // 2
    while bit > 1:
        far = [got | {k ^ bit: swap(x, bit, "head") for k, x in got.items()} for got in far]
        bit //= 2
    near = [swap(out_grad[:half], 1, "head"), swap(out_grad[half:], 1, "head")]
    own = turn(project_kv, inputs, w_key, value_projection)
    near_blocks, (far[0], near[0]) = gather_even(own, "ctx", (far[0], near[0]))
    query = turn(project, inputs, w_query)
    query, near_blocks = lax.optimization_barrier((query, near_blocks))
    blocks = (*near_blocks, *[swap(block, 1, "ctx") for block in near_blocks])
    query, far[1], near[1] = lax.optimization_barrier((query, far[1], near[1]))
    *upper_stats, w_first, held = attend(True, stats, query, *blocks, w_out)
    *lower_stats, w_second = attend(False, stats, query, held, w_out)
    passed = [{k ^ 1: swap(x, 1, "head") for k, x in got.items() if k} for got in far]
    come = {0: (out_grad,), 1: tuple(near)}
    come |= {k: (far[0][k], far[1][k]) for k in range(2, heads, 2)}
    come |= {k: (passed[0][k], passed[1][k]) for k in range(3, heads, 2)}
    blocks = [come[k] for k in range(heads)]
    mid = heads // 2
    total = context(
        blocks[:-1], (w_first, w_second), [(0, mid), (0, mid - 1)], None, jnp.float32
    )
    context_grad = context(blocks[-1:], (w_second,), [(mid - 1, mid)], total, jnp.bfloat16)
    weights = (w_query, w_key, value_projection)
    upper_dq, even, *odd, rest, stay_q, stay_k, stay_v = attend(
        True, grads, query, context_grad, *upper_stats, held, *weights
    )
    upper = scatter_ctx(turn(pair_sums, even, *[swap(x, 1, "ctx") for x in odd]))
    lower_dq, even, *odd, wq, wk, wv = attend(
        False, grads, query, context_grad, *lower_stats, rest, held, *weights
    )
    sides = [list(range(heads - 1, 0, -2)), list(range(heads - 2, -1, -2))]
    weights = [(wq, wk, wv), (stay_q, stay_k, stay_v)]

    def firsts_of(side):
        return turn(
            lambda a, b, w: query_terms(a, b, w, heads, sides[side]),
            upper_dq,
            lower_dq,
            weights[side][0],
        )

    def terms_of(first, terms, side, stacked=False):
        outs = turn(
            lambda a, k, v, *b: all_terms(a, b, k, v, heads, sides[side], stacked),
            first,
            *weights[side][1:],
            *terms,
        )
        return outs[0] if stacked else dict(zip(sides[side], outs))

    first = [firsts_of(0)]
    lower_odd = [swap(x, 1, "ctx") for x in odd]
    upper_got = send_first(None, terms_of(first[0][0], upper, 0, True))
    lower = scatter_ctx(turn(pair_sums, even, *lower_odd))
    first.append(firsts_of(1))
    upper = terms_of(first[1][0], upper, 1)
    parts = terms_of(first[0][1], lower, 0)
    lower_got = send_first(parts, None, sides[0][:-1])
    upper = send_rest(upper, upper_got)
    lower = terms_of(first[1][1], lower, 1)
    lower = send_rest(lower, lower_got)
    stack, at = upper[1]
    upper = [(turn(lambda a, b: merge(a, b, at), upper[0][0], stack), None)] + upper[2:]
    last_part, held = lax.optimization_barrier((parts[1], last[0]))
    last_part = (swap(last_part, 1, "head"), None)
    total = upper[0][0]
    for block, at in upper[1:]:
        total = turn(lambda a, b: merge(a, b, None), total, block)
    upper = [(total, None)]
    total = lower[0][0]
    for block, at in lower[2:]:
        total = turn(lambda a, b: merge(a, b, None), total, block)
    lower = [(total, None), last_part]
    return join_rows(upper, lower, span_order)


def solution(mesh):
    in_specs = (
        P("ctx", None),
        P("ctx", "head"),
        P(None, "head"),
        P(None, "head"),
        P(None, "head"),
        P("head", None),
        P(),
        P(),
    )
    out_specs = P("ctx", "head")
    return jax.shard_map(shards, mesh=mesh, in_specs=in_specs, out_specs=out_specs, check_vma=False)
```

```python
import functools
import math

import jax
import jax.numpy as jnp
from jax import lax
from jax.experimental import pallas as pl
from jax.experimental.pallas import tpu as pltpu
from jax.sharding import PartitionSpec as P

ASKER_NUM = 32
SHARED_KV_NUM = 8
CHANNEL_DIM = 128

masked_score = -1e30
MIB = 1 << 20
AT_ONCE = 4
VMEM = pltpu.VMEM
HBM = pltpu.HBM


def mm(a, b):
    return lax.dot_general(a, b, (((1,), (0,)), ((), ())), preferred_element_type=jnp.float32)


def mm_nt(a, b):
    return lax.dot_general(a, b, (((1,), (1,)), ((), ())), preferred_element_type=jnp.float32)


def mm_tn(a, b):
    return lax.dot_general(a, b, (((0,), (0,)), ((), ())), preferred_element_type=jnp.float32)


def params():
    return pltpu.CompilerParams(vmem_limit_bytes=24 * MIB)


def cost():
    return pl.CostEstimate(flops=0, bytes_accessed=1, transcendentals=0)


def upper_half(order):
    first = order[2 * lax.axis_index("ctx")]
    return jnp.where(2 * first >= order.shape[0], 0, 1)


def in_hbm(x):
    return pltpu.with_memory_space_constraint(x, HBM)


def fetch(src, dst, sem):
    copy = pltpu.make_async_copy(src, dst, sem)
    copy.start()
    return copy


def kv_body(parts, x_ref, wk_ref, wv_ref, out_ref, x, wk, wv, acc, sems):
    width = wk.shape[1]
    depth = wk.shape[0] // parts
    copies = []
    for i in range(parts):
        rows = slice(i * depth, (i + 1) * depth)
        copies.append(
            [
                fetch(x_ref.at[:, rows], x.at[:, rows], sems.at[i, 0]),
                fetch(wk_ref.at[rows], wk.at[rows], sems.at[i, 1]),
                fetch(wv_ref.at[rows], wv.at[rows], sems.at[i, 2]),
            ]
        )
    for i in range(parts):
        rows = slice(i * depth, (i + 1) * depth)
        for copy in copies[i]:
            copy.wait()
        left = x[:, rows]
        terms = mm(left, wk[rows, :]), mm(left, wv[rows, :])
        for j, term in enumerate(terms):
            columns = slice(j * width, (j + 1) * width)
            total = term if i == 0 else acc[:, columns] + term
            if i < parts - 1:
                acc[:, columns] = total
            else:
                out_ref[:, columns] = total.astype(out_ref.dtype)


def project_kv(x, wk, wv):
    tokens, depth = x.shape
    width = wk.shape[1]
    parts = 4
    return pl.pallas_call(
        functools.partial(kv_body, parts),
        in_specs=[pl.BlockSpec(memory_space=HBM)] * 3,
        out_specs=pl.BlockSpec(memory_space=VMEM),
        out_shape=jax.ShapeDtypeStruct((tokens, 2 * width), jnp.bfloat16),
        scratch_shapes=[
            VMEM(x.shape, x.dtype),
            VMEM(wk.shape, wk.dtype),
            VMEM(wv.shape, wv.dtype),
            VMEM((tokens, 2 * width), jnp.float32),
            pltpu.SemaphoreType.DMA((parts, 3)),
        ],
        compiler_params=params(),
        cost_estimate=cost(),
        name="project_kv",
    )(in_hbm(x), in_hbm(wk), in_hbm(wv))


def project_body(parts, x_ref, w_ref, out_ref, x, w, acc, sems):
    depth = w.shape[0] // parts
    copies = []
    for i in range(parts):
        rows = slice(i * depth, (i + 1) * depth)
        copies.append(
            [
                fetch(x_ref.at[:, rows], x.at[:, rows], sems.at[i, 0]),
                fetch(w_ref.at[rows], w.at[rows], sems.at[i, 1]),
            ]
        )
    for i in range(parts):
        rows = slice(i * depth, (i + 1) * depth)
        for copy in copies[i]:
            copy.wait()
        total = mm(x[:, rows], w[rows, :])
        if i:
            total = acc[...] + total
        if i < parts - 1:
            acc[...] = total
        else:
            out_ref[...] = total.astype(out_ref.dtype)


def project(x, w):
    tokens, depth = x.shape
    width = w.shape[1]
    parts = 4
    return pl.pallas_call(
        functools.partial(project_body, parts),
        in_specs=[pl.BlockSpec(memory_space=HBM)] * 2,
        out_specs=pl.BlockSpec(memory_space=VMEM),
        out_shape=jax.ShapeDtypeStruct((tokens, width), jnp.bfloat16),
        scratch_shapes=[
            VMEM(x.shape, x.dtype),
            VMEM(w.shape, w.dtype),
            VMEM((tokens, width), jnp.float32),
            pltpu.SemaphoreType.DMA((parts, 2)),
        ],
        compiler_params=params(),
        cost_estimate=cost(),
        name="project",
    )(in_hbm(x), in_hbm(w))


def back_body(given, rows, spans, *refs):
    refs, out_ref = list(refs[:-1]), refs[-1]
    total = refs.pop(0)[...] if given else None
    stacks = [refs.pop() for _ in spans][::-1]
    for w, (low, high) in zip(stacks, spans):
        for i in range(low, high):
            x = refs.pop(0)[...]
            if x.shape[0] < rows:
                x = jnp.concatenate([x, refs.pop(0)[...]], axis=0)
            term = mm_nt(x, w[i])
            total = term if total is None else total + term
    out_ref[...] = total.astype(out_ref.dtype)


def back_project(blocks, stacks, spans, total, dtype):
    rows = blocks[0][0].shape[0] * len(blocks[0])
    given = [] if total is None else [total]
    flat = [x for block in blocks for x in block]
    operands = (*given, *flat, *stacks)
    return pl.pallas_call(
        functools.partial(back_body, len(given), rows, spans),
        in_specs=[pl.BlockSpec(memory_space=VMEM)] * len(operands),
        out_specs=pl.BlockSpec(memory_space=VMEM),
        out_shape=jax.ShapeDtypeStruct((rows, stacks[0].shape[1]), dtype),
        compiler_params=params(),
        cost_estimate=cost(),
        name="context_grad",
    )(*operands)


def fetch_columns(places, ref, out, sems):
    me = lax.axis_index("head")
    depth = out.shape[2]
    return [
        fetch(ref.at[:, pl.ds(pl.multiple_of((me ^ k) * depth, depth), depth)], out.at[i], sems.at[i])
        for i, k in enumerate(places)
    ]


def fetch_rows(places, ref, out, sems, at):
    me = lax.axis_index("head")
    share = out.shape[1]
    return [
        fetch(ref.at[pl.ds(pl.multiple_of((me ^ k) * share, share), share)], out.at[i], sems.at[i, at])
        for i, k in enumerate(places)
    ]


def rows_shape(places, w, heads):
    return jax.ShapeDtypeStruct((len(places), w.shape[0] // heads, w.shape[1]), w.dtype)


def query_terms_body(places, upper_ref, lower_ref, w_ref, *refs):
    upper_out, lower_out = refs[:2]
    copies, w = [], w_ref
    if places is not None:
        w, sems = refs[2:]
        copies = fetch_rows(places, w_ref, w, sems, 0)
    half = upper_ref.shape[0]
    x = jnp.concatenate([upper_ref[...], lower_ref[...]], axis=0)
    for i in range(w.shape[0]):
        if copies:
            copies[i].wait()
        total = mm_nt(x, w[i])
        upper_out[i] = total[:half]
        lower_out[i] = total[half:]


def query_terms(upper, lower, w, heads, places):
    rows, depth = upper.shape
    scratch = []
    shape = w
    if w.ndim == 2:
        shape = rows_shape(places, w, heads)
        scratch = [VMEM(shape.shape, w.dtype), pltpu.SemaphoreType.DMA((len(places), 1))]
        w = in_hbm(w)
    else:
        places = None
    size, share = shape.shape[:2]
    return pl.pallas_call(
        functools.partial(query_terms_body, places),
        in_specs=[pl.BlockSpec(memory_space=VMEM)] * 2
        + [pl.BlockSpec(memory_space=HBM if scratch else VMEM)],
        out_specs=[pl.BlockSpec(memory_space=VMEM)] * 2,
        out_shape=[jax.ShapeDtypeStruct((size, rows, share), jnp.float32)] * 2,
        scratch_shapes=scratch,
        compiler_params=params(),
        cost_estimate=cost(),
        name="query_terms",
    )(upper, lower, w)


def all_terms_body(places, count, first_ref, *refs):
    terms, (wk_ref, wv_ref), refs = refs[:count], refs[count : count + 2], refs[count + 2 :]
    wk, wv, copies = wk_ref, wv_ref, []
    if places is not None:
        refs, (wk, wv, sems) = refs[:-3], refs[-3:]
        copies = [fetch_rows(places, wk_ref, wk, sems, 0), fetch_rows(places, wv_ref, wv, sems, 1)]
    outs = refs
    width = wk.shape[2]
    grads = terms[0][...].astype(jnp.float32)
    for term in terms[1:]:
        grads = grads + term[...].astype(jnp.float32)
    grads = grads.astype(jnp.bfloat16)
    for i in range(wk.shape[0]):
        for some in copies:
            some[i].wait()
        total = first_ref[i] + mm_nt(grads[:, :width], wk[i])
        total = total + mm_nt(grads[:, width:], wv[i])
        if len(outs) == 1:
            outs[0][i] = total.astype(outs[0].dtype)
        else:
            outs[i][...] = total.astype(outs[i].dtype)


def all_terms(first, terms, wk, wv, heads, places, stacked):
    size, rows, share = first.shape
    scratch = []
    if wk.ndim == 2:
        shape = rows_shape(places, wk, heads).shape
        scratch = [
            VMEM(shape, wk.dtype),
            VMEM(shape, wv.dtype),
            pltpu.SemaphoreType.DMA((size, 2)),
        ]
        wk, wv = in_hbm(wk), in_hbm(wv)
    else:
        places = None
    return pl.pallas_call(
        functools.partial(all_terms_body, places, len(terms)),
        in_specs=[pl.BlockSpec(memory_space=VMEM)] * (1 + len(terms))
        + [pl.BlockSpec(memory_space=HBM if scratch else VMEM)] * 2,
        out_specs=[pl.BlockSpec(memory_space=VMEM)] * (1 if stacked else size),
        out_shape=[jax.ShapeDtypeStruct((size, rows, share), jnp.bfloat16)]
        if stacked
        else [jax.ShapeDtypeStruct((rows, share), jnp.bfloat16)] * size,
        scratch_shapes=scratch,
        compiler_params=params(),
        cost_estimate=cost(),
        name="all_terms",
    )(first, *terms, wk, wv)


def part_of(ref, at):
    return (ref[...] if at is None else ref[at]).astype(jnp.float32)


def add_body(at, a_ref, b_ref, out_ref):
    out_ref[...] = (a_ref[...].astype(jnp.float32) + part_of(b_ref, at)).astype(out_ref.dtype)


def add(a, b, at):
    return pl.pallas_call(
        functools.partial(add_body, at),
        in_specs=[pl.BlockSpec(memory_space=VMEM)] * 2,
        out_specs=pl.BlockSpec(memory_space=VMEM),
        out_shape=jax.ShapeDtypeStruct(a.shape, a.dtype),
        compiler_params=params(),
        cost_estimate=cost(),
        name="add",
    )(a, b)


def merge_body(at, a_ref, b_ref, out_ref):
    out_ref[...] = a_ref[...].astype(jnp.float32) + part_of(b_ref, at)


def merge(a, b, at):
    return pl.pallas_call(
        functools.partial(merge_body, at),
        in_specs=[pl.BlockSpec(memory_space=VMEM)] * 2,
        out_specs=pl.BlockSpec(memory_space=VMEM),
        out_shape=jax.ShapeDtypeStruct(a.shape, jnp.float32),
        compiler_params=params(),
        cost_estimate=cost(),
        name="merge",
    )(a, b)


def join_body(ats, order, *refs):
    refs, out_ref = list(refs[:-1]), refs[-1]
    half = out_ref.shape[0] // 2
    at = upper_half(order) * half
    for j, place in enumerate((at, half - at)):
        total = None
        for i in ats[j]:
            term = part_of(refs.pop(0), i)
            total = term if total is None else total + term
        out_ref[pl.ds(pl.multiple_of(place, half), half), :] = total.astype(out_ref.dtype)


def join_rows(upper, lower, span_order):
    rows, width = upper[0][0].shape
    ats = [[at for _, at in terms] for terms in (upper, lower)]
    blocks = [block for block, _ in upper + lower]
    return pl.pallas_call(
        functools.partial(join_body, ats),
        in_specs=[pl.BlockSpec(memory_space=pltpu.SMEM)]
        + [pl.BlockSpec(memory_space=VMEM)] * len(blocks),
        out_specs=pl.BlockSpec(memory_space=VMEM),
        out_shape=jax.ShapeDtypeStruct((2 * rows, width), jnp.bfloat16),
        compiler_params=params(),
        cost_estimate=cost(),
        name="join_rows",
    )(span_order, *blocks)


def find_places(order, places, me, spans):
    for i in range(spans):
        k = (i // 2) ^ me
        places[order[i]] = (k % 2) * (spans // 2) + (k // 2) * 2 + (i % 2)


def own_span(order, lengths, docs, me, j, half):
    span = order[2 * me + j]
    position = span * half + lax.broadcasted_iota(jnp.int32, (1, half), 1)
    first, end = 0, 0
    start = jnp.zeros((1, half), jnp.int32)
    for k in range(docs):
        end = end + lengths[k]
        start = jnp.where(position >= end, end, start)
        first = jnp.where(span * half >= end, end, first)
    return span, position, start, first // half


def stack_heads(ref, rows, group, share, dim):
    base = group * share
    return jnp.concatenate(
        [ref[rows, (base + h) * dim : (base + h + 1) * dim] for h in range(share)], axis=0
    )


def load_blocks(refs, held):
    rows = refs[0].shape[0]
    for k, ref in enumerate(refs):
        held[k * rows : (k + 1) * rows, :] = ref[...]


def span_group(i, span, held, places, half, count):
    numbers = [span - count * i - j for j in range(count - 1, -1, -1)]
    known = [jnp.maximum(p, 0) for p in numbers]
    at = [pl.multiple_of(places[p] * half, half) for p in known]
    block = jnp.concatenate([held[pl.ds(place, half), :] for place in at], axis=0)
    key = numbers[0] * half + lax.broadcasted_iota(jnp.int32, (count * half, 1), 0)
    return known, block, key


def keep(allowed, x, other):
    width = allowed.shape[1]
    return jnp.concatenate(
        [
            jnp.where(allowed, x[:, i : i + width], other)
            for i in range(0, x.shape[1], width)
        ],
        axis=1,
    )


def stats_body(sizes, upper, spare, order, lengths, q_ref, *refs):
    peers, half, groups, share, dim, docs = sizes
    if upper:
        w_ref, level_ref, mixed_ref, w, held, kept, places, sems = refs[peers:]
    else:
        held, w_ref, level_ref, mixed_ref, w, kept, places, sems = refs
    copies = fetch_columns(spare, w_ref, w, sems)
    if upper:
        load_blocks(refs[:peers], held)
    me = lax.axis_index("ctx")
    width = groups * dim
    factor = math.log2(math.e) / math.sqrt(dim)
    find_places(order, places, me, 2 * peers)
    columns = share * half
    at = upper_half(order)
    j = at if upper else 1 - at
    span, position, start, lowest = own_span(order, lengths, docs, me, j, half)
    rows = pl.ds(pl.multiple_of(j * half, half), half)
    queries = [stack_heads(q_ref, rows, g, share, dim) for g in range(groups)]

    deep = AT_ONCE * half
    steps = (span - lowest) // AT_ONCE + 1

    def score(i, carry):
        known, block, key = span_group(i, span, held, places, half, AT_ONCE)
        allowed = (key <= position) & (key >= start)
        fresh = []
        for g in range(groups):
            logits = keep(allowed, mm_nt(block[:, g * dim : (g + 1) * dim], queries[g]), masked_score)
            kept[g, pl.ds(pl.multiple_of(i * deep, deep), deep), :] = logits
            high = jnp.max(logits.reshape(deep // 8, 8, columns), axis=0)
            fresh.append(jnp.maximum(carry[g], high))
        return tuple(fresh)

    empty = jnp.full((8, columns), masked_score, jnp.float32)
    tops = lax.fori_loop(0, steps, score, (empty,) * groups)
    tops = [jnp.max(top, axis=0, keepdims=True) for top in tops]

    def mix(i, carry):
        known, block, key = span_group(i, span, held, places, half, AT_ONCE)
        fresh = []
        for g in range(groups):
            total, mixed = carry[g]
            values = block[:, width + g * dim : width + (g + 1) * dim]
            logits = kept[g, pl.ds(pl.multiple_of(i * deep, deep), deep), :]
            weights = jnp.exp2((logits - tops[g]) * factor)
            total = total + jnp.sum(weights.reshape(deep // 8, 8, columns), axis=0)
            mixed = mixed + mm_tn(values, weights.astype(jnp.bfloat16))
            fresh.append((total, mixed))
        return tuple(fresh)

    empty = (jnp.zeros((8, columns), jnp.float32), jnp.zeros((dim, columns), jnp.float32))
    done = lax.fori_loop(0, steps, mix, (empty,) * groups)
    for g in range(groups):
        top, (total, mixed) = tops[g], done[g]
        total = jnp.sum(total, axis=0, keepdims=True)
        level_ref[g, 0:1] = top
        level_ref[g, 1:2] = jnp.log2(total)
        mixed_ref[g] = mixed / total
    for copy in copies:
        copy.wait()


def stats(upper, q, *args):
    *blocks, w, span_order, doc_lengths, sizes = args
    heads = lax.axis_size("head")
    spare = list(range(heads))[: heads // 2] if upper else list(range(heads))[heads // 2 :]
    peers, half, groups, share, dim, docs = sizes
    columns = share * half
    return pl.pallas_call(
        functools.partial(stats_body, sizes, upper, spare),
        in_specs=[pl.BlockSpec(memory_space=pltpu.SMEM)] * 2
        + [pl.BlockSpec(memory_space=VMEM)] * (1 + len(blocks))
        + [pl.BlockSpec(memory_space=HBM)],
        out_specs=[pl.BlockSpec(memory_space=VMEM)] * (4 if upper else 3),
        out_shape=[
            jax.ShapeDtypeStruct((groups, 2, columns), jnp.float32),
            jax.ShapeDtypeStruct((groups, dim, columns), jnp.float32),
            jax.ShapeDtypeStruct((len(spare), w.shape[0], w.shape[1] // heads), w.dtype),
        ]
        + [jax.ShapeDtypeStruct((2 * peers * half, 2 * groups * dim), jnp.bfloat16)] * upper,
        scratch_shapes=[
            VMEM((groups, (2 * peers + AT_ONCE) * half, columns), jnp.float32),
            pltpu.SMEM((2 * peers,), jnp.int32),
            pltpu.SemaphoreType.DMA((len(spare),)),
        ],
        compiler_params=params(),
        cost_estimate=cost(),
        name="upper_stats" if upper else "lower_stats",
    )(span_order, doc_lengths, q, *blocks, in_hbm(w))


def grads_body(sizes, upper, spare, order, lengths, q_ref, g_ref, level_ref, mixed_ref, *refs):
    peers, half, groups, share, dim, docs = sizes
    spans = 2 * peers
    count = 3 if upper else AT_ONCE
    if upper:
        held, dq_ref, even_ref, *odd_refs, sums, places = refs
    else:
        rest_ref, held, wq_ref, wk_ref, wv_ref, dq_ref, even_ref, *odd_refs, wq, wk, wv, sums, places, sems = refs
        copies = []
        for i, (w_ref, w) in enumerate(((wq_ref, wq), (wk_ref, wk), (wv_ref, wv))):
            copies += fetch_rows(spare, w_ref, w, sems, i)
    me = lax.axis_index("ctx")
    width = groups * dim
    scale = 1.0 / math.sqrt(dim)
    factor = math.log2(math.e) * scale
    find_places(order, places, me, spans)
    columns = share * half
    at = upper_half(order)
    j = at if upper else 1 - at
    span, position, start, lowest = own_span(order, lengths, docs, me, j, half)
    steps = (span - lowest) // count + 1

    def fill(p, carry):
        target = pl.ds(pl.multiple_of(p * half, half), half)
        if upper:
            sums[target, :] = jnp.zeros((half, 2 * width), jnp.float32)
        else:
            sums[target, :] = rest_ref[target, :]
        return carry

    lax.fori_loop(0, jnp.maximum(span - count * steps + 1, 0), fill, 0)
    lax.fori_loop(span + 1, sums.shape[0] // half, fill, 0)
    rows = pl.ds(pl.multiple_of(j * half, half), half)
    queries = [stack_heads(q_ref, rows, g, share, dim) for g in range(groups)]
    outs = [stack_heads(g_ref, rows, g, share, dim) for g in range(groups)]
    tops = [level_ref[g, 0:1] for g in range(groups)]
    levels = [level_ref[g, 1:2] for g in range(groups)]
    deltas = []
    for g in range(groups):
        turned = jnp.concatenate(
            [outs[g][h * half : (h + 1) * half].astype(jnp.float32).T for h in range(share)],
            axis=1,
        )
        deltas.append(jnp.sum(turned * mixed_ref[g], axis=0, keepdims=True))

    def visit(i, carry):
        known, block, key = span_group(i, span, held, places, half, count)
        allowed = (key <= position) & (key >= start)
        targets = [pl.ds(pl.multiple_of(p * half, half), half) for p in known]
        fresh = []
        for g in range(groups):
            keys = block[:, g * dim : (g + 1) * dim]
            values = block[:, width + g * dim : width + (g + 1) * dim]
            logits = mm_nt(keys, queries[g])
            chance = keep(allowed, jnp.exp2((logits - tops[g]) * factor - levels[g]), 0.0)
            slopes = mm_nt(values, outs[g])
            score = (chance * (slopes - deltas[g])).astype(jnp.bfloat16)
            key_term = mm(score, queries[g])
            value_term = mm(chance.astype(jnp.bfloat16), outs[g])
            for j, target in enumerate(targets):
                part = slice(j * half, (j + 1) * half)
                for at, term in ((g * dim, key_term[part]), (width + g * dim, value_term[part])):
                    columns_at = slice(at, at + dim)
                    if not upper:
                        term = term + rest_ref[target, columns_at]
                    sums[target, columns_at] = term
            fresh.append(carry[g] + mm_tn(keys, score))
        return tuple(fresh)

    empty = jnp.zeros((dim, columns), jnp.float32)
    done = lax.fori_loop(0, steps, visit, (empty,) * groups)
    for g in range(groups):
        for h in range(share):
            head = g * share + h
            dq_ref[:, head * dim : (head + 1) * dim] = (
                (done[g][:, h * half : (h + 1) * half].T * scale).astype(dq_ref.dtype)
            )
    for k in range(peers):
        out, slot = even_ref, k // 2
        if k % 2:
            out, slot = odd_refs[slot // odd_refs[0].shape[0]], slot % odd_refs[0].shape[0]
        first = order[2 * (me ^ k)]
        other = spans - 1 - first
        pick = jnp.maximum(first, other) if upper else jnp.minimum(first, other)
        part = pl.ds(pl.multiple_of(pick * half, half), half)
        out[slot, :, :width] = (sums[part, :width] * scale).astype(out.dtype)
        out[slot, :, width:] = sums[part, width:].astype(out.dtype)
    if not upper:
        for copy in copies:
            copy.wait()


def grads(upper, q, g, level, mixed, *args):
    *blocks, span_order, doc_lengths, sizes = args
    weights, spare, scratch = [], [], []
    if not upper:
        heads = lax.axis_size("head")
        spare = list(range(heads - 1, 0, -2))
        weights, blocks = [in_hbm(w) for w in blocks[-3:]], blocks[:-3]
        scratch = [pltpu.SemaphoreType.DMA((len(spare), 3))]
    peers, half, groups, share, dim, docs = sizes
    tokens, width = 2 * half, groups * dim
    columns = share * half
    terms = jax.ShapeDtypeStruct((peers // 2, half, 2 * width), jnp.bfloat16)
    odds = jax.ShapeDtypeStruct((peers // 4, half, 2 * width), jnp.bfloat16)
    rests = jax.ShapeDtypeStruct((peers * tokens, 2 * width), jnp.float32)
    outs = [jax.ShapeDtypeStruct((half, g.shape[1]), jnp.bfloat16), terms, odds, odds] + [rests] * upper
    outs += [rows_shape(spare, w, heads) for w in weights]
    return pl.pallas_call(
        functools.partial(grads_body, sizes, upper, spare),
        in_specs=[pl.BlockSpec(memory_space=pltpu.SMEM)] * 2
        + [pl.BlockSpec(memory_space=VMEM)] * (4 + len(blocks))
        + [pl.BlockSpec(memory_space=HBM)] * len(weights),
        out_specs=[pl.BlockSpec(memory_space=VMEM)] * len(outs),
        out_shape=outs,
        scratch_shapes=[VMEM((peers * half, 2 * width), jnp.float32)] * (not upper)
        + [
            pltpu.SMEM((2 * peers,), jnp.int32),
        ]
        + scratch,
        compiler_params=params(),
        cost_estimate=cost(),
        name="upper_grads" if upper else "lower_grads",
    )(span_order, doc_lengths, q, g, level, mixed, *blocks, *weights)


def swap(x, k, axis):
    return lax.ppermute(x, axis, [(i, i ^ k) for i in range(lax.axis_size(axis))])


def gather_even(x, axis, held):
    size = lax.axis_size(axis)
    got, bit = {0: x}, 2
    while bit < size:
        passed = {k: block for k, block in got.items() if k}
        passed, held = lax.optimization_barrier((passed, held))
        got |= {bit: swap(x, bit, axis)}
        got |= {k ^ bit: swap(block, bit, axis) for k, block in passed.items()}
        bit *= 2
    return [got[k] for k in sorted(got)], held


def pair_body(even_ref, *refs):
    count = even_ref.shape[0]
    odd_refs, outs = refs[:-count], refs[-count:]
    part = odd_refs[0].shape[0]
    for k, out in enumerate(outs):
        total = even_ref[k].astype(jnp.float32) + odd_refs[k // part][k % part].astype(jnp.float32)
        out[...] = total.astype(out.dtype)


def pair_sums(even, *got):
    count, rows, width = even.shape
    return pl.pallas_call(
        pair_body,
        in_specs=[pl.BlockSpec(memory_space=VMEM)] * (1 + len(got)),
        out_specs=[pl.BlockSpec(memory_space=VMEM)] * count,
        out_shape=[jax.ShapeDtypeStruct((rows, width), jnp.bfloat16)] * count,
        compiler_params=params(),
        cost_estimate=cost(),
        name="pair_sums",
    )(even, *got)


def scatter_ctx(pairs):
    return [part if k == 0 else swap(part, 2 * k, "ctx") for k, part in enumerate(pairs)]


def shards(inputs, out_grad, w_query, w_key, value_projection, w_out, doc_lengths, span_order):
    tokens = inputs.shape[0]
    share = ASKER_NUM // SHARED_KV_NUM
    half = tokens // 2
    sizes = (
        lax.axis_size("ctx"),
        tokens // 2,
        w_key.shape[1] // CHANNEL_DIM,
        share,
        CHANNEL_DIM,
        doc_lengths.shape[0],
    )
    heads = lax.axis_size("head")
    last = [span_order]

    def turn(call, *args):
        held, *args = lax.optimization_barrier((last[0], *args))
        out = call(*args)
        last[0] = out if hasattr(out, "shape") else out[0]
        return out

    def attend(upper, call, *args):
        return turn(lambda *a: call(upper, *a, span_order, doc_lengths, sizes), *args)

    def context(blocks, stacks, spans, total, dtype):
        shape = jax.tree.structure((blocks, stacks, total))

        def call(*flat):
            parts, weights, given = jax.tree.unflatten(shape, flat)
            return back_project(parts, weights, spans, given, dtype)

        return turn(call, *jax.tree.leaves((blocks, stacks, total)))

    def send_first(parts, stack, places=None):
        if stack is None:
            return {k ^ 1: (swap(parts[k], 1, "head"), None) for k in places} | {0: None}
        places = range(heads - 1, 0, -2)
        got = swap(stack, 1, "head")
        return {k ^ 1: (got, i) for i, k in enumerate(places)}

    def send_rest(parts, got):
        ends, bit = [(parts[0], None), got[0]], 2
        parts = {
            k: turn(lambda a, b, at=got[k][1]: add(a, b, at), parts[k], got[k][0])
            for k in range(2, heads, 2)
        }
        while bit < heads:
            moved = {k ^ bit: swap(parts[k], bit, "head") for k in parts if k & bit}
            ends.append((moved.pop(0), None))
            parts = {k: turn(lambda a, b: add(a, b, None), parts[k], moved[k]) for k in moved}
            bit *= 2
        return ends

    def spread(x):
        got, bit = {0: x}, heads // 2
        while bit > 1:
            got |= {k ^ bit: swap(x, bit, "head") for k, x in got.items()}
            bit //= 2
        return got, swap(x, 1, "head")

    first_half = spread(out_grad[:half])
    own = turn(project_kv, inputs, w_key, value_projection)
    own, rest_rows = lax.optimization_barrier((own, out_grad))
    far, near = (list(x) for x in zip(first_half, spread(rest_rows[half:])))
    near_blocks, (far[0], near[0]) = gather_even(own, "ctx", (far[0], near[0]))
    query = turn(project, inputs, w_query)
    query, near_blocks = lax.optimization_barrier((query, near_blocks))
    blocks = (*near_blocks, *[swap(block, 1, "ctx") for block in near_blocks])
    query, far[1], near[1] = lax.optimization_barrier((query, far[1], near[1]))
    *upper_stats, w_first, held = attend(True, stats, query, *blocks, w_out)
    *lower_stats, w_second = attend(False, stats, query, held, w_out)
    passed = [{k ^ 1: swap(x, 1, "head") for k, x in got.items() if k} for got in far]
    come = {0: (out_grad,), 1: tuple(near)}
    come |= {k: (far[0][k], far[1][k]) for k in range(2, heads, 2)}
    come |= {k: (passed[0][k], passed[1][k]) for k in range(3, heads, 2)}
    blocks = [come[k] for k in range(heads)]
    mid = heads // 2
    total = context(
        blocks[:-1], (w_first, w_second), [(0, mid), (0, mid - 1)], None, jnp.float32
    )
    context_grad = context(blocks[-1:], (w_second,), [(mid - 1, mid)], total, jnp.bfloat16)
    upper_dq, even, *odd, rest = attend(True, grads, query, context_grad, *upper_stats, held)
    upper = scatter_ctx(turn(pair_sums, even, *[swap(x, 1, "ctx") for x in odd]))
    weights = (w_query, w_key, value_projection)
    lower_dq, even, *odd, wq, wk, wv = attend(
        False, grads, query, context_grad, *lower_stats, rest, held, *weights
    )
    sides = [list(range(heads - 1, 0, -2)), list(range(heads - 2, -1, -2))]
    weights = [(wq, wk, wv), weights]

    def firsts_of(side):
        return turn(
            lambda a, b, w: query_terms(a, b, w, heads, sides[side]),
            upper_dq,
            lower_dq,
            weights[side][0],
        )

    def terms_of(first, terms, side, stacked=False):
        outs = turn(
            lambda a, k, v, *b: all_terms(a, b, k, v, heads, sides[side], stacked),
            first,
            *weights[side][1:],
            *terms,
        )
        return outs[0] if stacked else dict(zip(sides[side], outs))

    first = [firsts_of(0)]
    lower_odd = [swap(x, 1, "ctx") for x in odd]
    upper_got = send_first(None, terms_of(first[0][0], upper, 0, True))
    lower = scatter_ctx(turn(pair_sums, even, *lower_odd))
    first.append(firsts_of(1))
    upper = terms_of(first[1][0], upper, 1)
    parts = terms_of(first[0][1], lower, 0)
    lower_got = send_first(parts, None, sides[0][:-1])
    upper = send_rest(upper, upper_got)
    lower = terms_of(first[1][1], lower, 1)
    lower = send_rest(lower, lower_got)
    stack, at = upper[1]
    upper = [(turn(lambda a, b: merge(a, b, at), upper[0][0], stack), None)] + upper[2:]
    last_part, held = lax.optimization_barrier((parts[1], last[0]))
    last_part = (swap(last_part, 1, "head"), None)
    total = upper[0][0]
    for block, at in upper[1:]:
        total = turn(lambda a, b: merge(a, b, None), total, block)
    upper = [(total, None)]
    total = lower[0][0]
    for block, at in lower[2:]:
        total = turn(lambda a, b: merge(a, b, None), total, block)
    lower = [(total, None), last_part]
    return join_rows(upper, lower, span_order)


def solution(mesh):
    in_specs = (
        P("ctx", None),
        P("ctx", "head"),
        P(None, "head"),
        P(None, "head"),
        P(None, "head"),
        P("head", None),
        P(),
        P(),
    )
    out_specs = P("ctx", "head")
    return jax.shard_map(shards, mesh=mesh, in_specs=in_specs, out_specs=out_specs, check_vma=False)
```
